256 devices in a mesh: grp: 2 (over z_lo), wide: 32 (over z_hi, y, core), narrow: 4 (over x).
Axes of the slice: x: 4, y: 4, z: 8 (z_hi: 4, z_lo: 2; z = z_hi * 2 + z_lo), core: 2. Of those that a mesh axis runs over, the one named last changes fastest.
Arguments:
- tokens: bfloat16 [5120, 50, 384], P(('grp', 'wide', 'narrow')), may hold values from -21 to 21
- grad_out: bfloat16 [5120, 50, 384], P(('grp', 'wide', 'narrow')), may hold values from -21 to 21
- weight_qkv: float32 [2, 384, 1152], replicated, may hold values from -0.3125 to 0.3125
- weight_proj: float32 [2, 384, 384], replicated, may hold values from -0.625 to 0.625
- weight_up: float32 [2, 384, 1536], replicated, may hold values from -0.3125 to 0.3125
- weight_down: float32 [2, 1536, 384], replicated, may hold values from -0.15625 to 0.15625
- weight_vector: float32 [2, 4608], replicated, may hold values from 0.5 to 1.5
- old_first_qkv: float32 [2, 384, 1152], P(None, ('wide', 'narrow')), may hold values from -112 to 112
- old_first_proj: float32 [2, 384, 384], P(None, ('wide', 'narrow')), may hold values from -112 to 112
- old_first_up: float32 [2, 384, 1536], P(None, ('wide', 'narrow')), may hold values from -112 to 112
- old_first_down: float32 [2, 1536, 384], P(None, ('wide', 'narrow')), may hold values from -256 to 256
- old_first_vector: float32 [2, 4608], P(None, ('wide', 'narrow')), may hold values from -160 to 160
- old_second_qkv: float32 [2, 384, 1152], P(None, ('wide', 'narrow')), may hold values from 1696 to 6784
- old_second_proj: float32 [2, 384, 384], P(None, ('wide', 'narrow')), may hold values from 1696 to 6784
- old_second_up: float32 [2, 384, 1536], P(None, ('wide', 'narrow')), may hold values from 1696 to 6784
- old_second_down: float32 [2, 1536, 384], P(None, ('wide', 'narrow')), may hold values from 9768.96 to 39075.84
- old_second_vector: float32 [2, 4608], P(None, ('wide', 'narrow')), may hold values from 67840 to 271360
- old_outer_qkv: float32 [2, 384, 1152], P(None, ('wide', 'narrow')), may hold values from -0.15625 to 0.15625
- old_outer_proj: float32 [2, 384, 384], P(None, ('wide', 'narrow')), may hold values from -0.3125 to 0.3125
- old_outer_up: float32 [2, 384, 1536], P(None, ('wide', 'narrow')), may hold values from -0.15625 to 0.15625
- old_outer_down: float32 [2, 1536, 384], P(None, ('wide', 'narrow')), may hold values from -0.078125 to 0.078125
- old_outer_vector: float32 [2, 4608], P(None, ('wide', 'narrow')), may hold values from -1.25 to 1.25
Outputs:
- block_out: bfloat16 [5120, 50, 384], P(('grp', 'wide', 'narrow'))
- grad_tokens: float32 [5120, 50, 384], P(('grp', 'wide', 'narrow'))
- new_first_qkv: float32 [2, 2, 384, 1152], P('grp', None, ('wide', 'narrow'))
- new_first_proj: float32 [2, 2, 384, 384], P('grp', None, ('wide', 'narrow'))
- new_first_up: float32 [2, 2, 384, 1536], P('grp', None, ('wide', 'narrow'))
- new_first_down: float32 [2, 2, 1536, 384], P('grp', None, ('wide', 'narrow'))
- new_first_vector: float32 [2, 2, 4608], P('grp', None, ('wide', 'narrow'))
- new_second_qkv: float32 [2, 2, 384, 1152], P('grp', None, ('wide', 'narrow'))
- new_second_proj: float32 [2, 2, 384, 384], P('grp', None, ('wide', 'narrow'))
- new_second_up: float32 [2, 2, 384, 1536], P('grp', None, ('wide', 'narrow'))
- new_second_down: float32 [2, 2, 1536, 384], P('grp', None, ('wide', 'narrow'))
- new_second_vector: float32 [2, 2, 4608], P('grp', None, ('wide', 'narrow'))
- change_qkv: float32 [2, 384, 1152], P(None, ('wide', 'narrow'))
- change_proj: float32 [2, 384, 384], P(None, ('wide', 'narrow'))
- change_up: float32 [2, 384, 1536], P(None, ('wide', 'narrow'))
- change_down: float32 [2, 1536, 384], P(None, ('wide', 'narrow'))
- change_vector: float32 [2, 4608], P(None, ('wide', 'narrow'))
- new_outer_qkv: float32 [2, 384, 1152], P(None, ('wide', 'narrow'))
- new_outer_proj: float32 [2, 384, 384], P(None, ('wide', 'narrow'))
- new_outer_up: float32 [2, 384, 1536], P(None, ('wide', 'narrow'))
- new_outer_down: float32 [2, 1536, 384], P(None, ('wide', 'narrow'))
- new_outer_vector: float32 [2, 4608], P(None, ('wide', 'narrow'))
- final_qkv: float32 [2, 384, 1152], P(None, ('wide', 'narrow'))
- final_proj: float32 [2, 384, 384], P(None, ('wide', 'narrow'))
- final_up: float32 [2, 384, 1536], P(None, ('wide', 'narrow'))
- final_down: float32 [2, 1536, 384], P(None, ('wide', 'narrow'))
- final_vector: float32 [2, 4608], P(None, ('wide', 'narrow'))
- copy_qkv: bfloat16 [2, 384, 1152], P(None, ('wide', 'narrow'))
- copy_proj: bfloat16 [2, 384, 384], P(None, ('wide', 'narrow'))
- copy_up: bfloat16 [2, 384, 1536], P(None, ('wide', 'narrow'))
- copy_down: bfloat16 [2, 1536, 384], P(None, ('wide', 'narrow'))
- copy_vector: bfloat16 [2, 4608], P(None, ('wide', 'narrow'))
- stream_rms: float32 [2, 3], replicated
The draws below stay inside these ranges and needn't reach their ends.
All inputs are finite; a program needn't handle non-finite values.
Results may differ from the reference program's by a relative error of at most 0.02.
Values sent between devices are 32-bit elements; how exact they have to be, the bound alone decides.
No kernel may reach another device: no remote copies, remote signals or barrier semaphores. Data moves between devices by JAX's collectives and lax.ppermute only.
A program may use at most 192 MiB of HBM per device.

```python
import math
import jax
import jax.numpy as jnp
from jax import lax

D = 384
HEADS = 6
HEAD_DIM = 64
FF = 1536
SEQ = 50
LAYERS = 2
STEP = 10
IMG_DEV = 20
IMAGES = 5120
GROUPS = 2
WIDE_DEVS = 32
NARROW_DEVS = 4
GROUP_IMAGES = 2560
BLOCK_IMAGES = 80
GROUP_TOKENS = 128000
VEC = 4608


def device_scale(spread):
    images = jnp.arange(IMAGES, dtype=jnp.int32)
    device = images // IMG_DEV
    narrow_pos = (device % NARROW_DEVS).astype(jnp.float32) / max(NARROW_DEVS - 1, 1)
    wide_pos = (device // NARROW_DEVS % WIDE_DEVS).astype(jnp.float32) / max(WIDE_DEVS - 1, 1)
    group_pos = (device // (NARROW_DEVS * WIDE_DEVS)).astype(jnp.float32) / max(GROUPS - 1, 1)
    return spread ** (narrow_pos + wide_pos + group_pos - 1.5)


def scaled_field(key, spread):
    values = jnp.clip(jax.random.normal(key, (IMAGES, SEQ, D), jnp.float32), -4.0, 4.0)
    return values * device_scale(spread)[:, None, None]


def row_scale(key):
    exponent = jax.random.uniform(key, (IMAGES, SEQ, 1), jnp.float32)
    return jnp.exp(-jnp.log(5.0) * exponent)


def draw_tokens(key, part):
    key = jax.random.fold_in(key, 5)
    rows = row_scale(jax.random.fold_in(key, 11))
    field = scaled_field(key, 3.0)
    return (field * rows).astype(jnp.bfloat16)


def draw_grad_out(key, part):
    key = jax.random.fold_in(key, 7)
    field = scaled_field(key, 3.0)
    return field.astype(jnp.bfloat16)


def steps_of(stream_key, dims, cuts, low, high):
    def one(axis_at, shards_of):
        heights = jax.random.uniform(jax.random.fold_in(jax.random.fold_in(stream_key, 6), axis_at), (shards_of,), jnp.float32, low / len(cuts), high / len(cuts))
        return jnp.repeat(jnp.exp(heights), dims[axis_at] // shards_of).reshape((-1,) + (1,) * (len(dims) - axis_at - 1))

    loudness = one(*cuts[0])
    for cut in cuts[1:]:
        loudness = loudness * one(*cut)
    return loudness


def normal_values(key, dims, scale, limit, shards=(), kind=jnp.bfloat16):
    entries = jax.random.normal(key, dims, jnp.float32) * scale
    if len(shards) > 0:
        entries = steps_of(key, dims, shards, -0.22, 0.18) * entries
    return jnp.clip(entries, min=-limit, max=limit).astype(kind)


def setup_inputs(seed: int = 0) -> dict:
    keys = jax.random.split(jax.random.key(seed), 23)
    return {
        "tokens": draw_tokens(jax.random.fold_in(keys[22], 71), 0),
        "grad_out": draw_grad_out(jax.random.fold_in(keys[22], 71), 0),
        "weight_qkv": normal_values(keys[2], (LAYERS, D, 3 * D), D ** -0.5, 0.3125, (), jnp.float32),
        "weight_proj": normal_values(keys[3], (LAYERS, D, D), (D // 4) ** -0.5, 0.625, (), jnp.float32),
        "weight_up": normal_values(keys[4], (LAYERS, D, FF), D ** -0.5, 0.3125, (), jnp.float32),
        "weight_down": normal_values(keys[5], (LAYERS, FF, D), FF ** -0.5, 0.15625, (), jnp.float32),
        "weight_vector": jnp.clip(1.0 + 0.1 * jax.random.normal(keys[6], (LAYERS, VEC), jnp.float32), 0.5, 1.5),
        "old_first_qkv": normal_values(keys[7], (LAYERS, D, 3 * D), (0.11 * 0.5 * GROUP_TOKENS ** 0.5), 112.0, ((1, 128),), jnp.float32),
        "old_first_proj": normal_values(keys[8], (LAYERS, D, D), (0.11 * 0.5 * GROUP_TOKENS ** 0.5), 112.0, ((1, 128),), jnp.float32),
        "old_first_up": normal_values(keys[9], (LAYERS, D, FF), (0.11 * 0.5 * GROUP_TOKENS ** 0.5), 112.0, ((1, 128),), jnp.float32),
        "old_first_down": normal_values(keys[10], (LAYERS, FF, D), (0.11 * 1.2 * GROUP_TOKENS ** 0.5), 256.0, ((1, 128),), jnp.float32),
        "old_first_vector": normal_values(keys[11], (LAYERS, VEC), (0.11 * 0.7 * GROUP_TOKENS ** 0.5), 160.0, ((1, 128),), jnp.float32),
        "old_second_qkv": jnp.clip(jnp.exp(math.log(6784.0) - 1.3862944 * jax.random.uniform(keys[12], (LAYERS, D, 3 * D), jnp.float32) ** steps_of(keys[12], (LAYERS, D, 3 * D), ((1, 128),), -0.2, 0.2)), 1696.0, 6784.0),
        "old_second_proj": jnp.clip(jnp.exp(math.log(6784.0) - 1.3862944 * jax.random.uniform(keys[13], (LAYERS, D, D), jnp.float32) ** steps_of(keys[13], (LAYERS, D, D), ((1, 128),), -0.2, 0.2)), 1696.0, 6784.0),
        "old_second_up": jnp.clip(jnp.exp(math.log(6784.0) - 1.3862944 * jax.random.uniform(keys[14], (LAYERS, D, FF), jnp.float32) ** steps_of(keys[14], (LAYERS, D, FF), ((1, 128),), -0.2, 0.2)), 1696.0, 6784.0),
        "old_second_down": jnp.clip(jnp.exp(math.log(39075.84) - 1.3862944 * jax.random.uniform(keys[15], (LAYERS, FF, D), jnp.float32) ** steps_of(keys[15], (LAYERS, FF, D), ((1, 128),), -0.2, 0.2)), 9768.96, 39075.84),
        "old_second_vector": jnp.clip(jnp.exp(math.log(271360.0) - 1.3862944 * jax.random.uniform(keys[16], (LAYERS, VEC), jnp.float32) ** steps_of(keys[16], (LAYERS, VEC), ((1, 128),), -0.2, 0.2)), 67840.0, 271360.0),
        "old_outer_qkv": normal_values(keys[17], (LAYERS, D, 3 * D), (0.5 * D ** -0.5), 0.15625, ((1, 128),), jnp.float32),
        "old_outer_proj": normal_values(keys[18], (LAYERS, D, D), (D ** -0.5), 0.3125, ((1, 128),), jnp.float32),
        "old_outer_up": normal_values(keys[19], (LAYERS, D, FF), (0.5 * D ** -0.5), 0.15625, ((1, 128),), jnp.float32),
        "old_outer_down": normal_values(keys[20], (LAYERS, FF, D), (0.5 * FF ** -0.5), 0.078125, ((1, 128),), jnp.float32),
        "old_outer_vector": normal_values(keys[21], (LAYERS, VEC), 0.2, 1.25, ((1, 128),), jnp.float32),
    }


exact_mode = lax.Precision.HIGHEST
beta_one = 0.9
beta_two = 0.95
adam_eps = 1e-08
decay_rate = 0.1
outer_decay = 0.9
outer_rate = 0.7

@jax.custom_vjp
def low(v):
    return lax.optimization_barrier(v.astype(jnp.bfloat16)).astype(jnp.float32)

@jax.custom_vjp
def low_back(v):
    return v

def low_keep(v):
    return (low(v), None)

def low_pass(kept, grad):
    return (grad,)

def back_keep(v):
    return (v, None)

def back_low(kept, grad):
    return (low(grad),)
low.defvjp(low_keep, low_pass)
low_back.defvjp(back_keep, back_low)

def matmul(left, right):
    return jnp.dot(left, right, precision=exact_mode, preferred_element_type=jnp.float32)

def rates():
    return (1.5 * D ** (-0.5), 1.5 * (D // 4) ** (-0.5), 1.5 * D ** (-0.5), 1.5 * FF ** (-0.5), 2.0)

def split_vector(vector):
    return jnp.split(vector, [D, 2 * D, 3 * D, 4 * D, 5 * D, 6 * D, 7 * D, 7 * D + FF])

def norm_rows(stream, gain, shift):
    center = stream - lax.optimization_barrier(jnp.mean(stream, -1, keepdims=True))
    spread = lax.optimization_barrier(jnp.mean(center * center, -1, keepdims=True))
    return center * lax.rsqrt(spread + 1e-06) * gain + shift

def layer_forward(stream, w_attn, w_out, w_up, w_down, vector):
    gain_one, shift_one, bias_query, bias_value, bias_out, gain_two, shift_two, bias_up, bias_down = split_vector(vector)
    images = stream.shape[0] // SEQ
    normed = norm_rows(stream, gain_one, shift_one)
    projected = matmul(low(normed), low(w_attn)) + jnp.concatenate([bias_query, jnp.zeros_like(bias_query), bias_value])
    projected = low(low_back(projected)).reshape(images, SEQ, 3, HEADS, HEAD_DIM)
    scores = jnp.einsum('nqhd,nkhd->nhqk', projected[:, :, 0], projected[:, :, 1], precision=exact_mode) * HEAD_DIM ** (-0.5)
    attend = jax.nn.softmax(low_back(scores), axis=-1)
    mixed_heads = jnp.einsum('nhqk,nkhd->nqhd', low(attend), projected[:, :, 2], precision=exact_mode).reshape(images * SEQ, D)
    attn_branch = low_back(matmul(low(low_back(mixed_heads)), low(w_out)) + bias_out)
    middle = stream + attn_branch
    normed_two = norm_rows(middle, gain_two, shift_two)
    hidden = low_back(matmul(low(normed_two), low(w_up)) + bias_up)
    mlp_branch = low_back(matmul(low(jax.nn.gelu(hidden, approximate=False)), low(w_down)) + bias_down)
    square_sums = jnp.stack([jnp.sum(stream * stream), jnp.sum(attn_branch * attn_branch), jnp.sum(mlp_branch * mlp_branch)])
    return (middle + mlp_branch, square_sums)

def blocks_forward(stream, weights):
    collected = []
    for layer_index in range(LAYERS):
        stream, square_sums = layer_forward(stream, weights[0][layer_index], weights[1][layer_index], weights[2][layer_index], weights[3][layer_index], weights[4][layer_index])
        collected.append(square_sums)
    return (stream, jnp.stack(collected))

def adam_step(gradient, moment_one, moment_two, weight, rate):
    moment_one = beta_one * moment_one + (1 - beta_one) * gradient
    moment_two = beta_two * moment_two + (1 - beta_two) * gradient * gradient
    fix_one = 1 - beta_one ** STEP
    fix_two = 1 - beta_two ** STEP
    update = moment_one / fix_one / (jnp.sqrt(moment_two / fix_two) + adam_eps) + decay_rate * weight
    return (moment_one, moment_two, weight - rate * update)

def reference(tokens, grad_out, weight_qkv, weight_proj, weight_up, weight_down, weight_vector, old_first_qkv, old_first_proj, old_first_up, old_first_down, old_first_vector, old_second_qkv, old_second_proj, old_second_up, old_second_down, old_second_vector, old_outer_qkv, old_outer_proj, old_outer_up, old_outer_down, old_outer_vector):
    weights = (weight_qkv, weight_proj, weight_up, weight_down, weight_vector)
    old_firsts = (old_first_qkv, old_first_proj, old_first_up, old_first_down, old_first_vector)
    old_seconds = (old_second_qkv, old_second_proj, old_second_up, old_second_down, old_second_vector)
    old_outers = (old_outer_qkv, old_outer_proj, old_outer_up, old_outer_down, old_outer_vector)
    block_count = GROUP_IMAGES // BLOCK_IMAGES
    outputs_all = []
    grads_all = []
    total_sums = jnp.zeros((LAYERS, 3), jnp.float32)
    firsts = [[] for kind_index in range(5)]
    seconds = [[] for kind_index in range(5)]
    decreases = [jnp.zeros_like(weights[kind_index]) for kind_index in range(5)]
    for group_index in range(GROUPS):
        first_image = group_index * GROUP_IMAGES
        x_group = tokens[first_image:first_image + GROUP_IMAGES].astype(jnp.float32).reshape(block_count, BLOCK_IMAGES * SEQ, D)
        d_group = grad_out[first_image:first_image + GROUP_IMAGES].astype(jnp.float32).reshape(block_count, BLOCK_IMAGES * SEQ, D)

        def step(running, block_pair):
            gradients, sums_now = running
            x_block, d_block = block_pair
            result, pull_back, block_sums = jax.vjp(blocks_forward, x_block, weights, has_aux=True)
            d_tokens, d_weights = pull_back(d_block)
            gradients = jax.tree.map(lambda total_grad, block_grad: total_grad + block_grad, gradients, d_weights)
            return ((gradients, sums_now + block_sums), (result, d_tokens))
        start_state = (jax.tree.map(jnp.zeros_like, weights), jnp.zeros((LAYERS, 3), jnp.float32))
        (gradients, group_sums), (results, d_tokens) = lax.scan(step, start_state, (x_group, d_group))
        total_sums = total_sums + group_sums
        outputs_all.append(results.reshape(GROUP_IMAGES, SEQ, D))
        grads_all.append(d_tokens.reshape(GROUP_IMAGES, SEQ, D))
        for kind_index in range(5):
            moment_one, moment_two, weight_new = adam_step(gradients[kind_index], old_firsts[kind_index], old_seconds[kind_index], weights[kind_index], rates()[kind_index])
            firsts[kind_index].append(moment_one)
            seconds[kind_index].append(moment_two)
            decreases[kind_index] = decreases[kind_index] + (weights[kind_index] - weight_new)
    block_out = jnp.concatenate(outputs_all, 0).astype(jnp.bfloat16)
    grad_tokens = jnp.concatenate(grads_all, 0)
    new_firsts = [jnp.stack(firsts[kind_index]) for kind_index in range(5)]
    new_seconds = [jnp.stack(seconds[kind_index]) for kind_index in range(5)]
    changes = [decreases[kind_index] / GROUPS for kind_index in range(5)]
    outers = [outer_decay * old_outers[kind_index] + changes[kind_index] for kind_index in range(5)]
    finals = [weights[kind_index] - outer_rate * (changes[kind_index] + outer_decay * outers[kind_index]) for kind_index in range(5)]
    copies = [finals[kind_index].astype(jnp.bfloat16) for kind_index in range(5)]
    stream_rms = jnp.sqrt(total_sums / (IMAGES * SEQ * D))
    return (block_out, grad_tokens, new_firsts[0], new_firsts[1], new_firsts[2], new_firsts[3], new_firsts[4], new_seconds[0], new_seconds[1], new_seconds[2], new_seconds[3], new_seconds[4], changes[0], changes[1], changes[2], changes[3], changes[4], outers[0], outers[1], outers[2], outers[3], outers[4], finals[0], finals[1], finals[2], finals[3], finals[4], copies[0], copies[1], copies[2], copies[3], copies[4], stream_rms)
```

```python
import jax
import jax.numpy as jnp
from jax import lax
from jax.experimental import pallas as pl
from jax.experimental.pallas import tpu as pltpu
from jax.sharding import PartitionSpec as P

D = 384
HEADS = 6
HEAD_DIM = 64
FF = 1536
SEQ = 50
STEP = 10


beta_one = 0.9
beta_two = 0.95
adam_eps = 1e-08
decay_rate = 0.1
outer_decay = 0.9
outer_rate = 0.7


def rates():
    return (1.5 * D ** (-0.5), 1.5 * (D // 4) ** (-0.5), 1.5 * D ** (-0.5), 1.5 * FF ** (-0.5), 2.0)


def split_vector(vector):
    return jnp.split(vector, [D, 2 * D, 3 * D, 4 * D, 5 * D, 6 * D, 7 * D, 7 * D + FF])


def norm_rows(stream, gain, shift):
    center = stream - jnp.mean(stream, -1, keepdims=True)
    spread = jnp.mean(center * center, -1, keepdims=True)
    return center * lax.rsqrt(spread + 1e-06) * gain + shift


def column_sums(values):
    return jnp.sum(values.astype(jnp.float32), 0)


def forward_layer(stream, w_attn, w_out, w_up, w_down, vector):
    (
        gain_one,
        shift_one,
        bias_query,
        bias_value,
        bias_out,
        gain_two,
        shift_two,
        bias_up,
        bias_down,
    ) = split_vector(vector)
    images = stream.shape[0] // SEQ
    normed = norm_rows(stream, gain_one, shift_one)
    projected = jnp.dot(normed.astype(jnp.bfloat16), w_attn, preferred_element_type=jnp.float32)
    projected = projected + jnp.concatenate([bias_query, jnp.zeros_like(bias_query), bias_value])
    projected = projected.astype(jnp.bfloat16).reshape(images, SEQ, 3, HEADS, HEAD_DIM)
    scores = jnp.einsum(
        "nqhd,nkhd->nhqk",
        projected[:, :, 0],
        projected[:, :, 1],
        preferred_element_type=jnp.float32,
    ) * HEAD_DIM ** (-0.5)
    row_max = jnp.max(scores, -1, keepdims=True)
    raised = jnp.exp(scores - row_max)
    row_total = jnp.sum(raised, -1, keepdims=True)
    attend = raised / row_total
    log_sum = row_max + jnp.log(row_total)
    mixed_heads = jnp.einsum(
        "nhqk,nkhd->nqhd",
        attend.astype(jnp.bfloat16),
        projected[:, :, 2],
        preferred_element_type=jnp.float32,
    )
    mixed_heads = mixed_heads.reshape(images * SEQ, D).astype(jnp.bfloat16)
    attn_branch = jnp.dot(mixed_heads, w_out, preferred_element_type=jnp.float32) + bias_out
    middle = stream + attn_branch
    normed_two = norm_rows(middle, gain_two, shift_two)
    hidden = (
        jnp.dot(normed_two.astype(jnp.bfloat16), w_up, preferred_element_type=jnp.float32) + bias_up
    )
    activated = jax.nn.gelu(hidden, approximate=False).astype(jnp.bfloat16)
    mlp_branch = jnp.dot(activated, w_down, preferred_element_type=jnp.float32) + bias_down
    square_sums = jnp.stack(
        [
            jnp.sum(stream * stream),
            jnp.sum(attn_branch * attn_branch),
            jnp.sum(mlp_branch * mlp_branch),
        ]
    )
    kept_values = (stream, projected, log_sum, mixed_heads, middle, hidden, activated)
    return (middle + mlp_branch, kept_values, square_sums)


def backward_layer(grad_stream, kept_values, w_attn, w_out, w_up, w_down, vector):
    stream, projected, log_sum, mixed_heads, middle, hidden, activated = kept_values
    (
        gain_one,
        shift_one,
        bias_query,
        bias_value,
        bias_out,
        gain_two,
        shift_two,
        bias_up,
        bias_down,
    ) = split_vector(vector)
    images = stream.shape[0] // SEQ
    scale = HEAD_DIM ** (-0.5)
    grad_down = grad_stream.astype(jnp.bfloat16)
    dw_down = jnp.dot(activated.T, grad_down, preferred_element_type=jnp.float32)
    db_down = column_sums(grad_down)
    grad_act = jnp.dot(grad_down, w_down.T, preferred_element_type=jnp.float32)
    gelu_back = jax.vjp(lambda value: jax.nn.gelu(value, approximate=False), hidden)[1]
    grad_hidden = gelu_back(grad_act)[0].astype(jnp.bfloat16)
    normed_two, norm_back_two = jax.vjp(norm_rows, middle, gain_two, shift_two)
    dw_up = jnp.dot(
        normed_two.astype(jnp.bfloat16).T, grad_hidden, preferred_element_type=jnp.float32
    )
    db_up = column_sums(grad_hidden)
    d_middle, dg_two, ds_two = norm_back_two(
        jnp.dot(grad_hidden, w_up.T, preferred_element_type=jnp.float32)
    )
    grad_middle = grad_stream + d_middle
    grad_branch = grad_middle.astype(jnp.bfloat16)
    dw_out = jnp.dot(mixed_heads.T, grad_branch, preferred_element_type=jnp.float32)
    db_out = column_sums(grad_branch)
    grad_heads = jnp.dot(grad_branch, w_out.T, preferred_element_type=jnp.float32).astype(
        jnp.bfloat16
    )
    grad_heads = grad_heads.reshape(images, SEQ, HEADS, HEAD_DIM)
    queries = projected[:, :, 0]
    key_rows = projected[:, :, 1]
    value_rows = projected[:, :, 2]
    scores = (
        jnp.einsum("nqhd,nkhd->nhqk", queries, key_rows, preferred_element_type=jnp.float32) * scale
    )
    attend = jnp.exp(scores - log_sum)
    grad_attend = jnp.einsum(
        "nqhd,nkhd->nhqk", grad_heads, value_rows, preferred_element_type=jnp.float32
    )
    grad_values = jnp.einsum(
        "nhqk,nqhd->nkhd",
        attend.astype(jnp.bfloat16),
        grad_heads,
        preferred_element_type=jnp.float32,
    )
    grad_scores = (
        attend * (grad_attend - jnp.sum(attend * grad_attend, -1, keepdims=True))
    ).astype(jnp.bfloat16)
    grad_queries = (
        jnp.einsum("nhqk,nkhd->nqhd", grad_scores, key_rows, preferred_element_type=jnp.float32)
        * scale
    )
    grad_keys = (
        jnp.einsum("nhqk,nqhd->nkhd", grad_scores, queries, preferred_element_type=jnp.float32)
        * scale
    )
    grad_projected = (
        jnp.stack([grad_queries, grad_keys, grad_values], 2)
        .reshape(images * SEQ, 3 * D)
        .astype(jnp.bfloat16)
    )
    normed, norm_back = jax.vjp(norm_rows, stream, gain_one, shift_one)
    dw_attn = jnp.dot(
        normed.astype(jnp.bfloat16).T, grad_projected, preferred_element_type=jnp.float32
    )
    bias_grads = column_sums(grad_projected)
    d_stream, dg_one, ds_one = norm_back(
        jnp.dot(grad_projected, w_attn.T, preferred_element_type=jnp.float32)
    )
    vector_grad = jnp.concatenate(
        [
            dg_one,
            ds_one,
            bias_grads[:D],
            bias_grads[2 * D :],
            db_out,
            dg_two,
            ds_two,
            db_up,
            db_down,
        ]
    )
    return (grad_middle + d_stream, (dw_attn, dw_out, dw_up, dw_down, vector_grad))


ROWS = 112
QKV_AT, PROJ_AT, UP_AT, DOWN_AT, SMALL_AT = 0, 27, 36, 72, 108
SUMS_AT = 64
VMEM_WHOLE = pl.BlockSpec(memory_space=pltpu.VMEM)
GROUP_AXES = ("wide", "narrow")


def place_of(owner):
    return owner // 32, owner // 8 % 4, owner // 4 % 2, owner % 4


def owner_of(deep, high, core, across):
    return ((deep * 4 + high) * 2 + core) * 4 + across


def core_pairs():
    return [(o, o ^ 4) for o in range(128)]


def ring_pairs(stage, shift):
    pairs = []
    for o in range(128):
        deep, high, core, across = place_of(o)
        if stage == 2:
            deep = (deep + shift) % 4
        elif core == stage:
            across = (across + shift) % 4
        else:
            high = (high + shift) % 4
        pairs.append((o, owner_of(deep, high, core, across)))
    return pairs


def pack_kernel(qkv, proj, up, down, small, keep, send):
    def emit(halves):
        @pl.loop(0, 16)
        def _(block):
            deep, high = block // 4, block % 4
            base = pl.multiple_of(block * 24, 8)
            base_down = pl.multiple_of(block * 96, 8)
            base_small = pl.multiple_of(block * 8, 8)

            def target(core, across):
                if core == 0:
                    return halves[0].at[across, high, deep]
                return halves[1].at[high, across, deep]

            for source, start, width in ((qkv, QKV_AT, 9), (proj, PROJ_AT, 3), (up, UP_AT, 12)):
                for column in range(width):
                    rows = source[pl.ds(base, 24), column * 128 : (column + 1) * 128]
                    for k in range(8):
                        at = start + 3 * column
                        target(k // 4, k % 4)[at : at + 3, :] = rows[3 * k : 3 * k + 3]
            for column in range(3):
                rows = down[pl.ds(base_down, 96), column * 128 : (column + 1) * 128]
                for k in range(8):
                    at = DOWN_AT + 12 * column
                    target(k // 4, k % 4)[at : at + 12, :] = rows[12 * k : 12 * k + 12]
            rows = small[pl.ds(base_small, 8), :]
            for k in range(8):
                target(k // 4, k % 4)[SMALL_AT : SMALL_AT + 1, :] = rows[k : k + 1]
                target(k // 4, k % 4)[SMALL_AT + 1 : ROWS, :] = jnp.zeros((3, 128), jnp.float32)

    core = lax.axis_index(GROUP_AXES) // 4 % 2

    @pl.when(core == 0)
    def _():
        emit((keep, send))

    @pl.when(core == 1)
    def _():
        emit((send, keep))


def pack(qkv, proj, up, down, small):
    half = jax.ShapeDtypeStruct((4, 4, 4, ROWS, 128), jnp.float32)
    return pl.pallas_call(
        pack_kernel,
        out_shape=(half, half),
        in_specs=[VMEM_WHOLE] * 5,
        out_specs=(VMEM_WHOLE, VMEM_WHOLE),
        compiler_params=pltpu.CompilerParams(vmem_limit_bytes=40 * 2**20),
        name="pack",
    )(qkv, proj, up, down, small)


def stage_position(stage):
    deep, high, core, across = place_of(lax.axis_index(GROUP_AXES))
    if stage == 2:
        return deep
    return jnp.where(core == stage, across, high)


def add_first_kernel(keep, got, *outs):
    me = stage_position(0)
    for shift in range(4):
        at = (me + shift) % 4

        @pl.loop(0, 16)
        def _(i):
            outs[shift][i // 4, i % 4] = keep[at, i // 4, i % 4] + got[at, i // 4, i % 4]


def add_ring_kernel(stage, own, one, two, three, *outs):
    if stage == 3:
        outs[0][...] = (own[...] + one[...]) + (two[...] + three[...])
        return
    me = stage_position(stage)
    for shift in range(4):
        at = (me + shift) % 4
        if stage == 2:
            outs[shift][...] = (own[at] + one[at]) + (two[at] + three[at])
        else:

            @pl.loop(0, 4)
            def _(i):
                outs[shift][i] = (own[at, i] + one[at, i]) + (two[at, i] + three[at, i])


def call_add(kernel, values, out_dims, count, name):
    return pl.pallas_call(
        kernel,
        out_shape=[jax.ShapeDtypeStruct(out_dims + (ROWS, 128), jnp.float32)] * count,
        in_specs=[VMEM_WHOLE] * len(values),
        out_specs=[VMEM_WHOLE] * count,
        compiler_params=pltpu.CompilerParams(vmem_limit_bytes=32 * 2**20),
        name=name,
    )(*values)


def ring(stage, parts):
    got = [lax.ppermute(parts[s], GROUP_AXES, ring_pairs(stage, s)) for s in range(1, 4)]
    return [parts[0]] + got


def reduce_packed(keep, send):
    got = lax.ppermute(send, GROUP_AXES, core_pairs())
    parts = call_add(add_first_kernel, [keep, got], (4, 4), 4, "add_core")
    parts = ring(0, parts)
    parts = call_add(lambda *a: add_ring_kernel(1, *a), parts, (4,), 4, "add_first")
    parts = ring(1, parts)
    parts = call_add(lambda *a: add_ring_kernel(2, *a), parts, (), 4, "add_second")
    parts = ring(2, parts)
    return call_add(lambda *a: add_ring_kernel(3, *a), parts, (), 1, "add_third")[0]


def adam_step(gradient, moment_one, moment_two, weight, rate):
    moment_one = beta_one * moment_one + (1 - beta_one) * gradient
    moment_two = beta_two * moment_two + (1 - beta_two) * gradient * gradient
    fix_one = 1 - beta_one**STEP
    fix_two = 1 - beta_two**STEP
    update = (
        moment_one / fix_one / (jnp.sqrt(moment_two / fix_two) + adam_eps) + decay_rate * weight
    )
    return (moment_one, moment_two, weight - rate * update)


def finish_kernel(*refs):
    own, other = refs[:2], refs[2:4]
    weights, firsts, seconds, outers = (refs[4 + 5 * k : 9 + 5 * k] for k in range(4))
    outs = refs[24:]
    new_firsts, new_seconds, changes, new_outers, finals, copies = (
        outs[5 * k : 5 * k + 5] for k in range(6)
    )
    rms = outs[30]

    def gathered(ref, kind):
        if kind == 4:
            return ref[SMALL_AT : SMALL_AT + 1, 0:36]
        start, rows, width = (
            (QKV_AT, 3, 9),
            (PROJ_AT, 3, 3),
            (UP_AT, 3, 12),
            (DOWN_AT, 12, 3),
        )[kind]
        return jnp.concatenate(
            [ref[start + rows * c : start + rows * (c + 1), :] for c in range(width)], axis=1
        )

    for layer in range(2):
        for kind in range(5):
            at = slice(layer, layer + 1) if kind == 4 else layer
            weight = weights[kind][at]
            rate = rates()[kind]
            moments = (firsts[kind][at], seconds[kind][at])
            one, two, updated = adam_step(gathered(own[layer], kind), *moments, weight, rate)
            updated_other = adam_step(gathered(other[layer], kind), *moments, weight, rate)[2]
            change = ((weight - updated) + (weight - updated_other)) / 2
            outer = outer_decay * outers[kind][at] + change
            final = weight - outer_rate * (change + outer_decay * outer)
            new_firsts[kind][0, at] = one
            new_seconds[kind][0, at] = two
            changes[kind][at] = change
            new_outers[kind][at] = outer
            finals[kind][at] = final
            copies[kind][at] = final.astype(jnp.bfloat16)
        totals = [
            ref[SMALL_AT : SMALL_AT + 1, SUMS_AT : SUMS_AT + 3] for ref in (own[layer], other[layer])
        ]
        rms[layer : layer + 1, :] = jnp.sqrt((totals[0] + totals[1]) / ENTRIES)


ENTRIES = 98304000


def finish(own, other, weights, firsts, seconds, outers):
    shapes = [w.shape for w in weights]
    full = [jax.ShapeDtypeStruct(s, jnp.float32) for s in shapes]
    stacked = [jax.ShapeDtypeStruct((1,) + s, jnp.float32) for s in shapes]
    low = [jax.ShapeDtypeStruct(s, jnp.bfloat16) for s in shapes]
    out_shape = stacked * 2 + full * 3 + low + [jax.ShapeDtypeStruct((2, 3), jnp.float32)]
    return pl.pallas_call(
        finish_kernel,
        out_shape=out_shape,
        in_specs=[VMEM_WHOLE] * 24,
        out_specs=[VMEM_WHOLE] * 31,
        name="finish",
    )(*own, *other, *weights, *firsts, *seconds, *outers)


def body(
    tokens,
    grad_out,
    weight_qkv,
    weight_proj,
    weight_up,
    weight_down,
    weight_vector,
    old_first_qkv,
    old_first_proj,
    old_first_up,
    old_first_down,
    old_first_vector,
    old_second_qkv,
    old_second_proj,
    old_second_up,
    old_second_down,
    old_second_vector,
    old_outer_qkv,
    old_outer_proj,
    old_outer_up,
    old_outer_down,
    old_outer_vector,
):
    masters = (weight_qkv, weight_proj, weight_up, weight_down, weight_vector)
    old_firsts = (old_first_qkv, old_first_proj, old_first_up, old_first_down, old_first_vector)
    old_seconds = (
        old_second_qkv,
        old_second_proj,
        old_second_up,
        old_second_down,
        old_second_vector,
    )
    old_outers = (old_outer_qkv, old_outer_proj, old_outer_up, old_outer_down, old_outer_vector)
    lowered = tuple((masters[kind_index].astype(jnp.bfloat16) for kind_index in range(4)))
    layer_total = weight_qkv.shape[0]
    stream = tokens.astype(jnp.float32).reshape(-1, D)
    kept_all = []
    sums_all = []
    for layer_index in range(layer_total):
        stream, kept_values, square_sums = forward_layer(
            stream,
            lowered[0][layer_index],
            lowered[1][layer_index],
            lowered[2][layer_index],
            lowered[3][layer_index],
            weight_vector[layer_index],
        )
        kept_all.append(kept_values)
        sums_all.append(square_sums)
    block_out = stream.reshape(tokens.shape).astype(jnp.bfloat16)
    owner_index = lax.axis_index(("wide", "narrow"))
    grad_stream = grad_out.astype(jnp.float32).reshape(-1, D)
    shares = []
    for kind_index in range(5):
        share_rows = old_firsts[kind_index].shape[1]
        shares.append(
            lax.dynamic_slice_in_dim(masters[kind_index], owner_index * share_rows, share_rows, 1)
        )
    reduced = [None] * layer_total
    for layer_index in reversed(range(layer_total)):
        grad_stream, gradients = backward_layer(
            grad_stream,
            kept_all[layer_index],
            lowered[0][layer_index],
            lowered[1][layer_index],
            lowered[2][layer_index],
            lowered[3][layer_index],
            weight_vector[layer_index],
        )
        sums = jnp.broadcast_to(sums_all[layer_index][None], (128, 3))
        small = jnp.concatenate(
            [
                gradients[4].reshape(128, 36),
                jnp.zeros((128, SUMS_AT - 36), jnp.float32),
                sums,
                jnp.zeros((128, 128 - SUMS_AT - 3), jnp.float32),
            ],
            1,
        )
        reduced[layer_index] = reduce_packed(*pack(*gradients[:4], small))
    grad_tokens = grad_stream.reshape(tokens.shape)
    others = [lax.ppermute(value, "grp", [(0, 1), (1, 0)]) for value in reduced]
    results = finish(reduced, others, shares, old_firsts, old_seconds, old_outers)
    return (block_out, grad_tokens, *results)


def solution(mesh):
    placed = (
        P(("grp", "wide", "narrow"), None, None),
        P(("grp", "wide", "narrow"), None, None),
        P(),
        P(),
        P(),
        P(),
        P(),
        P(None, ("wide", "narrow"), None),
        P(None, ("wide", "narrow"), None),
        P(None, ("wide", "narrow"), None),
        P(None, ("wide", "narrow"), None),
        P(None, ("wide", "narrow")),
        P(None, ("wide", "narrow"), None),
        P(None, ("wide", "narrow"), None),
        P(None, ("wide", "narrow"), None),
        P(None, ("wide", "narrow"), None),
        P(None, ("wide", "narrow")),
        P(None, ("wide", "narrow"), None),
        P(None, ("wide", "narrow"), None),
        P(None, ("wide", "narrow"), None),
        P(None, ("wide", "narrow"), None),
        P(None, ("wide", "narrow")),
    )
    return jax.shard_map(
        body,
        mesh=mesh,
        in_specs=placed,
        out_specs=(
            P(("grp", "wide", "narrow"), None, None),
            P(("grp", "wide", "narrow"), None, None),
            P("grp", None, ("wide", "narrow"), None),
            P("grp", None, ("wide", "narrow"), None),
            P("grp", None, ("wide", "narrow"), None),
            P("grp", None, ("wide", "narrow"), None),
            P("grp", None, ("wide", "narrow")),
            P("grp", None, ("wide", "narrow"), None),
            P("grp", None, ("wide", "narrow"), None),
            P("grp", None, ("wide", "narrow"), None),
            P("grp", None, ("wide", "narrow"), None),
            P("grp", None, ("wide", "narrow")),
            P(None, ("wide", "narrow"), None),
            P(None, ("wide", "narrow"), None),
            P(None, ("wide", "narrow"), None),
            P(None, ("wide", "narrow"), None),
            P(None, ("wide", "narrow")),
            P(None, ("wide", "narrow"), None),
            P(None, ("wide", "narrow"), None),
            P(None, ("wide", "narrow"), None),
            P(None, ("wide", "narrow"), None),
            P(None, ("wide", "narrow")),
            P(None, ("wide", "narrow"), None),
            P(None, ("wide", "narrow"), None),
            P(None, ("wide", "narrow"), None),
            P(None, ("wide", "narrow"), None),
            P(None, ("wide", "narrow")),
            P(None, ("wide", "narrow"), None),
            P(None, ("wide", "narrow"), None),
            P(None, ("wide", "narrow"), None),
            P(None, ("wide", "narrow"), None),
            P(None, ("wide", "narrow")),
            P(),
        ),
        check_vma=False,
    )
```

```python
import jax
import jax.numpy as jnp
from jax import lax
from jax.experimental import pallas as pl
from jax.experimental.pallas import tpu as pltpu
from jax.sharding import PartitionSpec as P

D = 384
HEADS = 6
HEAD_DIM = 64
FF = 1536
SEQ = 50
STEP = 10


beta_one = 0.9
beta_two = 0.95
adam_eps = 1e-08
decay_rate = 0.1
outer_decay = 0.9
outer_rate = 0.7


def rates():
    return (1.5 * D ** (-0.5), 1.5 * (D // 4) ** (-0.5), 1.5 * D ** (-0.5), 1.5 * FF ** (-0.5), 2.0)


ROWS = 112
UP_AT, DOWN_AT, QKV_AT, PROJ_AT, SMALL_AT = 0, 36, 72, 99, 108
SUMS_AT = 64
VMEM_WHOLE = pl.BlockSpec(memory_space=pltpu.VMEM)
GROUP_AXES = ("wide", "narrow")


def place_of(owner):
    return owner // 32, owner // 8 % 4, owner // 4 % 2, owner % 4


def owner_of(deep, high, core, across):
    return ((deep * 4 + high) * 2 + core) * 4 + across


def core_pairs():
    return [(o, o ^ 4) for o in range(128)]


def ring_pairs(stage, shift):
    pairs = []
    for o in range(128):
        deep, high, core, across = place_of(o)
        if stage == 2:
            deep = (deep + shift) % 4
        elif core == stage:
            across = (across + shift) % 4
        else:
            high = (high + shift) % 4
        pairs.append((o, owner_of(deep, high, core, across)))
    return pairs


IMG = 10
CHUNKS = 2
RUN = 512
REAL = IMG * SEQ
STEP_ROWS = 512
TOGETHER = 5
TOGETHER_BACK = 5
G1, B1, BQ, BV, BO, G2, B2, BU, BD = 0, 384, 768, 1152, 1536, 1920, 2304, 2688, 4224
BF = jnp.bfloat16
F32 = jnp.float32


def dot(left, right, left_dim=1, right_dim=0):
    return lax.dot_general(
        left, right, (((left_dim,), (right_dim,)), ((), ())), preferred_element_type=F32
    )


def normalise(rows):
    center = rows - jnp.sum(rows, -1, keepdims=True) * (1 / D)
    rate = lax.rsqrt(jnp.sum(center * center, -1, keepdims=True) * (1 / D) + 1e-06)
    return center * rate, rate


def norm_back(grad, unit, rate, gain):
    scaled = grad * gain
    first = jnp.sum(scaled, -1, keepdims=True) * (1 / D)
    second = jnp.sum(scaled * unit, -1, keepdims=True) * (1 / D)
    return rate * (scaled - first - unit * second)


def gelu_parts(value):
    area = 0.5 + 0.5 * lax.erf(value * 0.7071067811865476)
    bell = jnp.exp(-0.5 * value * value)
    return value * area, area + value * bell * 0.3989422804014327


def fold(values):
    return jnp.sum(values.reshape(-1, 8, values.shape[-1]), 0)


def halves_of(rows, low, keep):
    zero = jnp.zeros_like(rows)
    top = jnp.where(keep & low, rows, zero)
    bottom = jnp.where(keep & ~low, rows, zero)
    return jnp.concatenate([top, bottom], 0).astype(BF)


def masks():
    low = lax.broadcasted_iota(jnp.int32, (64, 128), 1) < 64
    keep = lax.broadcasted_iota(jnp.int32, (64, 128), 0) < SEQ
    return low, keep


def forward_kernel(first, *refs):
    x_in, *masters, vec = refs[:6]
    outs = list(refs[6:-6])
    p_img, a_img, mixed, middle, act, slope, sums, w_attn, w_out, w_up, w_down, x_out = outs[:12]
    proj, heads, normed, hidden, stream, totals = refs[-6:]
    if first:
        stream = outs[12]
    step = pl.program_id(0)

    @pl.when(step == 0)
    def _():
        totals[...] = jnp.zeros_like(totals)
        for low, master in zip((w_attn, w_out, w_up, w_down), masters):
            low[...] = master[...].astype(BF)
        for block in range(9):
            proj[block, RUN : RUN + 16, :] = jnp.zeros((16, 128), F32)
        for block in range(3):
            heads[block, REAL - 4 : RUN + 16, :] = jnp.zeros((RUN + 20 - REAL, 128), F32)

    if first:
        stream[0, REAL - 4 : RUN, :] = jnp.zeros((RUN + 4 - REAL, D), F32)
        for image in range(IMG):
            stream[0, SEQ * image : SEQ * (image + 1), :] = x_in[image].astype(F32)
    else:
        stream = x_in

    def norm_block(i, carry):
        rows = pl.ds(pl.multiple_of(i * 64, 64), 64)
        unit, _ = normalise(stream[0, rows, :])
        normed[rows, :] = (unit * vec[0:1, G1:B1] + vec[0:1, B1:BQ]).astype(BF)
        return carry

    lax.fori_loop(0, RUN // 64, norm_block, 0)

    for third in range(3):
        result = dot(normed[...], w_attn[0, :, D * third : D * (third + 1)])
        if third == 0:
            result = result + vec[0:1, BQ:BV]
        if third == 2:
            result = result + vec[0:1, BV:BO]
        for block in range(3):
            proj[3 * third + block, 0:RUN, :] = result[:, 128 * block : 128 * (block + 1)]

    low, keep = masks()
    keep_keys = keep[0:56]

    def attend(i, carry):
        items = [(i * TOGETHER + k, pair) for k in range(TOGETHER) for pair in range(3)]
        loaded = []
        for image, pair in items:
            at = pl.ds(image * SEQ, 64)
            query = proj[pair, at, :]
            key = jnp.where(keep, proj[3 + pair, at, :], 0.0).astype(BF)
            value = jnp.where(keep, proj[6 + pair, at, :], 0.0).astype(BF)
            p_img[image, pair] = jnp.where(keep, query, 0.0).astype(BF)
            p_img[image, 3 + pair] = key
            p_img[image, 6 + pair] = value
            loaded.append((key, halves_of(query * 0.125, low, keep), value))
        scores = [dot(key, spread, 1, 1)[0:56] for key, spread, _ in loaded]
        weights = []
        for (image, pair), score in zip(items, scores):
            score = jnp.where(keep_keys, score, -1e30)
            raised = jnp.exp(score - jnp.max(score, 0, keepdims=True))
            weight = raised * (1.0 / jnp.sum(raised, 0, keepdims=True))
            weight = jnp.concatenate([weight, jnp.zeros((8, 128), F32)], 0).astype(BF)
            a_img[image, pair] = weight
            weights.append(weight)
        results = [dot(weight, value, 0, 0) for weight, (_, _, value) in zip(weights, loaded)]
        for (image, pair), both in zip(items, results):
            one = jnp.where(low, both[0:64], both[64:128])
            heads[pair, pl.ds(image * SEQ, SEQ), :] = one[0:SEQ]
        return carry

    lax.fori_loop(0, IMG // TOGETHER, attend, 0)

    for block in range(3):
        mixed[0, :, 128 * block : 128 * (block + 1)] = heads[block, 0:RUN, :].astype(BF)

    def mlp(i, carry):
        base = pl.multiple_of(i * STEP_ROWS, STEP_ROWS)
        rows = pl.ds(base, STEP_ROWS)
        real = lax.broadcasted_iota(jnp.int32, (STEP_ROWS, D), 0) + base < REAL
        before = stream[0, rows, :]
        branch = dot(mixed[0, rows, :], w_out[0]) + vec[0:1, BO:G2]
        between = before + branch
        middle[0, rows, :] = between
        unit, _ = normalise(between)
        normed_two = (unit * vec[0:1, G2:B2] + vec[0:1, B2:BU]).astype(BF)
        totals[0:8, :] += fold(jnp.where(real, before * before, 0.0))
        totals[8:16, :] += fold(jnp.where(real, branch * branch, 0.0))
        hidden[...] = dot(normed_two, w_up[0])
        for row in range(0, STEP_ROWS, 32):
            for column in range(0, FF, 256):
                part = hidden[row : row + 32, column : column + 256]
                part = part + vec[0:1, BU + column : BU + column + 256]
                bent, tilt = gelu_parts(part)
                at = pl.ds(base + row, 32)
                act[0, at, column : column + 256] = bent.astype(BF)
                slope[0, at, column : column + 256] = tilt.astype(BF)
        tail = dot(act[0, rows, :], w_down[0]) + vec[0:1, BD : BD + D]
        totals[16:24, :] += fold(jnp.where(real, tail * tail, 0.0))
        after = middle[0, rows, :] + tail
        if first:
            x_out[0, rows, :] = after
        else:
            hidden_stream[rows, :] = after
        return carry

    hidden_stream = refs[-2] if not first else None
    lax.fori_loop(0, RUN // STEP_ROWS, mlp, 0)

    if not first:
        for image in range(IMG):
            x_out[image] = hidden_stream[SEQ * image : SEQ * (image + 1), :].astype(BF)

    @pl.when(step == CHUNKS - 1)
    def _():
        lane = lax.broadcasted_iota(jnp.int32, (1, 128), 1)
        row = jnp.zeros((1, 128), F32)
        for k in range(3):
            row = jnp.where(lane == SUMS_AT + k, jnp.sum(totals[8 * k : 8 * k + 8, :]), row)
        sums[...] = row


def chunked(*dims):
    return pl.BlockSpec((1,) + dims, lambda c: (c,) + (0,) * len(dims))


def imaged(*dims):
    return pl.BlockSpec((IMG,) + dims, lambda c: (c,) + (0,) * len(dims))


WEIGHT_SIZES = ((D, 3 * D), (D, D), (D, FF), (FF, D))


def weight_specs(layer):
    return [
        pl.BlockSpec((1,) + s, lambda c: (layer, 0, 0), pipeline_mode=pl.Buffered(1))
        for s in WEIGHT_SIZES
    ] + [pl.BlockSpec((1, 12 * D), lambda c: (0, 0))]


def whole(*dims):
    return pl.BlockSpec(dims, lambda c: (0,) * len(dims))


def shape(kind, *dims):
    return jax.ShapeDtypeStruct(dims, kind)


def forward(layer, x_in, masters, vector):
    first = layer == 0
    out_shape = [
        shape(BF, IMG * CHUNKS, 9, 64, 128),
        shape(BF, IMG * CHUNKS, 3, 64, 128),
        shape(BF, CHUNKS, RUN, D),
        shape(F32, CHUNKS, RUN, D),
        shape(BF, CHUNKS, RUN, FF),
        shape(BF, CHUNKS, RUN, FF),
        shape(F32, 1, 128),
    ]
    out_specs = [
        imaged(9, 64, 128),
        imaged(3, 64, 128),
        chunked(RUN, D),
        chunked(RUN, D),
        chunked(RUN, FF),
        chunked(RUN, FF),
        whole(1, 128),
    ]
    out_shape += [shape(BF, 1, *size) for size in WEIGHT_SIZES]
    out_specs += [whole(1, *size) for size in WEIGHT_SIZES]
    if first:
        out_shape += [shape(F32, CHUNKS, RUN, D)] * 2
        out_specs += [chunked(RUN, D)] * 2
    else:
        out_shape += [shape(BF, IMG * CHUNKS, SEQ, D)]
        out_specs += [imaged(SEQ, D)]
    return pl.pallas_call(
        lambda *refs: forward_kernel(first, *refs),
        grid=(CHUNKS,),
        out_shape=out_shape,
        in_specs=[imaged(SEQ, D) if first else chunked(RUN, D)] + weight_specs(layer),
        out_specs=out_specs,
        scratch_shapes=[
            pltpu.VMEM((9, RUN + 16, 128), F32),
            pltpu.VMEM((3, RUN + 16, 128), F32),
            pltpu.VMEM((RUN, D), BF),
            pltpu.VMEM((STEP_ROWS, FF), F32),
            pltpu.VMEM((RUN, D), F32),
            pltpu.VMEM((24, D), F32),
        ],
        compiler_params=pltpu.CompilerParams(vmem_limit_bytes=56 * 2**20),
        name=f"forward_{layer}",
    )(x_in, *masters, vector[layer : layer + 1])


def emit_packed(core, plan, keep, send):
    def emit(halves):
        @pl.loop(0, 16)
        def _(block):
            deep, high = block // 4, block % 4

            def target(k):
                if k < 4:
                    return halves[0].at[k, high, deep]
                return halves[1].at[high, k - 4, deep]

            for source, start, each, width in plan:
                height = 8 * each
                base = pl.multiple_of(block * height, 8)
                for column in range(width):
                    rows = source[pl.ds(base, height), column * 128 : (column + 1) * 128]
                    at = start + each * column
                    for k in range(8):
                        target(k)[at : at + each, :] = rows[each * k : each * (k + 1)]

    @pl.when(core == 0)
    def _():
        emit((keep, send))

    @pl.when(core == 1)
    def _():
        emit((send, keep))


def back_mlp(r, grad):
    vec = r["vec"]

    def block(i, carry):
        base = pl.multiple_of(i * STEP_ROWS, STEP_ROWS)
        rows = pl.ds(base, STEP_ROWS)
        here = grad[0, rows, :]
        r["acc_vec"][:, BD : BD + D] += fold(here)
        here_low = here.astype(BF)
        r["low_grad"][rows, :] = here_low
        r["d_act"][...] = dot(here_low, r["w_down"][0], 1, 1)
        for column in range(0, FF, 256):
            total = jnp.zeros((8, 256), F32)
            for row in range(0, STEP_ROWS, 32):
                at = pl.ds(base + row, 32)
                part = r["d_act"][row : row + 32, column : column + 256]
                part = part * r["slope"][0, at, column : column + 256].astype(F32)
                r["d_hidden"][at, column : column + 256] = part.astype(BF)
                total = total + fold(part)
            r["acc_vec"][:, BU + column : BU + column + 256] += total
        d_normed = dot(r["d_hidden"][rows, :], r["w_up"][0], 1, 1)
        unit, rate = normalise(r["middle"][0, rows, :])
        gain = vec[0:1, G2:B2]
        r["normed"][rows, :] = (unit * gain + vec[0:1, B2:BU]).astype(BF)
        r["acc_vec"][:, G2:B2] += fold(d_normed * unit)
        r["acc_vec"][:, B2:BU] += fold(d_normed)
        between = grad[0, rows, :] + norm_back(d_normed, unit, rate, gain)
        r["d_mid"][0, rows, :] = between
        return carry

    lax.fori_loop(0, RUN // STEP_ROWS, block, 0)
    r["acc_down"][...] += dot(r["act"][0], r["low_grad"][...], 0, 0)
    r["acc_up"][...] += dot(r["normed"][...], r["d_hidden"][...], 0, 0)


def back_attention(r, d_mid, store):
    vec = r["vec"]

    def branch(i, carry):
        rows = pl.ds(pl.multiple_of(i * STEP_ROWS, STEP_ROWS), STEP_ROWS)
        between = d_mid[0, rows, :]
        r["acc_vec"][:, BO:G2] += fold(between)
        between = between.astype(BF)
        r["d_branch"][rows, :] = between
        result = dot(between, r["w_out"][0], 1, 1)
        for block in range(3):
            r["d_heads"][block, rows, :] = result[:, 128 * block : 128 * (block + 1)]
        return carry

    lax.fori_loop(0, RUN // STEP_ROWS, branch, 0)
    r["acc_out"][...] += dot(r["mixed"][0], r["d_branch"][...], 0, 0)
    low, keep = masks()
    p_img, a_img, d_heads, d_proj = r["p_img"], r["a_img"], r["d_heads"], r["d_proj"]

    def attend(i, carry):
        items = [(i * TOGETHER_BACK + k, pair) for k in range(TOGETHER_BACK) for pair in range(3)]
        loaded = []
        for image, pair in items:
            rows = d_heads[pair, pl.ds(image * SEQ, 64), :]
            spread = halves_of(p_img[image, pair].astype(F32) * 0.125, low, keep)
            loaded.append((spread, halves_of(rows, low, keep)))
        d_weights = [
            dot(p_img[image, 6 + pair], d_spread, 1, 1)
            for (image, pair), (_, d_spread) in zip(items, loaded)
        ]
        d_values = [
            dot(a_img[image, pair], d_spread) for (image, pair), (_, d_spread) in zip(items, loaded)
        ]
        d_scores = []
        for (image, pair), d_weight in zip(items, d_weights):
            weight = a_img[image, pair].astype(F32)
            product = weight * d_weight
            d_scores.append((product - weight * jnp.sum(product, 0, keepdims=True)).astype(BF))
        d_keys = [dot(d_score, spread) for d_score, (spread, _) in zip(d_scores, loaded)]
        d_both = [
            dot(d_score, p_img[image, 3 + pair], 0, 0)
            for (image, pair), d_score in zip(items, d_scores)
        ]
        for (image, pair), d_key, both, d_value in zip(items, d_keys, d_both, d_values):
            d_query = jnp.where(low, both[0:64], both[64:128]) * 0.125
            at = pl.ds(image * SEQ, SEQ)
            d_proj[pair, at, :] = d_query[0:SEQ]
            d_proj[3 + pair, at, :] = d_key[0:SEQ]
            d_proj[6 + pair, at, :] = d_value[0:SEQ]
        return carry

    lax.fori_loop(0, IMG // TOGETHER_BACK, attend, 0)

    def tail(i, carry):
        rows = pl.ds(pl.multiple_of(i * STEP_ROWS, STEP_ROWS), STEP_ROWS)
        for block in range(9):
            part = d_proj[block, rows, :]
            r["d_low"][rows, 128 * block : 128 * (block + 1)] = part.astype(BF)
            if block < 3:
                r["acc_vec"][:, BQ + 128 * block : BQ + 128 * (block + 1)] += fold(part)
            if block >= 6:
                r["acc_vec"][:, BV + 128 * (block - 6) : BV + 128 * (block - 5)] += fold(part)
        d_normed = dot(r["d_low"][rows, :], r["w_attn"][0], 1, 1)
        unit, rate = normalise(r["stream"][0, rows, :])
        gain = vec[0:1, G1:B1]
        r["normed"][rows, :] = (unit * gain + vec[0:1, B1:BQ]).astype(BF)
        r["acc_vec"][:, G1:B1] += fold(d_normed * unit)
        r["acc_vec"][:, B1:BQ] += fold(d_normed)
        store(rows, d_mid[0, rows, :] + norm_back(d_normed, unit, rate, gain))
        return carry

    lax.fori_loop(0, RUN // STEP_ROWS, tail, 0)
    r["acc_attn"][...] += dot(r["normed"][...], r["d_low"][...], 0, 0)


def backward_kernel(names, last, with_mlp, with_attention, *refs):
    r = dict(zip(names, refs))
    step = pl.program_id(0)

    @pl.when(step == 0)
    def _():
        for name in ("acc_attn", "acc_out", "acc_up", "acc_down", "acc_vec"):
            if name not in r:
                continue
            ref = r[name]

            @pl.loop(0, ref.shape[0] // 8)
            def _(i):
                rows = pl.ds(pl.multiple_of(i * 8, 8), 8)
                if name == "acc_vec" and not with_mlp:
                    ref[...] = r["vec_sums"][...]
                else:
                    ref[rows, :] = jnp.zeros((8, ref.shape[1]), F32)

        if with_attention:
            for block in range(3):
                r["d_heads"][block, RUN : RUN + 16, :] = jnp.zeros((16, 128), F32)
            for block in range(9):
                r["d_proj"][block, REAL - 4 : RUN + 16, :] = jnp.zeros((RUN + 20 - REAL, 128), F32)

    grad = r["grad_in"]
    if last:
        grad = r["grad"]
        grad[0, REAL - 4 : RUN, :] = jnp.zeros((RUN + 4 - REAL, D), F32)
        for image in range(IMG):
            grad[0, SEQ * image : SEQ * (image + 1), :] = r["grad_in"][image].astype(F32)
    plan = []
    if with_mlp:
        back_mlp(r, grad)
        plan += [(r["acc_up"], UP_AT, 3, 12), (r["acc_down"], DOWN_AT, 12, 3)]
    if with_attention:
        shift = 0 if with_mlp else QKV_AT
        plan += [(r["acc_attn"], QKV_AT - shift, 3, 9), (r["acc_out"], PROJ_AT - shift, 3, 3)]
        plan += [(r["small"], SMALL_AT - shift, 1, 1)]
        middle = r["d_mid"] if with_mlp else grad
        result = r["grad_out"] if last else r["grad"]

        def store(rows, value):
            result[0, rows, :] = value

        back_attention(r, middle, store)
        if not last:
            for image in range(IMG):
                r["grad_out"][image] = result[0, SEQ * image : SEQ * (image + 1), :]

    @pl.when(step == CHUNKS - 1)
    def _():
        if with_attention:
            small = r["small"]
            total = jnp.sum(r["acc_vec"][...], 0, keepdims=True)
            small[...] = jnp.broadcast_to(r["sums"][...], (128, 128))
            for owner in range(128):
                small[owner : owner + 1, 0:36] = total[:, 36 * owner : 36 * (owner + 1)]
        else:
            r["vec_sums"][...] = r["acc_vec"][...]
        emit_packed(r["core"][0], plan, r["keep"], r["send"])


def backward(layer, last, with_mlp, with_attention, core, grad_in, vector, saved):
    rows = (72 if with_mlp else 0) + (40 if with_attention else 0)
    half = shape(F32, 4, 4, 4, rows, 128)
    half_spec = whole(4, 4, 4, rows, 128)
    specs = weight_specs(0)
    ins = {
        "core": (core, pl.BlockSpec(memory_space=pltpu.SMEM)),
        "grad_in": (grad_in, imaged(SEQ, D) if last else chunked(RUN, D)),
        "vec": (vector[layer : layer + 1], specs[4]),
    }
    stream_shape, stream_spec = shape(F32, CHUNKS, RUN, D), chunked(RUN, D)
    outs = {"keep": (half, half_spec), "send": (half, half_spec)}
    scratch = {
        "grad": pltpu.VMEM((1, RUN, D), F32),
        "normed": pltpu.VMEM((RUN, D), BF),
        "acc_vec": pltpu.VMEM((8, 12 * D), F32),
    }
    if with_mlp:
        ins["w_up"] = (saved["w_up"], specs[2])
        ins["w_down"] = (saved["w_down"], specs[3])
        ins["middle"] = (saved["middle"], chunked(RUN, D))
        ins["act"] = (saved["act"], chunked(RUN, FF))
        ins["slope"] = (saved["slope"], chunked(RUN, FF))
        scratch["low_grad"] = pltpu.VMEM((RUN, D), BF)
        scratch["d_act"] = pltpu.VMEM((STEP_ROWS, FF), F32)
        scratch["d_hidden"] = pltpu.VMEM((RUN, FF), BF)
        scratch["acc_up"] = pltpu.VMEM((D, FF), F32)
        scratch["acc_down"] = pltpu.VMEM((FF, D), F32)
        if with_attention:
            scratch["d_mid"] = pltpu.VMEM((1, RUN, D), F32)
        else:
            outs["d_mid"] = (stream_shape, stream_spec)
            outs["vec_sums"] = (shape(F32, 8, 12 * D), whole(8, 12 * D))
    if with_attention:
        ins["w_attn"] = (saved["w_attn"], specs[0])
        ins["w_out"] = (saved["w_out"], specs[1])
        ins["p_img"] = (saved["p_img"], imaged(9, 64, 128))
        ins["a_img"] = (saved["a_img"], imaged(3, 64, 128))
        ins["mixed"] = (saved["mixed"], chunked(RUN, D))
        ins["sums"] = (saved["sums"], whole(1, 128))
        ins["stream"] = (saved["stream"], chunked(RUN, D))
        if not with_mlp:
            ins["vec_sums"] = (saved["vec_sums"], whole(8, 12 * D))
        outs["grad_out"] = (
            (stream_shape, stream_spec)
            if last
            else (shape(F32, IMG * CHUNKS, SEQ, D), imaged(SEQ, D))
        )
        scratch["d_branch"] = pltpu.VMEM((RUN, D), BF)
        scratch["d_heads"] = pltpu.VMEM((3, RUN + 16, 128), F32)
        scratch["d_proj"] = pltpu.VMEM((9, RUN + 16, 128), F32)
        scratch["d_low"] = pltpu.VMEM((RUN, 3 * D), BF)
        scratch["acc_attn"] = pltpu.VMEM((D, 3 * D), F32)
        scratch["acc_out"] = pltpu.VMEM((D, D), F32)
        scratch["small"] = pltpu.VMEM((128, 128), F32)
    limit = 60 if with_mlp and with_attention else 44
    names = [*ins, *outs, *scratch]
    results = pl.pallas_call(
        lambda *refs: backward_kernel(names, last, with_mlp, with_attention, *refs),
        grid=(CHUNKS,),
        out_shape=[v[0] for v in outs.values()],
        in_specs=[v[1] for v in ins.values()],
        out_specs=[v[1] for v in outs.values()],
        scratch_shapes=list(scratch.values()),
        compiler_params=pltpu.CompilerParams(vmem_limit_bytes=limit * 2**20),
        name=f"backward_{layer}" + "m" * with_mlp + "a" * with_attention,
    )(*[v[0] for v in ins.values()])
    return dict(zip(outs, results))


def forward_saved(layer, x_in, masters, vector):
    names = ["p_img", "a_img", "mixed", "middle", "act", "slope", "sums"]
    names += ["w_attn", "w_out", "w_up", "w_down", "x_out", "stream"]
    saved = dict(zip(names, forward(layer, x_in, masters, vector)))
    saved.setdefault("stream", x_in)
    return saved


def local_step(core, tokens, grad_out, masters, vector, between=lambda packed: packed):
    zero = forward_saved(0, tokens, masters, vector)
    one = forward_saved(1, zero["x_out"], masters, vector)
    back_one = backward(1, True, True, True, core, grad_out, vector, one)
    packed_one = (back_one["keep"], back_one["send"])
    mlp = backward(0, False, True, False, core, back_one["grad_out"], vector, zero)
    zero["vec_sums"] = mlp["vec_sums"]
    d_mid, packed_one = lax.optimization_barrier((mlp["d_mid"], between(packed_one)))
    tail = backward(0, False, False, True, core, d_mid, vector, zero)
    packed_zero = [mlp["keep"], mlp["send"], tail["keep"], tail["send"]]
    return one["x_out"], tail["grad_out"], packed_zero, packed_one


def stage_position(stage):
    deep, high, core, across = place_of(lax.axis_index(GROUP_AXES))
    if stage == 2:
        return deep
    return jnp.where(core == stage, across, high)


def add_core_kernel(count, *refs):
    me = stage_position(0)
    outs = refs[2 * count :]
    for shift in range(4):
        at = (me + shift) % 4

        @pl.loop(0, 16)
        def _(i):
            row = 0
            for k in range(count):
                keep, got = refs[2 * k : 2 * k + 2]
                end = row + keep.shape[3]
                value = keep[at, i // 4, i % 4] + got[at, i // 4, i % 4]
                outs[shift][i // 4, i % 4, row:end] = value
                row = end


def add_ring_kernel(stage, count, *refs):
    values, outs = refs[: 4 * count], refs[4 * count :]
    if stage == 3:
        own, one, two, three = values
        outs[0][...] = (own[...] + one[...]) + (two[...] + three[...])
        return
    me = stage_position(stage)
    for shift in range(4):
        at = (me + shift) % 4
        if stage == 2:
            own, one, two, three = values
            outs[shift][...] = (own[at] + one[at]) + (two[at] + three[at])
        else:

            @pl.loop(0, 4)
            def _(i):
                for layer in range(2):
                    own, one, two, three = values[4 * layer : 4 * layer + 4]
                    outs[shift][i, layer] = (own[at, i] + one[at, i]) + (two[at, i] + three[at, i])


def call_add(kernel, values, out_dims, count, name):
    return pl.pallas_call(
        kernel,
        out_shape=[jax.ShapeDtypeStruct(out_dims + (ROWS, 128), jnp.float32)] * count,
        in_specs=[VMEM_WHOLE] * len(values),
        out_specs=[VMEM_WHOLE] * count,
        compiler_params=pltpu.CompilerParams(vmem_limit_bytes=32 * 2**20),
        name=name,
    )(*values)


def ring(stage, parts):
    got = [lax.ppermute(parts[s], GROUP_AXES, ring_pairs(stage, s)) for s in range(1, 4)]
    return [parts[0]] + got


def core_sums(packed, name):
    values = core_swap(packed)
    count = len(packed) // 2
    return call_add(lambda *a: add_core_kernel(count, *a), values, (4, 4), 4, name)


def core_swap(packed):
    values = []
    for keep, send in zip(packed[::2], packed[1::2]):
        values += [keep, lax.ppermute(send, GROUP_AXES, core_pairs())]
    return values


def start_one(packed):
    return core_sums(packed, "add_core_one")


def finish_sums(packed_zero, parts_one):
    parts_one = ring(0, parts_one)
    packed_zero[3], parts_one = lax.optimization_barrier((packed_zero[3], parts_one))
    parts_zero = ring(0, core_sums(packed_zero, "add_core_zero"))
    parts = parts_zero + parts_one
    parts = call_add(lambda *a: add_ring_kernel(1, 2, *a), parts, (4, 2), 4, "add_first")
    parts = ring(1, parts)
    parts = call_add(lambda *a: add_ring_kernel(2, 1, *a), parts, (2,), 4, "add_second")
    parts = ring(2, parts)
    return call_add(lambda *a: add_ring_kernel(3, 1, *a), parts, (2,), 1, "add_third")[0]


def adam_step(gradient, moment_one, moment_two, weight, rate):
    moment_one = beta_one * moment_one + (1 - beta_one) * gradient
    moment_two = beta_two * moment_two + (1 - beta_two) * gradient * gradient
    fix_one = 1 - beta_one**STEP
    fix_two = 1 - beta_two**STEP
    update = (
        moment_one / fix_one / (jnp.sqrt(moment_two / fix_two) + adam_eps) + decay_rate * weight
    )
    return (moment_one, moment_two, weight - rate * update)


def finish_kernel(*refs):
    own, other = ([ref.at[k] for k in range(2)] for ref in refs[:2])
    weights, firsts, seconds, outers = (refs[2 + 5 * k : 7 + 5 * k] for k in range(4))
    outs = refs[22:]
    new_firsts, new_seconds, changes, new_outers, finals, copies = (
        outs[5 * k : 5 * k + 5] for k in range(6)
    )
    rms = outs[30]

    def gathered(refs, kind, row):
        if kind == 4:
            return jnp.concatenate([ref[SMALL_AT : SMALL_AT + 1, 0:36] for ref in refs], 0)
        start, rows, width = (
            (QKV_AT, 3, 9),
            (PROJ_AT, 3, 3),
            (UP_AT, 3, 12),
            (DOWN_AT, 12, 3),
        )[kind]
        lines = [start + rows * c + row for c in range(width)]
        return jnp.concatenate(
            [
                jnp.concatenate([ref[line : line + 1, :] for ref in refs], 0)
                for line in lines
            ],
            1,
        )

    for kind in range(5):
        rate = rates()[kind]
        for row in range(1 if kind == 4 else weights[kind].shape[0]):
            at = slice(None) if kind == 4 else row
            weight = weights[kind][at]
            moments = (firsts[kind][at], seconds[kind][at])
            one, two, updated = adam_step(gathered(own, kind, row), *moments, weight, rate)
            updated_other = adam_step(gathered(other, kind, row), *moments, weight, rate)[2]
            change = ((weight - updated) + (weight - updated_other)) / 2
            outer = outer_decay * outers[kind][at] + change
            final = weight - outer_rate * (change + outer_decay * outer)
            new_firsts[kind][at] = one
            new_seconds[kind][at] = two
            changes[kind][at] = change
            new_outers[kind][at] = outer
            finals[kind][at] = final
            copies[kind][at] = final.astype(jnp.bfloat16)
    for layer in range(2):
        totals = [
            ref[SMALL_AT : SMALL_AT + 1, SUMS_AT : SUMS_AT + 3] for ref in (own[layer], other[layer])
        ]
        rms[layer : layer + 1, :] = jnp.sqrt((totals[0] + totals[1]) / ENTRIES)


ENTRIES = 98304000


def rows_first(value):
    return value if value.ndim == 2 else jnp.swapaxes(value, 0, 1)


def finish(own, other, weights, firsts, seconds, outers):
    given = [rows_first(v) for v in (*weights, *firsts, *seconds, *outers)]
    full = [jax.ShapeDtypeStruct(v.shape, jnp.float32) for v in given[:5]]
    low = [jax.ShapeDtypeStruct(v.shape, jnp.bfloat16) for v in given[:5]]
    results = pl.pallas_call(
        finish_kernel,
        out_shape=full * 5 + low + [jax.ShapeDtypeStruct((2, 3), jnp.float32)],
        in_specs=[VMEM_WHOLE] * 22,
        out_specs=[VMEM_WHOLE] * 31,
        name="finish",
    )(own, other, *given)
    results = [rows_first(v) for v in results[:30]] + [results[30]]
    return [v[None] for v in results[:10]] + results[10:]

def body(
    tokens,
    grad_out,
    weight_qkv,
    weight_proj,
    weight_up,
    weight_down,
    weight_vector,
    old_first_qkv,
    old_first_proj,
    old_first_up,
    old_first_down,
    old_first_vector,
    old_second_qkv,
    old_second_proj,
    old_second_up,
    old_second_down,
    old_second_vector,
    old_outer_qkv,
    old_outer_proj,
    old_outer_up,
    old_outer_down,
    old_outer_vector,
):
    masters = (weight_qkv, weight_proj, weight_up, weight_down, weight_vector)
    old_firsts = (old_first_qkv, old_first_proj, old_first_up, old_first_down, old_first_vector)
    old_seconds = (
        old_second_qkv,
        old_second_proj,
        old_second_up,
        old_second_down,
        old_second_vector,
    )
    old_outers = (old_outer_qkv, old_outer_proj, old_outer_up, old_outer_down, old_outer_vector)
    owner_index = lax.axis_index(GROUP_AXES)
    core = jnp.reshape(owner_index // 4 % 2, (1,)).astype(jnp.int32)
    block_out, grad_tokens, packed_zero, parts_one = local_step(
        core, tokens, grad_out, masters[:4], weight_vector, start_one
    )
    shares = []
    for kind_index in range(5):
        share_rows = old_firsts[kind_index].shape[1]
        shares.append(
            lax.dynamic_slice_in_dim(masters[kind_index], owner_index * share_rows, share_rows, 1)
        )
    own = finish_sums(packed_zero, parts_one)
    other = lax.ppermute(own, "grp", [(0, 1), (1, 0)])
    results = finish(own, other, shares, old_firsts, old_seconds, old_outers)
    return (block_out, grad_tokens, *results)


def solution(mesh):
    placed = (
        P(("grp", "wide", "narrow"), None, None),
        P(("grp", "wide", "narrow"), None, None),
        P(),
        P(),
        P(),
        P(),
        P(),
        P(None, ("wide", "narrow"), None),
        P(None, ("wide", "narrow"), None),
        P(None, ("wide", "narrow"), None),
        P(None, ("wide", "narrow"), None),
        P(None, ("wide", "narrow")),
        P(None, ("wide", "narrow"), None),
        P(None, ("wide", "narrow"), None),
        P(None, ("wide", "narrow"), None),
        P(None, ("wide", "narrow"), None),
        P(None, ("wide", "narrow")),
        P(None, ("wide", "narrow"), None),
        P(None, ("wide", "narrow"), None),
        P(None, ("wide", "narrow"), None),
        P(None, ("wide", "narrow"), None),
        P(None, ("wide", "narrow")),
    )
    return jax.shard_map(
        body,
        mesh=mesh,
        in_specs=placed,
        out_specs=(
            P(("grp", "wide", "narrow"), None, None),
            P(("grp", "wide", "narrow"), None, None),
            P("grp", None, ("wide", "narrow"), None),
            P("grp", None, ("wide", "narrow"), None),
            P("grp", None, ("wide", "narrow"), None),
            P("grp", None, ("wide", "narrow"), None),
            P("grp", None, ("wide", "narrow")),
            P("grp", None, ("wide", "narrow"), None),
            P("grp", None, ("wide", "narrow"), None),
            P("grp", None, ("wide", "narrow"), None),
            P("grp", None, ("wide", "narrow"), None),
            P("grp", None, ("wide", "narrow")),
            P(None, ("wide", "narrow"), None),
            P(None, ("wide", "narrow"), None),
            P(None, ("wide", "narrow"), None),
            P(None, ("wide", "narrow"), None),
            P(None, ("wide", "narrow")),
            P(None, ("wide", "narrow"), None),
            P(None, ("wide", "narrow"), None),
            P(None, ("wide", "narrow"), None),
            P(None, ("wide", "narrow"), None),
            P(None, ("wide", "narrow")),
            P(None, ("wide", "narrow"), None),
            P(None, ("wide", "narrow"), None),
            P(None, ("wide", "narrow"), None),
            P(None, ("wide", "narrow"), None),
            P(None, ("wide", "narrow")),
            P(None, ("wide", "narrow"), None),
            P(None, ("wide", "narrow"), None),
            P(None, ("wide", "narrow"), None),
            P(None, ("wide", "narrow"), None),
            P(None, ("wide", "narrow")),
            P(),
        ),
        check_vma=False,
    )
```

```python
import types
import typing

import jax
import jax.numpy as jnp
from jax import lax
from jax.experimental import pallas as pl
from jax.experimental.pallas import tpu as pltpu
from jax.sharding import PartitionSpec as P

D = 384
HEADS = 6
HEAD_DIM = 64
FF = 1536
SEQ = 50
STEP = 10


beta_one = 0.9
beta_two = 0.95
adam_eps = 1e-08
decay_rate = 0.1
outer_decay = 0.9
outer_rate = 0.7

ROWS = 112
UP_AT, DOWN_AT, QKV_AT, PROJ_AT, SMALL_AT = 0, 36, 72, 99, 108
SUMS_AT = 64
ENTRIES = 98304000
VMEM_WHOLE = pl.BlockSpec(memory_space=pltpu.VMEM)
ANYWHERE = pl.BlockSpec(memory_space=pl.ANY)
GROUP_AXES = ("wide", "narrow")
IMG = 10
CHUNKS = 2
RUN = 512
REAL = IMG * SEQ
TOGETHER = 5
TOGETHER_BACK = 5
G1, B1, BQ, BV, BO, G2, B2, BU, BD = 0, 384, 768, 1152, 1536, 1920, 2304, 2688, 4224
BF = jnp.bfloat16
F32 = jnp.float32
WEIGHT_SIZES = ((D, 3 * D), (D, D), (D, FF), (FF, D))


def rates():
    return (1.5 * D ** (-0.5), 1.5 * (D // 4) ** (-0.5), 1.5 * D ** (-0.5), 1.5 * FF ** (-0.5), 2.0)


def place_of(owner):
    return owner // 32, owner // 8 % 4, owner // 4 % 2, owner % 4


def owner_of(deep, high, core, across):
    return ((deep * 4 + high) * 2 + core) * 4 + across


def core_pairs():
    return [(o, o ^ 4) for o in range(128)]


def ring_pairs(stage, shift):
    pairs = []
    for o in range(128):
        deep, high, core, across = place_of(o)
        if stage == 2:
            deep = deep ^ shift
        elif core == stage:
            across = across ^ shift
        else:
            high = high ^ shift
        pairs.append((o, owner_of(deep, high, core, across)))
    return pairs


def dot(left, right, left_dim=1, right_dim=0):
    return lax.dot_general(
        left, right, (((left_dim,), (right_dim,)), ((), ())), preferred_element_type=F32
    )


def normalise(rows):
    center = rows - jnp.sum(rows, -1, keepdims=True) * (1 / D)
    rate = lax.rsqrt(jnp.sum(center * center, -1, keepdims=True) * (1 / D) + 1e-06)
    return center * rate, rate


def norm_back(grad, unit, rate, gain):
    scaled = grad * gain
    first = jnp.sum(scaled, -1, keepdims=True) * (1 / D)
    second = jnp.sum(scaled * unit, -1, keepdims=True) * (1 / D)
    return rate * (scaled - first - unit * second)


def gelu_parts(value):
    area = 0.5 + 0.5 * lax.erf(value * 0.7071067811865476)
    bell = jnp.exp(-0.5 * value * value)
    return value * area, area + value * bell * 0.3989422804014327


def fold(values):
    return jnp.sum(values.reshape(-1, 8, values.shape[-1]), 0)


def halves_of(rows, low, keep):
    zero = jnp.zeros_like(rows)
    top = jnp.where(keep & low, rows, zero)
    bottom = jnp.where(keep & ~low, rows, zero)
    return jnp.concatenate([top, bottom], 0).astype(BF)


def masks():
    low = lax.broadcasted_iota(jnp.int32, (64, 128), 1) < 64
    keep = lax.broadcasted_iota(jnp.int32, (64, 128), 0) < SEQ
    return low, keep


def bias(r, start, stop):
    return r.vec[r.layer : r.layer + 1, start:stop]


def unpack(images, base, target):
    target[0, REAL - 4 : RUN, :] = jnp.zeros((RUN + 4 - REAL, D), F32)
    for image in range(IMG):
        target[0, SEQ * image : SEQ * (image + 1), :] = images[base + image].astype(F32)


def ahead_norm(r):
    def norm_block(i, carry):
        rows = pl.ds(pl.multiple_of(i * 64, 64), 64)
        unit, _ = normalise(r.stream[0, rows, :])
        r.normed[rows, :] = (unit * bias(r, G1, B1) + bias(r, B1, BQ)).astype(BF)
        return carry

    lax.fori_loop(0, RUN // 64, norm_block, 0)


def ahead_attention(r):
    proj, heads = r.proj, r.heads
    for third in range(3):
        result = dot(r.normed[...], r.w_attn[0, :, D * third : D * (third + 1)])
        if third == 0:
            result = result + bias(r, BQ, BV)
        if third == 2:
            result = result + bias(r, BV, BO)
        for block in range(3):
            proj[3 * third + block, 0:RUN, :] = result[:, 128 * block : 128 * (block + 1)]

    low, keep = masks()
    keep_keys = keep[0:56]

    def attend(i, carry):
        items = [(i * TOGETHER + k, pair) for k in range(TOGETHER) for pair in range(3)]
        loaded = []
        for image, pair in items:
            at = pl.ds(image * SEQ, 64)
            query = proj[pair, at, :]
            key = jnp.where(keep, proj[3 + pair, at, :], 0.0).astype(BF)
            value = jnp.where(keep, proj[6 + pair, at, :], 0.0).astype(BF)
            r.p_img[image, pair] = jnp.where(keep, query, 0.0).astype(BF)
            r.p_img[image, 3 + pair] = key
            r.p_img[image, 6 + pair] = value
            loaded.append((key, halves_of(query * 0.125, low, keep), value))
        scores = [dot(key, spread, 1, 1)[0:56] for key, spread, _ in loaded]
        weights = []
        for (image, pair), score in zip(items, scores):
            score = jnp.where(keep_keys, score, -1e30)
            raised = jnp.exp(score - jnp.max(score, 0, keepdims=True))
            weight = raised * (1.0 / jnp.sum(raised, 0, keepdims=True))
            weight = jnp.concatenate([weight, jnp.zeros((8, 128), F32)], 0).astype(BF)
            r.a_img[image, pair] = weight
            weights.append(weight)
        results = [dot(weight, value, 0, 0) for weight, (_, _, value) in zip(weights, loaded)]
        for (image, pair), both in zip(items, results):
            one = jnp.where(low, both[0:64], both[64:128])
            heads[pair, pl.ds(image * SEQ, SEQ), :] = one[0:SEQ]
        return carry

    lax.fori_loop(0, IMG // TOGETHER, attend, 0)
    for block in range(3):
        r.mixed[0, :, 128 * block : 128 * (block + 1)] = heads[block, 0:RUN, :].astype(BF)


def ahead_mlp(r):
    totals = r.totals
    real = lax.broadcasted_iota(jnp.int32, (RUN, D), 0) < REAL
    before = r.stream[0]
    branch = dot(r.mixed[0], r.w_out[0]) + bias(r, BO, G2)
    between = before + branch
    r.middle[0] = between
    totals[0:8, :] += fold(jnp.where(real, before * before, 0.0))
    totals[8:16, :] += fold(jnp.where(real, branch * branch, 0.0))

    def norm_block(i, carry):
        rows = pl.ds(pl.multiple_of(i * 64, 64), 64)
        unit, _ = normalise(r.middle[0, rows, :])
        r.normed[rows, :] = (unit * bias(r, G2, B2) + bias(r, B2, BU)).astype(BF)
        return carry

    lax.fori_loop(0, RUN // 64, norm_block, 0)
    r.hidden[...] = dot(r.normed[...], r.w_up[0])
    for row in range(0, RUN, 32):
        for column in range(0, FF, 256):
            part = r.hidden[row : row + 32, column : column + 256]
            part = part + bias(r, BU + column, BU + column + 256)
            bent, tilt = gelu_parts(part)
            r.act[0, row : row + 32, column : column + 256] = bent.astype(BF)
            r.slope[0, row : row + 32, column : column + 256] = tilt.astype(BF)
    tail = dot(r.act[0], r.w_down[0]) + bias(r, BD, BD + D)
    totals[16:24, :] += fold(jnp.where(real, tail * tail, 0.0))
    r.after[0] = r.middle[0] + tail


def total_row(totals):
    lane = lax.broadcasted_iota(jnp.int32, (1, 128), 1)
    row = jnp.zeros((1, 128), F32)
    for k in range(3):
        row = jnp.where(lane == SUMS_AT + k, jnp.sum(totals[8 * k : 8 * k + 8, :]), row)
    return row


def chunked(*dims):
    return pl.BlockSpec((1,) + dims, lambda c: (c,) + (0,) * len(dims))


def imaged(*dims):
    return pl.BlockSpec((IMG,) + dims, lambda c: (c,) + (0,) * len(dims))


def whole(*dims):
    return pl.BlockSpec(dims, lambda c: (0,) * len(dims))


def held(*dims):
    return pl.BlockSpec(dims, lambda c: (0,) * len(dims), pipeline_mode=pl.Buffered(1))


def shape(kind, *dims):
    return jax.ShapeDtypeStruct(dims, kind)


def emit_packed(core, plan):
    def emit(own):
        @pl.loop(0, 16)
        def _(block):
            deep, high = block // 4, block % 4
            for source, each, width, *targets in plan:
                height = 8 * each
                base = pl.multiple_of(block * height, 8)
                for column in range(width):
                    rows = source[pl.ds(base, height), column * 128 : (column + 1) * 128]
                    for k in range(8):
                        target, start = targets[0 if k // 4 == own else 1]
                        at = start + each * column
                        first, second = (k, high) if k < 4 else (high, k - 4)
                        target.at[first, second, deep][at : at + each, :] = rows[
                            each * k : each * (k + 1)
                        ]

    for own in range(2):

        @pl.when(core == own)
        def _():
            emit(own)


def back_mlp(r, grad):
    here = grad[0]
    r.acc_vec[:, BD : BD + D] += fold(here)
    r.low_grad[...] = here.astype(BF)
    r.hidden[...] = dot(r.low_grad[...], r.w_down[0], 1, 1)
    for column in range(0, FF, 256):
        total = jnp.zeros((8, 256), F32)
        for row in range(0, RUN, 32):
            at = slice(row, row + 32)
            part = r.hidden[at, column : column + 256]
            part = part * r.slope[0, at, column : column + 256].astype(F32)
            r.d_hidden[at, column : column + 256] = part.astype(BF)
            total = total + fold(part)
        r.acc_vec[:, BU + column : BU + column + 256] += total
    d_normed = dot(r.d_hidden[...], r.w_up[0], 1, 1)
    unit, rate = normalise(r.middle[0])
    gain = bias(r, G2, B2)
    r.normed[...] = (unit * gain + bias(r, B2, BU)).astype(BF)
    r.acc_vec[:, G2:B2] += fold(d_normed * unit)
    r.acc_vec[:, B2:BU] += fold(d_normed)
    r.d_mid[0] = grad[0] + norm_back(d_normed, unit, rate, gain)
    r.acc_down[...] = jnp.where(r.first, 0.0, r.acc_down[...]) + dot(r.act[0], r.low_grad[...], 0, 0)
    r.acc_up[...] = jnp.where(r.first, 0.0, r.acc_up[...]) + dot(r.normed[...], r.d_hidden[...], 0, 0)


def back_attention(r, d_mid, result):
    between = d_mid[0]
    r.acc_vec[:, BO:G2] += fold(between)
    r.d_branch[...] = between.astype(BF)
    product = dot(r.d_branch[...], r.w_out[0], 1, 1)
    for block in range(3):
        r.d_heads[block, 0:RUN, :] = product[:, 128 * block : 128 * (block + 1)]
    r.acc_out[...] = jnp.where(r.first, 0.0, r.acc_out[...]) + dot(r.mixed[0], r.d_branch[...], 0, 0)
    low, keep = masks()
    p_img, a_img, d_heads, d_proj = r.p_img, r.a_img, r.d_heads, r.proj
    for block in range(9):
        d_proj[block, REAL - 4 : RUN + 16, :] = jnp.zeros((RUN + 20 - REAL, 128), F32)

    def attend(i, carry):
        items = [(i * TOGETHER_BACK + k, pair) for k in range(TOGETHER_BACK) for pair in range(3)]
        loaded = []
        for image, pair in items:
            rows = d_heads[pair, pl.ds(image * SEQ, 64), :]
            spread = halves_of(p_img[image, pair].astype(F32) * 0.125, low, keep)
            loaded.append((spread, halves_of(rows, low, keep)))
        d_weights = [
            dot(p_img[image, 6 + pair], d_spread, 1, 1)
            for (image, pair), (_, d_spread) in zip(items, loaded)
        ]
        d_values = [
            dot(a_img[image, pair], d_spread) for (image, pair), (_, d_spread) in zip(items, loaded)
        ]
        d_scores = []
        for (image, pair), d_weight in zip(items, d_weights):
            weight = a_img[image, pair].astype(F32)
            product = weight * d_weight
            d_scores.append((product - weight * jnp.sum(product, 0, keepdims=True)).astype(BF))
        d_keys = [dot(d_score, spread) for d_score, (spread, _) in zip(d_scores, loaded)]
        d_both = [
            dot(d_score, p_img[image, 3 + pair], 0, 0)
            for (image, pair), d_score in zip(items, d_scores)
        ]
        for (image, pair), d_key, both, d_value in zip(items, d_keys, d_both, d_values):
            d_query = jnp.where(low, both[0:64], both[64:128]) * 0.125
            at = pl.ds(image * SEQ, SEQ)
            d_proj[pair, at, :] = d_query[0:SEQ]
            d_proj[3 + pair, at, :] = d_key[0:SEQ]
            d_proj[6 + pair, at, :] = d_value[0:SEQ]
        return carry

    lax.fori_loop(0, IMG // TOGETHER_BACK, attend, 0)
    for block in range(9):
        part = d_proj[block, 0:RUN, :]
        r.d_low[:, 128 * block : 128 * (block + 1)] = part.astype(BF)
        if block < 3:
            r.acc_vec[:, BQ + 128 * block : BQ + 128 * (block + 1)] += fold(part)
        if block >= 6:
            r.acc_vec[:, BV + 128 * (block - 6) : BV + 128 * (block - 5)] += fold(part)
    d_normed = dot(r.d_low[...], r.w_attn[0], 1, 1)
    unit, rate = normalise(r.stream[0])
    gain = bias(r, G1, B1)
    r.normed[...] = (unit * gain + bias(r, B1, BQ)).astype(BF)
    r.acc_vec[:, G1:B1] += fold(d_normed * unit)
    r.acc_vec[:, B1:BQ] += fold(d_normed)
    result[0] = d_mid[0] + norm_back(d_normed, unit, rate, gain)
    r.acc_attn[...] = jnp.where(r.first, 0.0, r.acc_attn[...]) + dot(r.normed[...], r.d_low[...], 0, 0)


def fill_small(small, acc_vec, row):
    total = jnp.sum(acc_vec[...], 0, keepdims=True)
    small[...] = jnp.broadcast_to(row, (128, 128))
    for owner in range(128):
        small[owner : owner + 1, 0:36] = total[:, 36 * owner : 36 * (owner + 1)]


def mlp_plan(r, keep, send_up, send_down, up_at, down_at):
    return [
        (r.acc_up, 3, 12, (keep, UP_AT), (send_up, up_at)),
        (r.acc_down, 12, 3, (keep, DOWN_AT), (send_down, down_at)),
    ]


def attention_plan(r, keep, send, shift):
    return [
        (r.acc_attn, 3, 9, (keep, QKV_AT - shift), (send, QKV_AT - shift)),
        (r.acc_out, 3, 3, (keep, PROJ_AT - shift), (send, PROJ_AT - shift)),
        (r.small, 1, 1, (keep, SMALL_AT - shift), (send, SMALL_AT - shift)),
    ]


def spaces(ins, outs, scratch, refs):
    return types.SimpleNamespace(**dict(zip([*ins, *outs, *scratch], refs)))


def call_kernel(kernel, ins, outs, scratch, limit, name):
    results = pl.pallas_call(
        lambda *refs: kernel(spaces(ins, outs, scratch, refs)),
        grid=(CHUNKS,),
        out_shape=[v[0] for v in outs.values()],
        in_specs=[v[1] for v in ins.values()],
        out_specs=[v[1] for v in outs.values()],
        scratch_shapes=list(scratch.values()),
        compiler_params=pltpu.CompilerParams(vmem_limit_bytes=limit * 2**20),
        name=name,
    )(*[v[0] for v in ins.values()])
    return types.SimpleNamespace(**dict(zip(outs, results)))


class Kept(typing.NamedTuple):
    p_img: typing.Any
    a_img: typing.Any
    mixed: typing.Any
    stream: typing.Any
    middle: typing.Any
    act: typing.Any
    slope: typing.Any


class Weights(typing.NamedTuple):
    w_attn: typing.Any
    w_out: typing.Any
    w_up: typing.Any
    w_down: typing.Any


KEPT_BLOCKS = Kept(
    ((IMG, 9, 64, 128), BF),
    ((IMG, 3, 64, 128), BF),
    ((1, RUN, D), BF),
    ((1, RUN, D), F32),
    ((1, RUN, D), F32),
    ((1, RUN, FF), BF),
    ((1, RUN, FF), BF),
)


def front_kernel(r):
    step = pl.program_id(0)
    first, final = step == 0, step == CHUNKS - 1
    kept = [Kept(*[getattr(r, n + s) for n in Kept._fields]) for s in ("_a", "_b")]
    weights = [Weights(*[getattr(r, n + s) for n in Weights._fields]) for s in ("_a", "_b")]
    kept_out = [getattr(r, n) for n in Kept._fields]
    weights_out = [getattr(r, n) for n in Weights._fields]
    masters = (r.m_attn, r.m_out, r.m_up, r.m_down)
    stages = (r.acc_attn, r.acc_out, r.acc_up, r.acc_down)

    def load(layer, k):
        return pltpu.make_async_copy(masters[k].at[layer], stages[k], r.load_sem.at[k])

    def save(k, chunk):
        size = kept[0][k].shape[0]
        target = kept_out[k].at[pl.ds(chunk * size, size)]
        return pltpu.make_async_copy(kept[0][k], target, r.save_sem.at[k])

    def save_weight(k):
        return pltpu.make_async_copy(weights[0][k], weights_out[k], r.weight_sem.at[k])

    def take(layer, k):
        load(layer, k).wait()
        weights[layer][k][0] = stages[k][...].astype(BF)

    def fetch(k):
        source, target = ((r.tokens, r.tokens_in), (r.grad_in, r.grad_low))[k]
        return pltpu.make_async_copy(source, target, r.fetch_sem.at[k])

    @pl.when(first)
    def _():
        fetch(0).start()
        for k in range(4):
            load(0, k).start()
        fetch(1).start()
        r.totals_a[...] = jnp.zeros_like(r.totals_a)
        r.totals_b[...] = jnp.zeros_like(r.totals_b)
        r.acc_vec[...] = jnp.zeros_like(r.acc_vec)
        for block in range(9):
            r.proj[block, RUN : RUN + 16, :] = jnp.zeros((16, 128), F32)
        for block in range(3):
            r.heads[block, REAL - 4 : RUN + 16, :] = jnp.zeros((RUN + 20 - REAL, 128), F32)
            r.d_heads[block, RUN : RUN + 16, :] = jnp.zeros((16, 128), F32)
        fetch(0).wait()

    @pl.when(step > 0)
    def _():
        for k in range(7):
            save(k, step - 1).wait()

    shared = dict(
        first=first,
        vec=r.vec,
        normed=r.normed,
        proj=r.proj,
        heads=r.heads,
        hidden=r.hidden,
    )
    zero = types.SimpleNamespace(
        **shared,
        **kept[0]._asdict(),
        **weights[0]._asdict(),
        layer=0,
        totals=r.totals_a,
        after=kept[1].stream,
    )
    one = types.SimpleNamespace(
        **shared,
        **kept[1]._asdict(),
        **weights[1]._asdict(),
        layer=1,
        totals=r.totals_b,
        after=r.d_mid,
        d_heads=r.d_heads,
        d_hidden=r.d_hidden,
        d_low=r.d_low,
        d_mid=r.d_mid,
        d_branch=r.d_branch,
        low_grad=r.low_grad,
        acc_vec=r.acc_vec,
        acc_attn=r.acc_attn,
        acc_out=r.acc_out,
        acc_up=r.acc_up,
        acc_down=r.acc_down,
        small=r.small,
    )
    unpack(r.tokens_in, step * IMG, zero.stream)
    ahead_norm(zero)

    @pl.when(first)
    def _():
        take(0, 0)

    ahead_attention(zero)
    for k in range(4):
        save(k, step).start()

    @pl.when(first)
    def _():
        for k in range(1, 4):
            take(0, k)
        for k in range(4):
            load(1, k).start()
            save_weight(k).start()

    ahead_mlp(zero)
    for k in range(4, 7):
        save(k, step).start()
    ahead_norm(one)

    @pl.when(first)
    def _():
        for k in range(4):
            take(1, k)
        fetch(1).wait()

    ahead_attention(one)
    ahead_mlp(one)
    for image in range(IMG):
        r.block_out[image] = one.after[0, SEQ * image : SEQ * (image + 1), :].astype(BF)
    unpack(r.grad_low, step * IMG, r.grad)
    back_mlp(one, r.grad)
    back_attention(one, one.d_mid, r.grad_out)

    @pl.when(final)
    def _():
        r.sums[...] = total_row(r.totals_a)
        fill_small(r.small, r.acc_vec, total_row(r.totals_b))
        plan = mlp_plan(r, r.keep, r.send, r.send, UP_AT, DOWN_AT)
        emit_packed(r.core[0], plan + attention_plan(r, r.keep, r.send, 0))
        for k in range(7):
            save(k, step).wait()
        for k in range(4):
            save_weight(k).wait()


def front(core, tokens, grad_out, masters, vector):
    smem = pl.BlockSpec(memory_space=pltpu.SMEM)
    ins = dict(
        core=(core, smem),
        tokens=(tokens, ANYWHERE),
        grad_in=(grad_out, ANYWHERE),
        vec=(vector, whole(2, 12 * D)),
        m_attn=(masters[0], ANYWHERE),
        m_out=(masters[1], ANYWHERE),
        m_up=(masters[2], ANYWHERE),
        m_down=(masters[3], ANYWHERE),
    )
    half = shape(F32, 4, 4, 4, ROWS, 128)
    outs = {
        n: (shape(kind, CHUNKS * dims[0], *dims[1:]), ANYWHERE)
        for n, (dims, kind) in KEPT_BLOCKS._asdict().items()
    }
    outs.update({n: (shape(BF, 1, *s), ANYWHERE) for n, s in zip(Weights._fields, WEIGHT_SIZES)})
    outs.update(
        sums=(shape(F32, 1, 128), whole(1, 128)),
        block_out=(shape(BF, IMG * CHUNKS, SEQ, D), imaged(SEQ, D)),
        grad_out=(shape(F32, CHUNKS, RUN, D), chunked(RUN, D)),
        keep=(half, VMEM_WHOLE),
        send=(half, VMEM_WHOLE),
    )
    scratch = {}
    for suffix in ("_a", "_b"):
        for n, (dims, kind) in KEPT_BLOCKS._asdict().items():
            scratch[n + suffix] = pltpu.VMEM(dims, kind)
        for n, size in zip(Weights._fields, WEIGHT_SIZES):
            scratch[n + suffix] = pltpu.VMEM((1,) + size, BF)
    scratch.update(
        totals_a=pltpu.VMEM((24, D), F32),
        totals_b=pltpu.VMEM((24, D), F32),
        heads=pltpu.VMEM((3, RUN + 16, 128), F32),
        **mlp_scratch(),
        **attention_scratch(),
        d_mid=pltpu.VMEM((1, RUN, D), F32),
        grad=pltpu.VMEM((1, RUN, D), F32),
        normed=pltpu.VMEM((RUN, D), BF),
        acc_vec=pltpu.VMEM((8, 12 * D), F32),
        tokens_in=pltpu.VMEM((IMG * CHUNKS, SEQ, D), BF),
        grad_low=pltpu.VMEM((IMG * CHUNKS, SEQ, D), BF),
        fetch_sem=pltpu.SemaphoreType.DMA((2,)),
        load_sem=pltpu.SemaphoreType.DMA((4,)),
        save_sem=pltpu.SemaphoreType.DMA((7,)),
        weight_sem=pltpu.SemaphoreType.DMA((4,)),
    )
    return call_kernel(front_kernel, ins, outs, scratch, FRONT_LIMIT, "front")


FRONT_LIMIT = 52


def mlp_scratch():
    return dict(
        low_grad=pltpu.VMEM((RUN, D), BF),
        hidden=pltpu.VMEM((RUN, FF), F32),
        d_hidden=pltpu.VMEM((RUN, FF), BF),
        acc_up=pltpu.VMEM((D, FF), F32),
        acc_down=pltpu.VMEM((FF, D), F32),
    )


def attention_scratch():
    return dict(
        d_branch=pltpu.VMEM((RUN, D), BF),
        d_heads=pltpu.VMEM((3, RUN + 16, 128), F32),
        proj=pltpu.VMEM((9, RUN + 16, 128), F32),
        d_low=pltpu.VMEM((RUN, 3 * D), BF),
        acc_attn=pltpu.VMEM((D, 3 * D), F32),
        acc_out=pltpu.VMEM((D, D), F32),
        small=pltpu.VMEM((128, 128), F32),
    )


def back_kernel(r):
    step = pl.program_id(0)
    r.layer = 0
    r.first = step == 0

    @pl.when(r.first)
    def _():
        r.acc_vec[...] = jnp.zeros_like(r.acc_vec)
        for block in range(3):
            r.d_heads[block, RUN : RUN + 16, :] = jnp.zeros((16, 128), F32)

    back_mlp(r, r.grad_in)
    back_attention(r, r.d_mid, r.grad)
    for image in range(IMG):
        r.grad_out[image] = r.grad[0, SEQ * image : SEQ * (image + 1), :]

    @pl.when(step == CHUNKS - 1)
    def _():
        fill_small(r.small, r.acc_vec, r.sums[...])
        plan = mlp_plan(r, r.keep, r.send, r.send, UP_AT, DOWN_AT)
        emit_packed(r.core[0], plan + attention_plan(r, r.keep, r.send, 0))


def back_call(core, grad, vector, ahead):
    half = shape(F32, 4, 4, 4, ROWS, 128)
    ins = dict(
        core=(core, pl.BlockSpec(memory_space=pltpu.SMEM)),
        grad_in=(grad, chunked(RUN, D)),
        vec=(vector, whole(2, 12 * D)),
        sums=(ahead.sums, whole(1, 128)),
    )
    for n, size in zip(Weights._fields, WEIGHT_SIZES):
        ins[n] = (getattr(ahead, n), held(1, *size))
    for n, (dims, _) in KEPT_BLOCKS._asdict().items():
        ins[n] = (getattr(ahead, n), imaged(*dims[1:]) if dims[0] == IMG else chunked(*dims[1:]))
    outs = dict(
        grad_out=(shape(F32, IMG * CHUNKS, SEQ, D), imaged(SEQ, D)),
        keep=(half, VMEM_WHOLE),
        send=(half, VMEM_WHOLE),
    )
    scratch = dict(
        **mlp_scratch(),
        **attention_scratch(),
        d_mid=pltpu.VMEM((1, RUN, D), F32),
        grad=pltpu.VMEM((1, RUN, D), F32),
        normed=pltpu.VMEM((RUN, D), BF),
        acc_vec=pltpu.VMEM((8, 12 * D), F32),
    )
    return call_kernel(back_kernel, ins, outs, scratch, BACK_LIMIT, "back")


BACK_LIMIT = 50


def local_step(core, tokens, grad_out, masters, vector):
    ahead = front(core, tokens, grad_out, masters, vector)
    parts = add_core(ahead.keep, swap_core(ahead.send))
    grad, parts = lax.optimization_barrier((ahead.grad_out, parts))
    parts_one = ring(0, parts)
    back = back_call(core, grad, vector, ahead)
    send, parts_one = lax.optimization_barrier((back.send, parts_one))
    parts_zero = ring(0, add_core(back.keep, swap_core(send)))
    return ahead.block_out, back.grad_out, parts_zero + parts_one


def stage_position(stage):
    deep, high, core, across = place_of(lax.axis_index(GROUP_AXES))
    if stage == 2:
        return deep
    return jnp.where(core == stage, across, high)


def add_core_kernel(keep, got, *outs):
    me = stage_position(0)
    for shift in range(4):
        at = me ^ shift

        @pl.loop(0, 16)
        def _(i):
            outs[shift][i // 4, i % 4] = keep[at, i // 4, i % 4] + got[at, i // 4, i % 4]


def add_first_kernel(*refs):
    sources = [refs[4 * k : 4 * k + 4] for k in range(2)]
    outs = refs[-4:]
    me = stage_position(1)
    for shift in range(4):
        at = me ^ shift

        @pl.loop(0, 4)
        def _(i):
            for layer, (own, one, two, three) in enumerate(sources):
                outs[shift][i, layer] = (own[at, i] + one[at, i]) + (two[at, i] + three[at, i])


def add_second_kernel(own, one, two, three, *outs):
    me = stage_position(2)
    for shift in range(4):
        at = me ^ shift
        outs[shift][...] = (own[at] + one[at]) + (two[at] + three[at])


def add_third_kernel(own, one, two, three, out):
    out[...] = (own[...] + one[...]) + (two[...] + three[...])


def call_add(kernel, values, out_dims, count, name):
    return pl.pallas_call(
        kernel,
        out_shape=[shape(F32, *out_dims, 128)] * count,
        in_specs=[VMEM_WHOLE] * len(values),
        out_specs=[VMEM_WHOLE] * count,
        compiler_params=pltpu.CompilerParams(vmem_limit_bytes=32 * 2**20),
        name=name,
    )(*values)


def ring(stage, parts):
    got = [lax.ppermute(parts[s], GROUP_AXES, ring_pairs(stage, s)) for s in range(1, 4)]
    return [parts[0]] + got


def swap_core(send):
    return lax.ppermute(send, GROUP_AXES, core_pairs())


def add_core(keep, got):
    return call_add(add_core_kernel, [keep, got], (4, 4, ROWS), 4, "add_core")


def finish_sums(parts):
    parts = call_add(add_first_kernel, parts, (4, 2, ROWS), 4, "add_first")
    parts = call_add(add_second_kernel, ring(1, parts), (2, ROWS), 4, "add_second")
    own = call_add(add_third_kernel, ring(2, parts), (2, ROWS), 1, "add_third")[0]
    return own, lax.ppermute(own, "grp", [(0, 1), (1, 0)])


def adam_step(gradient, moment_one, moment_two, weight, rate):
    moment_one = beta_one * moment_one + (1 - beta_one) * gradient
    moment_two = beta_two * moment_two + (1 - beta_two) * gradient * gradient
    fix_one = 1 - beta_one**STEP
    fix_two = 1 - beta_two**STEP
    update = (
        moment_one / fix_one / (jnp.sqrt(moment_two / fix_two) + adam_eps) + decay_rate * weight
    )
    return (moment_one, moment_two, weight - rate * update)


def finish_kernel(*refs):
    own, other = ([ref.at[k] for k in range(2)] for ref in refs[:2])
    weights, firsts, seconds, outers = (refs[2 + 5 * k : 7 + 5 * k] for k in range(4))
    outs = refs[22:]
    new_firsts, new_seconds, changes, new_outers, finals, copies = (
        outs[5 * k : 5 * k + 5] for k in range(6)
    )
    rms = outs[30]

    def gathered(refs, kind, row):
        if kind == 4:
            return jnp.concatenate([ref[SMALL_AT : SMALL_AT + 1, 0:36] for ref in refs], 0)
        start, rows, width = (
            (QKV_AT, 3, 9),
            (PROJ_AT, 3, 3),
            (UP_AT, 3, 12),
            (DOWN_AT, 12, 3),
        )[kind]
        lines = [start + rows * c + row for c in range(width)]
        return jnp.concatenate(
            [
                jnp.concatenate([ref[line : line + 1, :] for ref in refs], 0)
                for line in lines
            ],
            1,
        )

    for kind in range(5):
        rate = rates()[kind]
        for row in range(1 if kind == 4 else weights[kind].shape[0]):
            at = slice(None) if kind == 4 else row
            weight = weights[kind][at]
            moments = (firsts[kind][at], seconds[kind][at])
            one, two, updated = adam_step(gathered(own, kind, row), *moments, weight, rate)
            updated_other = adam_step(gathered(other, kind, row), *moments, weight, rate)[2]
            change = ((weight - updated) + (weight - updated_other)) / 2
            outer = outer_decay * outers[kind][at] + change
            final = weight - outer_rate * (change + outer_decay * outer)
            new_firsts[kind][at] = one
            new_seconds[kind][at] = two
            changes[kind][at] = change
            new_outers[kind][at] = outer
            finals[kind][at] = final
            copies[kind][at] = final.astype(jnp.bfloat16)
    for layer in range(2):
        totals = [
            ref[SMALL_AT : SMALL_AT + 1, SUMS_AT : SUMS_AT + 3] for ref in (own[layer], other[layer])
        ]
        rms[layer : layer + 1, :] = jnp.sqrt((totals[0] + totals[1]) / ENTRIES)


def rows_first(value):
    return value if value.ndim == 2 else jnp.swapaxes(value, 0, 1)


def finish(own, other, weights, firsts, seconds, outers):
    given = [rows_first(v) for v in (*weights, *firsts, *seconds, *outers)]
    full = [jax.ShapeDtypeStruct(v.shape, jnp.float32) for v in given[:5]]
    low = [jax.ShapeDtypeStruct(v.shape, jnp.bfloat16) for v in given[:5]]
    results = pl.pallas_call(
        finish_kernel,
        out_shape=full * 5 + low + [jax.ShapeDtypeStruct((2, 3), jnp.float32)],
        in_specs=[VMEM_WHOLE] * 22,
        out_specs=[VMEM_WHOLE] * 31,
        name="finish",
    )(own, other, *given)
    results = [rows_first(v) for v in results[:30]] + [results[30]]
    return [v[None] for v in results[:10]] + results[10:]

def body(
    tokens,
    grad_out,
    weight_qkv,
    weight_proj,
    weight_up,
    weight_down,
    weight_vector,
    old_first_qkv,
    old_first_proj,
    old_first_up,
    old_first_down,
    old_first_vector,
    old_second_qkv,
    old_second_proj,
    old_second_up,
    old_second_down,
    old_second_vector,
    old_outer_qkv,
    old_outer_proj,
    old_outer_up,
    old_outer_down,
    old_outer_vector,
):
    masters = (weight_qkv, weight_proj, weight_up, weight_down, weight_vector)
    old_firsts = (old_first_qkv, old_first_proj, old_first_up, old_first_down, old_first_vector)
    old_seconds = (
        old_second_qkv,
        old_second_proj,
        old_second_up,
        old_second_down,
        old_second_vector,
    )
    old_outers = (old_outer_qkv, old_outer_proj, old_outer_up, old_outer_down, old_outer_vector)
    owner_index = lax.axis_index(GROUP_AXES)
    core = jnp.reshape(owner_index // 4 % 2, (1,)).astype(jnp.int32)
    block_out, grad_tokens, parts = local_step(
        core, tokens, grad_out, masters[:4], weight_vector
    )
    shares = []
    for kind_index in range(5):
        share_rows = old_firsts[kind_index].shape[1]
        shares.append(
            lax.dynamic_slice_in_dim(masters[kind_index], owner_index * share_rows, share_rows, 1)
        )
    own, other = finish_sums(parts)
    results = finish(own, other, shares, old_firsts, old_seconds, old_outers)
    return (block_out, grad_tokens, *results)


def solution(mesh):
    placed = (
        P(("grp", "wide", "narrow"), None, None),
        P(("grp", "wide", "narrow"), None, None),
        P(),
        P(),
        P(),
        P(),
        P(),
        P(None, ("wide", "narrow"), None),
        P(None, ("wide", "narrow"), None),
        P(None, ("wide", "narrow"), None),
        P(None, ("wide", "narrow"), None),
        P(None, ("wide", "narrow")),
        P(None, ("wide", "narrow"), None),
        P(None, ("wide", "narrow"), None),
        P(None, ("wide", "narrow"), None),
        P(None, ("wide", "narrow"), None),
        P(None, ("wide", "narrow")),
        P(None, ("wide", "narrow"), None),
        P(None, ("wide", "narrow"), None),
        P(None, ("wide", "narrow"), None),
        P(None, ("wide", "narrow"), None),
        P(None, ("wide", "narrow")),
    )
    return jax.shard_map(
        body,
        mesh=mesh,
        in_specs=placed,
        out_specs=(
            P(("grp", "wide", "narrow"), None, None),
            P(("grp", "wide", "narrow"), None, None),
            P("grp", None, ("wide", "narrow"), None),
            P("grp", None, ("wide", "narrow"), None),
            P("grp", None, ("wide", "narrow"), None),
            P("grp", None, ("wide", "narrow"), None),
            P("grp", None, ("wide", "narrow")),
            P("grp", None, ("wide", "narrow"), None),
            P("grp", None, ("wide", "narrow"), None),
            P("grp", None, ("wide", "narrow"), None),
            P("grp", None, ("wide", "narrow"), None),
            P("grp", None, ("wide", "narrow")),
            P(None, ("wide", "narrow"), None),
            P(None, ("wide", "narrow"), None),
            P(None, ("wide", "narrow"), None),
            P(None, ("wide", "narrow"), None),
            P(None, ("wide", "narrow")),
            P(None, ("wide", "narrow"), None),
            P(None, ("wide", "narrow"), None),
            P(None, ("wide", "narrow"), None),
            P(None, ("wide", "narrow"), None),
            P(None, ("wide", "narrow")),
            P(None, ("wide", "narrow"), None),
            P(None, ("wide", "narrow"), None),
            P(None, ("wide", "narrow"), None),
            P(None, ("wide", "narrow"), None),
            P(None, ("wide", "narrow")),
            P(None, ("wide", "narrow"), None),
            P(None, ("wide", "narrow"), None),
            P(None, ("wide", "narrow"), None),
            P(None, ("wide", "narrow"), None),
            P(None, ("wide", "narrow")),
            P(),
        ),
        check_vma=False,
    )
```

```python
import types
import typing

import jax
import jax.numpy as jnp
from jax import lax
from jax.experimental import pallas as pl
from jax.experimental.pallas import tpu as pltpu
from jax.sharding import PartitionSpec as P

D = 384
HEADS = 6
HEAD_DIM = 64
FF = 1536
SEQ = 50
STEP = 10


beta_one = 0.9
beta_two = 0.95
adam_eps = 1e-08
decay_rate = 0.1
outer_decay = 0.9
outer_rate = 0.7

ROWS = 112
UP_AT, DOWN_AT, QKV_AT, PROJ_AT, SMALL_AT = 0, 36, 72, 99, 108
SUMS_AT = 64
ENTRIES = 98304000
VMEM_WHOLE = pl.BlockSpec(memory_space=pltpu.VMEM)
ANYWHERE = pl.BlockSpec(memory_space=pl.ANY)
GROUP_AXES = ("wide", "narrow")
IMG = 10
CHUNKS = 2
RUN = 512
REAL = IMG * SEQ
TOGETHER = 5
TOGETHER_BACK = 5
G1, B1, BQ, BV, BO, G2, B2, BU, BD = 0, 384, 768, 1152, 1536, 1920, 2304, 2688, 4224
BF = jnp.bfloat16
F32 = jnp.float32
WEIGHT_SIZES = ((D, 3 * D), (D, D), (D, FF), (FF, D))


def rates():
    return (1.5 * D ** (-0.5), 1.5 * (D // 4) ** (-0.5), 1.5 * D ** (-0.5), 1.5 * FF ** (-0.5), 2.0)


def place_of(owner):
    return owner // 32, owner // 8 % 4, owner // 4 % 2, owner % 4


def owner_of(deep, high, core, across):
    return ((deep * 4 + high) * 2 + core) * 4 + across


def core_pairs():
    return [(o, o ^ 4) for o in range(128)]


def ring_pairs(stage, shift):
    pairs = []
    for o in range(128):
        deep, high, core, across = place_of(o)
        if stage == 2:
            deep = deep ^ shift
        elif core == stage:
            across = across ^ shift
        else:
            high = high ^ shift
        pairs.append((o, owner_of(deep, high, core, across)))
    return pairs


def dot(left, right, left_dim=1, right_dim=0):
    return lax.dot_general(
        left, right, (((left_dim,), (right_dim,)), ((), ())), preferred_element_type=F32
    )


def normalise(rows):
    center = rows - jnp.sum(rows, -1, keepdims=True) * (1 / D)
    rate = lax.rsqrt(jnp.sum(center * center, -1, keepdims=True) * (1 / D) + 1e-06)
    return center * rate, rate


def norm_back(grad, unit, rate, gain):
    scaled = grad * gain
    first = jnp.sum(scaled, -1, keepdims=True) * (1 / D)
    second = jnp.sum(scaled * unit, -1, keepdims=True) * (1 / D)
    return rate * (scaled - first - unit * second)


def gelu_parts(value):
    area = 0.5 + 0.5 * lax.erf(value * 0.7071067811865476)
    bell = jnp.exp(-0.5 * value * value)
    return value * area, area + value * bell * 0.3989422804014327


def fold(values):
    return jnp.sum(values.reshape(-1, 8, values.shape[-1]), 0)


def halves_of(rows, low, keep):
    zero = jnp.zeros_like(rows)
    top = jnp.where(keep & low, rows, zero)
    bottom = jnp.where(keep & ~low, rows, zero)
    return jnp.concatenate([top, bottom], 0).astype(BF)


def masks():
    low = lax.broadcasted_iota(jnp.int32, (64, 128), 1) < 64
    keep = lax.broadcasted_iota(jnp.int32, (64, 128), 0) < SEQ
    return low, keep


def bias(r, start, stop):
    return r.vec[r.layer : r.layer + 1, start:stop]


def unpack(images, base, target):
    target[0, REAL - 4 : RUN, :] = jnp.zeros((RUN + 4 - REAL, D), F32)
    for image in range(IMG):
        target[0, SEQ * image : SEQ * (image + 1), :] = images[base + image].astype(F32)


def ahead_norm(r):
    def norm_block(i, carry):
        rows = pl.ds(pl.multiple_of(i * 64, 64), 64)
        unit, _ = normalise(r.stream[0, rows, :])
        r.normed[rows, :] = (unit * bias(r, G1, B1) + bias(r, B1, BQ)).astype(BF)
        return carry

    lax.fori_loop(0, RUN // 64, norm_block, 0)


def ahead_attention(r):
    proj, heads = r.proj, r.heads
    for third in range(3):
        result = dot(r.normed[...], r.w_attn[0, :, D * third : D * (third + 1)])
        if third == 0:
            result = result + bias(r, BQ, BV)
        if third == 2:
            result = result + bias(r, BV, BO)
        for block in range(3):
            proj[3 * third + block, 0:RUN, :] = result[:, 128 * block : 128 * (block + 1)]

    low, keep = masks()
    keep_keys = keep[0:56]

    def attend(i, carry):
        items = [(i * TOGETHER + k, pair) for k in range(TOGETHER) for pair in range(3)]
        loaded = []
        for image, pair in items:
            at = pl.ds(image * SEQ, 64)
            query = proj[pair, at, :]
            key = jnp.where(keep, proj[3 + pair, at, :], 0.0).astype(BF)
            value = jnp.where(keep, proj[6 + pair, at, :], 0.0).astype(BF)
            r.p_img[image, pair] = jnp.where(keep, query, 0.0).astype(BF)
            r.p_img[image, 3 + pair] = key
            r.p_img[image, 6 + pair] = value
            loaded.append((key, halves_of(query * 0.125, low, keep), value))
        scores = [dot(key, spread, 1, 1)[0:56] for key, spread, _ in loaded]
        weights = []
        for (image, pair), score in zip(items, scores):
            score = jnp.where(keep_keys, score, -1e30)
            raised = jnp.exp(score - jnp.max(score, 0, keepdims=True))
            weight = raised * (1.0 / jnp.sum(raised, 0, keepdims=True))
            weight = jnp.concatenate([weight, jnp.zeros((8, 128), F32)], 0).astype(BF)
            r.a_img[image, pair] = weight
            weights.append(weight)
        results = [dot(weight, value, 0, 0) for weight, (_, _, value) in zip(weights, loaded)]
        for (image, pair), both in zip(items, results):
            one = jnp.where(low, both[0:64], both[64:128])
            heads[pair, pl.ds(image * SEQ, SEQ), :] = one[0:SEQ]
        return carry

    lax.fori_loop(0, IMG // TOGETHER, attend, 0)
    for block in range(3):
        r.mixed[0, :, 128 * block : 128 * (block + 1)] = heads[block, 0:RUN, :].astype(BF)


def ahead_mlp(r):
    totals = r.totals
    real = lax.broadcasted_iota(jnp.int32, (RUN, D), 0) < REAL
    before = r.stream[0]
    branch = dot(r.mixed[0], r.w_out[0]) + bias(r, BO, G2)
    between = before + branch
    r.middle[0] = between
    totals[0:8, :] += fold(jnp.where(real, before * before, 0.0))
    totals[8:16, :] += fold(jnp.where(real, branch * branch, 0.0))

    def norm_block(i, carry):
        rows = pl.ds(pl.multiple_of(i * 64, 64), 64)
        unit, _ = normalise(r.middle[0, rows, :])
        r.normed[rows, :] = (unit * bias(r, G2, B2) + bias(r, B2, BU)).astype(BF)
        return carry

    lax.fori_loop(0, RUN // 64, norm_block, 0)
    r.hidden[...] = dot(r.normed[...], r.w_up[0])
    for row in range(0, RUN, 32):
        for column in range(0, FF, 256):
            part = r.hidden[row : row + 32, column : column + 256]
            part = part + bias(r, BU + column, BU + column + 256)
            bent, tilt = gelu_parts(part)
            r.act[0, row : row + 32, column : column + 256] = bent.astype(BF)
            r.slope[0, row : row + 32, column : column + 256] = tilt.astype(BF)
    tail = dot(r.act[0], r.w_down[0]) + bias(r, BD, BD + D)
    totals[16:24, :] += fold(jnp.where(real, tail * tail, 0.0))
    r.after[0] = r.middle[0] + tail


def total_row(totals):
    lane = lax.broadcasted_iota(jnp.int32, (1, 128), 1)
    row = jnp.zeros((1, 128), F32)
    for k in range(3):
        row = jnp.where(lane == SUMS_AT + k, jnp.sum(totals[8 * k : 8 * k + 8, :]), row)
    return row


def chunked(*dims):
    return pl.BlockSpec((1,) + dims, lambda c: (c,) + (0,) * len(dims))


def imaged(*dims):
    return pl.BlockSpec((IMG,) + dims, lambda c: (c,) + (0,) * len(dims))


def whole(*dims):
    return pl.BlockSpec(dims, lambda c: (0,) * len(dims))


def held(*dims):
    return pl.BlockSpec(dims, lambda c: (0,) * len(dims), pipeline_mode=pl.Buffered(1))


def shape(kind, *dims):
    return jax.ShapeDtypeStruct(dims, kind)


def emit_packed(core, plan):
    def emit(own):
        @pl.loop(0, 16)
        def _(block):
            deep, high = block // 4, block % 4
            for source, each, width, *targets in plan:
                height = 8 * each
                base = pl.multiple_of(block * height, 8)
                for column in range(width):
                    rows = source[pl.ds(base, height), column * 128 : (column + 1) * 128]
                    for k in range(8):
                        target, start = targets[0 if k // 4 == own else 1]
                        at = start + each * column
                        first, second = (k, high) if k < 4 else (high, k - 4)
                        target.at[first, second, deep][at : at + each, :] = rows[
                            each * k : each * (k + 1)
                        ]

    for own in range(2):

        @pl.when(core == own)
        def _():
            emit(own)


HEADS_P, HEADS_A, MIXED, STREAM, MIDDLE, ACT, SLOPE, GRAD, ATTN, OUT, UP, DOWN = range(12)


def back_mlp(r, grad):
    r.ready(GRAD, DOWN)
    here = grad[0]
    r.acc_vec[:, BD : BD + D] += fold(here)
    r.low_grad[...] = here.astype(BF)
    r.hidden[...] = dot(r.low_grad[...], r.w_down[0], 1, 1)
    r.ready(SLOPE)
    for column in range(0, FF, 256):
        total = jnp.zeros((8, 256), F32)
        for row in range(0, RUN, 32):
            at = slice(row, row + 32)
            part = r.hidden[at, column : column + 256]
            part = part * r.slope[0, at, column : column + 256].astype(F32)
            r.d_hidden[at, column : column + 256] = part.astype(BF)
            total = total + fold(part)
        r.acc_vec[:, BU + column : BU + column + 256] += total
    r.ready(UP, MIDDLE)
    d_normed = dot(r.d_hidden[...], r.w_up[0], 1, 1)
    unit, rate = normalise(r.middle[0])
    gain = bias(r, G2, B2)
    r.normed[...] = (unit * gain + bias(r, B2, BU)).astype(BF)
    r.acc_vec[:, G2:B2] += fold(d_normed * unit)
    r.acc_vec[:, B2:BU] += fold(d_normed)
    r.d_mid[0] = grad[0] + norm_back(d_normed, unit, rate, gain)
    r.ready(ACT)
    r.acc_down[...] = jnp.where(r.first, 0.0, r.acc_down[...]) + dot(r.act[0], r.low_grad[...], 0, 0)
    r.acc_up[...] = jnp.where(r.first, 0.0, r.acc_up[...]) + dot(r.normed[...], r.d_hidden[...], 0, 0)


def back_attention(r, d_mid, result):
    between = d_mid[0]
    r.acc_vec[:, BO:G2] += fold(between)
    r.d_branch[...] = between.astype(BF)
    r.ready(OUT, MIXED)
    product = dot(r.d_branch[...], r.w_out[0], 1, 1)
    for block in range(3):
        r.d_heads[block, 0:RUN, :] = product[:, 128 * block : 128 * (block + 1)]
    r.acc_out[...] = jnp.where(r.first, 0.0, r.acc_out[...]) + dot(r.mixed[0], r.d_branch[...], 0, 0)
    low, keep = masks()
    p_img, a_img, d_heads, d_proj = r.p_img, r.a_img, r.d_heads, r.proj
    for block in range(9):
        d_proj[block, REAL - 4 : RUN + 16, :] = jnp.zeros((RUN + 20 - REAL, 128), F32)

    def attend(i, carry):
        items = [(i * TOGETHER_BACK + k, pair) for k in range(TOGETHER_BACK) for pair in range(3)]
        loaded = []
        for image, pair in items:
            rows = d_heads[pair, pl.ds(image * SEQ, 64), :]
            spread = halves_of(p_img[image, pair].astype(F32) * 0.125, low, keep)
            loaded.append((spread, halves_of(rows, low, keep)))
        d_weights = [
            dot(p_img[image, 6 + pair], d_spread, 1, 1)
            for (image, pair), (_, d_spread) in zip(items, loaded)
        ]
        d_values = [
            dot(a_img[image, pair], d_spread) for (image, pair), (_, d_spread) in zip(items, loaded)
        ]
        d_scores = []
        for (image, pair), d_weight in zip(items, d_weights):
            weight = a_img[image, pair].astype(F32)
            product = weight * d_weight
            d_scores.append((product - weight * jnp.sum(product, 0, keepdims=True)).astype(BF))
        d_keys = [dot(d_score, spread) for d_score, (spread, _) in zip(d_scores, loaded)]
        d_both = [
            dot(d_score, p_img[image, 3 + pair], 0, 0)
            for (image, pair), d_score in zip(items, d_scores)
        ]
        for (image, pair), d_key, both, d_value in zip(items, d_keys, d_both, d_values):
            d_query = jnp.where(low, both[0:64], both[64:128]) * 0.125
            at = pl.ds(image * SEQ, SEQ)
            d_proj[pair, at, :] = d_query[0:SEQ]
            d_proj[3 + pair, at, :] = d_key[0:SEQ]
            d_proj[6 + pair, at, :] = d_value[0:SEQ]
        return carry

    r.ready(HEADS_P, HEADS_A)
    lax.fori_loop(0, IMG // TOGETHER_BACK, attend, 0)
    for block in range(9):
        part = d_proj[block, 0:RUN, :]
        r.d_low[:, 128 * block : 128 * (block + 1)] = part.astype(BF)
        if block < 3:
            r.acc_vec[:, BQ + 128 * block : BQ + 128 * (block + 1)] += fold(part)
        if block >= 6:
            r.acc_vec[:, BV + 128 * (block - 6) : BV + 128 * (block - 5)] += fold(part)
    r.ready(ATTN, STREAM)
    d_normed = dot(r.d_low[...], r.w_attn[0], 1, 1)
    unit, rate = normalise(r.stream[0])
    gain = bias(r, G1, B1)
    r.normed[...] = (unit * gain + bias(r, B1, BQ)).astype(BF)
    r.acc_vec[:, G1:B1] += fold(d_normed * unit)
    r.acc_vec[:, B1:BQ] += fold(d_normed)
    result[0] = d_mid[0] + norm_back(d_normed, unit, rate, gain)
    r.acc_attn[...] = jnp.where(r.first, 0.0, r.acc_attn[...]) + dot(r.normed[...], r.d_low[...], 0, 0)


def fill_small(small, acc_vec, row):
    total = jnp.sum(acc_vec[...], 0, keepdims=True)
    small[...] = jnp.broadcast_to(row, (128, 128))
    for owner in range(128):
        small[owner : owner + 1, 0:36] = total[:, 36 * owner : 36 * (owner + 1)]


def mlp_plan(r, keep, send_up, send_down, up_at, down_at):
    return [
        (r.acc_up, 3, 12, (keep, UP_AT), (send_up, up_at)),
        (r.acc_down, 12, 3, (keep, DOWN_AT), (send_down, down_at)),
    ]


def attention_plan(r, keep, send, shift):
    return [
        (r.acc_attn, 3, 9, (keep, QKV_AT - shift), (send, QKV_AT - shift)),
        (r.acc_out, 3, 3, (keep, PROJ_AT - shift), (send, PROJ_AT - shift)),
        (r.small, 1, 1, (keep, SMALL_AT - shift), (send, SMALL_AT - shift)),
    ]


def spaces(ins, outs, scratch, refs):
    return types.SimpleNamespace(**dict(zip([*ins, *outs, *scratch], refs)))


def call_kernel(kernel, ins, outs, scratch, limit, name):
    results = pl.pallas_call(
        lambda *refs: kernel(spaces(ins, outs, scratch, refs)),
        grid=(CHUNKS,),
        out_shape=[v[0] for v in outs.values()],
        in_specs=[v[1] for v in ins.values()],
        out_specs=[v[1] for v in outs.values()],
        scratch_shapes=list(scratch.values()),
        compiler_params=pltpu.CompilerParams(vmem_limit_bytes=limit * 2**20),
        name=name,
    )(*[v[0] for v in ins.values()])
    return types.SimpleNamespace(**dict(zip(outs, results)))


class Kept(typing.NamedTuple):
    p_img: typing.Any
    a_img: typing.Any
    mixed: typing.Any
    stream: typing.Any
    middle: typing.Any
    act: typing.Any
    slope: typing.Any


class Weights(typing.NamedTuple):
    w_attn: typing.Any
    w_out: typing.Any
    w_up: typing.Any
    w_down: typing.Any


KEPT_BLOCKS = Kept(
    ((IMG, 9, 64, 128), BF),
    ((IMG, 3, 64, 128), BF),
    ((1, RUN, D), BF),
    ((1, RUN, D), F32),
    ((1, RUN, D), F32),
    ((1, RUN, FF), BF),
    ((1, RUN, FF), BF),
)


def front_kernel(r):
    step = pl.program_id(0)
    first, final = step == 0, step == CHUNKS - 1
    kept = [Kept(*[getattr(r, n + s) for n in Kept._fields]) for s in ("_a", "_b")]
    weights = [Weights(*[getattr(r, n + s) for n in Weights._fields]) for s in ("_a", "_b")]
    kept_out = [getattr(r, n) for n in Kept._fields]
    weights_out = [getattr(r, n) for n in Weights._fields]
    masters = (r.m_attn, r.m_out, r.m_up, r.m_down)
    stages = (r.acc_attn, r.acc_out, r.acc_up, r.acc_down)

    def load(layer, k):
        return pltpu.make_async_copy(masters[k].at[layer], stages[k], r.load_sem.at[k])

    def save(k, chunk):
        size = kept[0][k].shape[0]
        target = kept_out[k].at[pl.ds(chunk * size, size)]
        return pltpu.make_async_copy(kept[0][k], target, r.save_sem.at[k])

    def save_weight(k):
        return pltpu.make_async_copy(weights[0][k], weights_out[k], r.weight_sem.at[k])

    def take(layer, k):
        load(layer, k).wait()
        weights[layer][k][0] = stages[k][...].astype(BF)

    def fetch(k):
        source, target = ((r.tokens, r.tokens_in), (r.grad_in, r.grad_low))[k]
        return pltpu.make_async_copy(source, target, r.fetch_sem.at[k])

    @pl.when(first)
    def _():
        fetch(0).start()
        for k in range(4):
            load(0, k).start()
        fetch(1).start()
        r.totals_a[...] = jnp.zeros_like(r.totals_a)
        r.totals_b[...] = jnp.zeros_like(r.totals_b)
        r.acc_vec[...] = jnp.zeros_like(r.acc_vec)
        for block in range(9):
            r.proj[block, RUN : RUN + 16, :] = jnp.zeros((16, 128), F32)
        for block in range(3):
            r.heads[block, REAL - 4 : RUN + 16, :] = jnp.zeros((RUN + 20 - REAL, 128), F32)
            r.d_heads[block, RUN : RUN + 16, :] = jnp.zeros((16, 128), F32)
        fetch(0).wait()

    @pl.when(step > 0)
    def _():
        for k in range(7):
            save(k, step - 1).wait()

    shared = dict(
        first=first,
        ready=lambda *which: None,
        vec=r.vec,
        normed=r.normed,
        proj=r.proj,
        heads=r.heads,
        hidden=r.hidden,
    )
    zero = types.SimpleNamespace(
        **shared,
        **kept[0]._asdict(),
        **weights[0]._asdict(),
        layer=0,
        totals=r.totals_a,
        after=kept[1].stream,
    )
    one = types.SimpleNamespace(
        **shared,
        **kept[1]._asdict(),
        **weights[1]._asdict(),
        layer=1,
        totals=r.totals_b,
        after=r.d_mid,
        d_heads=r.d_heads,
        d_hidden=r.d_hidden,
        d_low=r.d_low,
        d_mid=r.d_mid,
        d_branch=r.d_branch,
        low_grad=r.low_grad,
        acc_vec=r.acc_vec,
        acc_attn=r.acc_attn,
        acc_out=r.acc_out,
        acc_up=r.acc_up,
        acc_down=r.acc_down,
        small=r.small,
    )
    unpack(r.tokens_in, step * IMG, zero.stream)
    ahead_norm(zero)

    @pl.when(first)
    def _():
        take(0, 0)

    ahead_attention(zero)
    for k in range(4):
        save(k, step).start()

    @pl.when(first)
    def _():
        for k in range(1, 4):
            take(0, k)
        for k in range(4):
            load(1, k).start()
            save_weight(k).start()

    ahead_mlp(zero)
    for k in range(4, 7):
        save(k, step).start()
    ahead_norm(one)

    @pl.when(first)
    def _():
        for k in range(4):
            take(1, k)
        fetch(1).wait()

    ahead_attention(one)
    ahead_mlp(one)
    for image in range(IMG):
        r.block_out[image] = one.after[0, SEQ * image : SEQ * (image + 1), :].astype(BF)
    unpack(r.grad_low, step * IMG, r.grad)
    back_mlp(one, r.grad)
    back_attention(one, one.d_mid, r.grad_out)

    @pl.when(final)
    def _():
        r.sums[...] = total_row(r.totals_a)
        fill_small(r.small, r.acc_vec, total_row(r.totals_b))
        plan = mlp_plan(r, r.keep, r.send, r.send, UP_AT, DOWN_AT)
        emit_packed(r.core[0], plan + attention_plan(r, r.keep, r.send, 0))
        for k in range(7):
            save(k, step).wait()
        for k in range(4):
            save_weight(k).wait()


def front(core, tokens, grad_out, masters, vector):
    smem = pl.BlockSpec(memory_space=pltpu.SMEM)
    ins = dict(
        core=(core, smem),
        tokens=(tokens, ANYWHERE),
        grad_in=(grad_out, ANYWHERE),
        vec=(vector, whole(2, 12 * D)),
        m_attn=(masters[0], ANYWHERE),
        m_out=(masters[1], ANYWHERE),
        m_up=(masters[2], ANYWHERE),
        m_down=(masters[3], ANYWHERE),
    )
    half = shape(F32, 4, 4, 4, ROWS, 128)
    outs = {
        n: (shape(kind, CHUNKS * dims[0], *dims[1:]), ANYWHERE)
        for n, (dims, kind) in KEPT_BLOCKS._asdict().items()
    }
    outs.update({n: (shape(BF, 1, *s), ANYWHERE) for n, s in zip(Weights._fields, WEIGHT_SIZES)})
    outs.update(
        sums=(shape(F32, 1, 128), whole(1, 128)),
        block_out=(shape(BF, IMG * CHUNKS, SEQ, D), imaged(SEQ, D)),
        grad_out=(shape(F32, CHUNKS, RUN, D), chunked(RUN, D)),
        keep=(half, VMEM_WHOLE),
        send=(half, VMEM_WHOLE),
    )
    scratch = {}
    for suffix in ("_a", "_b"):
        for n, (dims, kind) in KEPT_BLOCKS._asdict().items():
            scratch[n + suffix] = pltpu.VMEM(dims, kind)
        for n, size in zip(Weights._fields, WEIGHT_SIZES):
            scratch[n + suffix] = pltpu.VMEM((1,) + size, BF)
    scratch.update(
        totals_a=pltpu.VMEM((24, D), F32),
        totals_b=pltpu.VMEM((24, D), F32),
        heads=pltpu.VMEM((3, RUN + 16, 128), F32),
        **mlp_scratch(),
        **attention_scratch(),
        d_mid=pltpu.VMEM((1, RUN, D), F32),
        grad=pltpu.VMEM((1, RUN, D), F32),
        normed=pltpu.VMEM((RUN, D), BF),
        acc_vec=pltpu.VMEM((8, 12 * D), F32),
        tokens_in=pltpu.VMEM((IMG * CHUNKS, SEQ, D), BF),
        grad_low=pltpu.VMEM((IMG * CHUNKS, SEQ, D), BF),
        fetch_sem=pltpu.SemaphoreType.DMA((2,)),
        load_sem=pltpu.SemaphoreType.DMA((4,)),
        save_sem=pltpu.SemaphoreType.DMA((7,)),
        weight_sem=pltpu.SemaphoreType.DMA((4,)),
    )
    return call_kernel(front_kernel, ins, outs, scratch, FRONT_LIMIT, "front")


FRONT_LIMIT = 60


def mlp_scratch():
    return dict(
        low_grad=pltpu.VMEM((RUN, D), BF),
        hidden=pltpu.VMEM((RUN, FF), F32),
        d_hidden=pltpu.VMEM((RUN, FF), BF),
        acc_up=pltpu.VMEM((D, FF), F32),
        acc_down=pltpu.VMEM((FF, D), F32),
    )


def attention_scratch():
    return dict(
        d_branch=pltpu.VMEM((RUN, D), BF),
        d_heads=pltpu.VMEM((3, RUN + 16, 128), F32),
        proj=pltpu.VMEM((9, RUN + 16, 128), F32),
        d_low=pltpu.VMEM((RUN, 3 * D), BF),
        acc_attn=pltpu.VMEM((D, 3 * D), F32),
        acc_out=pltpu.VMEM((D, D), F32),
        small=pltpu.VMEM((128, 128), F32),
    )


def back_kernel(r):
    step = pl.program_id(0)
    first = step == 0
    kept_in = [getattr(r, n + "_in") for n in Kept._fields] + [r.grad_in]
    kept = [getattr(r, n) for n in Kept._fields] + [r.grad_all]
    weights_in = [getattr(r, n + "_in") for n in Weights._fields]
    weights = [getattr(r, n) for n in Weights._fields]

    def load(k, chunk):
        if k >= ATTN:
            return pltpu.make_async_copy(weights_in[k - ATTN], weights[k - ATTN], r.sem.at[k, 0])
        size = kept[k].shape[0] // CHUNKS
        at = pl.ds(chunk * size, size)
        return pltpu.make_async_copy(kept_in[k].at[at], kept[k].at[at], r.sem.at[k, chunk])

    @pl.when(first)
    def _():
        for chunk in range(CHUNKS):
            for k in (GRAD, DOWN, SLOPE, UP, MIDDLE, ACT, OUT, MIXED, HEADS_P, HEADS_A, ATTN, STREAM):
                if k < ATTN or chunk == 0:
                    load(k, chunk).start()
        r.acc_vec[...] = jnp.zeros_like(r.acc_vec)
        for block in range(3):
            r.d_heads[block, RUN : RUN + 16, :] = jnp.zeros((16, 128), F32)

    def ready(*which):
        for k in which:
            if k < ATTN:
                load(k, step).wait()
            else:

                @pl.when(first)
                def _():
                    load(k, 0).wait()

    views = {}
    for n, ref in zip(Kept._fields, kept):
        size = ref.shape[0] // CHUNKS
        views[n] = ref.at[pl.ds(step * size, size)]
    q = types.SimpleNamespace(**{**vars(r), **views}, layer=0, first=first, ready=ready)
    back_mlp(q, r.grad_all.at[pl.ds(step, 1)])
    back_attention(q, r.d_mid, r.grad)
    for image in range(IMG):
        r.grad_out[image] = r.grad[0, SEQ * image : SEQ * (image + 1), :]

    @pl.when(step == CHUNKS - 1)
    def _():
        fill_small(r.small, r.acc_vec, r.sums[...])
        plan = mlp_plan(r, r.keep, r.send, r.send, UP_AT, DOWN_AT)
        emit_packed(r.core[0], plan + attention_plan(r, r.keep, r.send, 0))


def back_call(core, grad, vector, ahead):
    half = shape(F32, 4, 4, 4, ROWS, 128)
    ins = dict(
        core=(core, pl.BlockSpec(memory_space=pltpu.SMEM)),
        grad_in=(grad, ANYWHERE),
        vec=(vector, whole(2, 12 * D)),
        sums=(ahead.sums, whole(1, 128)),
    )
    scratch = {}
    for n, size in zip(Weights._fields, WEIGHT_SIZES):
        ins[n + "_in"] = (getattr(ahead, n), ANYWHERE)
        scratch[n] = pltpu.VMEM((1,) + size, BF)
    for n, (dims, kind) in KEPT_BLOCKS._asdict().items():
        ins[n + "_in"] = (getattr(ahead, n), ANYWHERE)
        scratch[n] = pltpu.VMEM((CHUNKS * dims[0],) + dims[1:], kind)
    outs = dict(
        grad_out=(shape(F32, IMG * CHUNKS, SEQ, D), imaged(SEQ, D)),
        keep=(half, VMEM_WHOLE),
        send=(half, VMEM_WHOLE),
    )
    scratch.update(
        **mlp_scratch(),
        **attention_scratch(),
        grad_all=pltpu.VMEM((CHUNKS, RUN, D), F32),
        d_mid=pltpu.VMEM((1, RUN, D), F32),
        grad=pltpu.VMEM((1, RUN, D), F32),
        normed=pltpu.VMEM((RUN, D), BF),
        acc_vec=pltpu.VMEM((8, 12 * D), F32),
        sem=pltpu.SemaphoreType.DMA((12, CHUNKS)),
    )
    return call_kernel(back_kernel, ins, outs, scratch, BACK_LIMIT, "back")


BACK_LIMIT = 58


def local_step(core, tokens, grad_out, masters, vector, shares):
    ahead = front(core, tokens, grad_out, masters, vector)
    got, shares = lax.optimization_barrier((swap_core(ahead.send), shares))
    parts = add_core(ahead.keep, got)
    grad, parts = lax.optimization_barrier((ahead.grad_out, parts))
    parts_one = ring(0, parts)
    back = back_call(core, grad, vector, ahead)
    send, parts_one = lax.optimization_barrier((back.send, parts_one))
    parts_zero = ring(0, add_core(back.keep, swap_core(send)))
    return ahead.block_out, back.grad_out, parts_zero + parts_one, shares


def stage_position(stage):
    deep, high, core, across = place_of(lax.axis_index(GROUP_AXES))
    if stage == 2:
        return deep
    return jnp.where(core == stage, across, high)


def add_core_kernel(keep, got, *refs):
    outs, (local, sem) = refs[:4], refs[4:]
    me = stage_position(0)

    def load(shift):
        return pltpu.make_async_copy(keep.at[me ^ shift], local.at[shift], sem.at[shift])

    for shift in range(4):
        load(shift).start()
    for shift in range(4):
        load(shift).wait()

        @pl.loop(0, 16)
        def _(i):
            outs[shift][i // 4, i % 4] = local[shift, i // 4, i % 4] + got[me ^ shift, i // 4, i % 4]


def add_first_kernel(*refs):
    sources = [refs[4 * k : 4 * k + 4] for k in range(2)]
    outs = refs[-4:]
    me = stage_position(1)
    for shift in range(4):
        at = me ^ shift

        @pl.loop(0, 4)
        def _(i):
            for layer, (own, one, two, three) in enumerate(sources):
                outs[shift][i, layer] = (own[at, i] + one[at, i]) + (two[at, i] + three[at, i])


def add_second_kernel(own, one, two, three, *outs):
    me = stage_position(2)
    for shift in range(4):
        at = me ^ shift
        outs[shift][...] = (own[at] + one[at]) + (two[at] + three[at])


def add_third_kernel(own, one, two, three, out):
    out[...] = (own[...] + one[...]) + (two[...] + three[...])


def call_add(kernel, values, out_dims, count, name):
    return pl.pallas_call(
        kernel,
        out_shape=[shape(F32, *out_dims, 128)] * count,
        in_specs=[VMEM_WHOLE] * len(values),
        out_specs=[VMEM_WHOLE] * count,
        compiler_params=pltpu.CompilerParams(vmem_limit_bytes=32 * 2**20),
        name=name,
    )(*values)


def ring(stage, parts):
    got = [lax.ppermute(parts[s], GROUP_AXES, ring_pairs(stage, s)) for s in (2, 1, 3)]
    return [parts[0]] + got


def swap_core(send):
    return lax.ppermute(send, GROUP_AXES, core_pairs())


def add_core(keep, got):
    return pl.pallas_call(
        add_core_kernel,
        out_shape=[shape(F32, 4, 4, ROWS, 128)] * 4,
        in_specs=[ANYWHERE, VMEM_WHOLE],
        out_specs=[VMEM_WHOLE] * 4,
        scratch_shapes=[
            pltpu.VMEM((4, 4, 4, ROWS, 128), F32),
            pltpu.SemaphoreType.DMA((4,)),
        ],
        compiler_params=pltpu.CompilerParams(vmem_limit_bytes=32 * 2**20),
        name="add_core",
    )(keep, got)


def finish_sums(parts):
    parts = call_add(add_first_kernel, parts, (4, 2, ROWS), 4, "add_first")
    parts = call_add(add_second_kernel, ring(1, parts), (2, ROWS), 4, "add_second")
    own = call_add(add_third_kernel, ring(2, parts), (2, ROWS), 1, "add_third")[0]
    return own, lax.ppermute(own, "grp", [(0, 1), (1, 0)])


def adam_step(gradient, moment_one, moment_two, weight, rate):
    moment_one = beta_one * moment_one + (1 - beta_one) * gradient
    moment_two = beta_two * moment_two + (1 - beta_two) * gradient * gradient
    fix_one = 1 - beta_one**STEP
    fix_two = 1 - beta_two**STEP
    update = (
        moment_one / fix_one / (jnp.sqrt(moment_two / fix_two) + adam_eps) + decay_rate * weight
    )
    return (moment_one, moment_two, weight - rate * update)


def finish_kernel(*refs):
    own, other = ([ref.at[k] for k in range(2)] for ref in refs[:2])
    weights, firsts, seconds, outers = (refs[2 + 5 * k : 7 + 5 * k] for k in range(4))
    outs = refs[22:]
    new_firsts, new_seconds, changes, new_outers, finals, copies = (
        outs[5 * k : 5 * k + 5] for k in range(6)
    )
    rms = outs[30]

    def gathered(refs, kind, row):
        if kind == 4:
            return jnp.concatenate([ref[SMALL_AT : SMALL_AT + 1, 0:36] for ref in refs], 0)
        start, rows, width = (
            (QKV_AT, 3, 9),
            (PROJ_AT, 3, 3),
            (UP_AT, 3, 12),
            (DOWN_AT, 12, 3),
        )[kind]
        lines = [start + rows * c + row for c in range(width)]
        return jnp.concatenate(
            [
                jnp.concatenate([ref[line : line + 1, :] for ref in refs], 0)
                for line in lines
            ],
            1,
        )

    for kind in range(5):
        rate = rates()[kind]
        for row in range(1 if kind == 4 else weights[kind].shape[0]):
            at = slice(None) if kind == 4 else row
            weight = weights[kind][at]
            moments = (firsts[kind][at], seconds[kind][at])
            one, two, updated = adam_step(gathered(own, kind, row), *moments, weight, rate)
            updated_other = adam_step(gathered(other, kind, row), *moments, weight, rate)[2]
            change = ((weight - updated) + (weight - updated_other)) / 2
            outer = outer_decay * outers[kind][at] + change
            final = weight - outer_rate * (change + outer_decay * outer)
            new_firsts[kind][at] = one
            new_seconds[kind][at] = two
            changes[kind][at] = change
            new_outers[kind][at] = outer
            finals[kind][at] = final
            copies[kind][at] = final.astype(jnp.bfloat16)
    for layer in range(2):
        totals = [
            ref[SMALL_AT : SMALL_AT + 1, SUMS_AT : SUMS_AT + 3] for ref in (own[layer], other[layer])
        ]
        rms[layer : layer + 1, :] = jnp.sqrt((totals[0] + totals[1]) / ENTRIES)


def rows_first(value):
    return value if value.ndim == 2 else jnp.swapaxes(value, 0, 1)


def finish(own, other, weights, firsts, seconds, outers):
    given = [*weights, *[rows_first(v) for v in (*firsts, *seconds, *outers)]]
    full = [jax.ShapeDtypeStruct(v.shape, jnp.float32) for v in given[:5]]
    low = [jax.ShapeDtypeStruct(v.shape, jnp.bfloat16) for v in given[:5]]
    results = pl.pallas_call(
        finish_kernel,
        out_shape=full * 5 + low + [jax.ShapeDtypeStruct((2, 3), jnp.float32)],
        in_specs=[VMEM_WHOLE] * 22,
        out_specs=[VMEM_WHOLE] * 31,
        name="finish",
    )(own, other, *given)
    results = [rows_first(v) for v in results[:30]] + [results[30]]
    return [v[None] for v in results[:10]] + results[10:]

def body(
    tokens,
    grad_out,
    weight_qkv,
    weight_proj,
    weight_up,
    weight_down,
    weight_vector,
    old_first_qkv,
    old_first_proj,
    old_first_up,
    old_first_down,
    old_first_vector,
    old_second_qkv,
    old_second_proj,
    old_second_up,
    old_second_down,
    old_second_vector,
    old_outer_qkv,
    old_outer_proj,
    old_outer_up,
    old_outer_down,
    old_outer_vector,
):
    masters = (weight_qkv, weight_proj, weight_up, weight_down, weight_vector)
    old_firsts = (old_first_qkv, old_first_proj, old_first_up, old_first_down, old_first_vector)
    old_seconds = (
        old_second_qkv,
        old_second_proj,
        old_second_up,
        old_second_down,
        old_second_vector,
    )
    old_outers = (old_outer_qkv, old_outer_proj, old_outer_up, old_outer_down, old_outer_vector)
    owner_index = lax.axis_index(GROUP_AXES)
    core = jnp.reshape(owner_index // 4 % 2, (1,)).astype(jnp.int32)
    shares = []
    for kind_index in range(5):
        share_rows = old_firsts[kind_index].shape[1]
        at = owner_index * share_rows
        share = lax.dynamic_slice_in_dim(masters[kind_index], at, share_rows, 1)
        shares.append(rows_first(share))
    block_out, grad_tokens, parts, shares = local_step(
        core, tokens, grad_out, masters[:4], weight_vector, shares
    )
    own, other = finish_sums(parts)
    results = finish(own, other, shares, old_firsts, old_seconds, old_outers)
    return (block_out, grad_tokens, *results)


def solution(mesh):
    placed = (
        P(("grp", "wide", "narrow"), None, None),
        P(("grp", "wide", "narrow"), None, None),
        P(),
        P(),
        P(),
        P(),
        P(),
        P(None, ("wide", "narrow"), None),
        P(None, ("wide", "narrow"), None),
        P(None, ("wide", "narrow"), None),
        P(None, ("wide", "narrow"), None),
        P(None, ("wide", "narrow")),
        P(None, ("wide", "narrow"), None),
        P(None, ("wide", "narrow"), None),
        P(None, ("wide", "narrow"), None),
        P(None, ("wide", "narrow"), None),
        P(None, ("wide", "narrow")),
        P(None, ("wide", "narrow"), None),
        P(None, ("wide", "narrow"), None),
        P(None, ("wide", "narrow"), None),
        P(None, ("wide", "narrow"), None),
        P(None, ("wide", "narrow")),
    )
    return jax.shard_map(
        body,
        mesh=mesh,
        in_specs=placed,
        out_specs=(
            P(("grp", "wide", "narrow"), None, None),
            P(("grp", "wide", "narrow"), None, None),
            P("grp", None, ("wide", "narrow"), None),
            P("grp", None, ("wide", "narrow"), None),
            P("grp", None, ("wide", "narrow"), None),
            P("grp", None, ("wide", "narrow"), None),
            P("grp", None, ("wide", "narrow")),
            P("grp", None, ("wide", "narrow"), None),
            P("grp", None, ("wide", "narrow"), None),
            P("grp", None, ("wide", "narrow"), None),
            P("grp", None, ("wide", "narrow"), None),
            P("grp", None, ("wide", "narrow")),
            P(None, ("wide", "narrow"), None),
            P(None, ("wide", "narrow"), None),
            P(None, ("wide", "narrow"), None),
            P(None, ("wide", "narrow"), None),
            P(None, ("wide", "narrow")),
            P(None, ("wide", "narrow"), None),
            P(None, ("wide", "narrow"), None),
            P(None, ("wide", "narrow"), None),
            P(None, ("wide", "narrow"), None),
            P(None, ("wide", "narrow")),
            P(None, ("wide", "narrow"), None),
            P(None, ("wide", "narrow"), None),
            P(None, ("wide", "narrow"), None),
            P(None, ("wide", "narrow"), None),
            P(None, ("wide", "narrow")),
            P(None, ("wide", "narrow"), None),
            P(None, ("wide", "narrow"), None),
            P(None, ("wide", "narrow"), None),
            P(None, ("wide", "narrow"), None),
            P(None, ("wide", "narrow")),
            P(),
        ),
        check_vma=False,
    )
```

```python
import types
import typing

import jax
import jax.numpy as jnp
from jax import lax
from jax.experimental import pallas as pl
from jax.experimental.pallas import tpu as pltpu
from jax.sharding import PartitionSpec as P

D = 384
HEADS = 6
HEAD_DIM = 64
FF = 1536
SEQ = 50
STEP = 10


beta_one = 0.9
beta_two = 0.95
adam_eps = 1e-08
decay_rate = 0.1
outer_decay = 0.9
outer_rate = 0.7

ROWS = 112
UP_AT, DOWN_AT, QKV_AT, PROJ_AT, SMALL_AT = 0, 36, 72, 99, 108
SUMS_AT = 64
ENTRIES = 98304000
VMEM_WHOLE = pl.BlockSpec(memory_space=pltpu.VMEM)
ANYWHERE = pl.BlockSpec(memory_space=pl.ANY)
GROUP_AXES = ("wide", "narrow")
IMG = 10
CHUNKS = 2
RUN = 512
REAL = IMG * SEQ
TOGETHER = 5
TOGETHER_BACK = 5
G1, B1, BQ, BV, BO, G2, B2, BU, BD = 0, 384, 768, 1152, 1536, 1920, 2304, 2688, 4224
BF = jnp.bfloat16
F32 = jnp.float32
WEIGHT_SIZES = ((D, 3 * D), (D, D), (D, FF), (FF, D))


def rates():
    return (1.5 * D ** (-0.5), 1.5 * (D // 4) ** (-0.5), 1.5 * D ** (-0.5), 1.5 * FF ** (-0.5), 2.0)


def place_of(owner):
    return owner // 32, owner // 8 % 4, owner // 4 % 2, owner % 4


def owner_of(deep, high, core, across):
    return ((deep * 4 + high) * 2 + core) * 4 + across


def core_pairs():
    return [(o, o ^ 4) for o in range(128)]


def ring_pairs(stage, shift):
    pairs = []
    for o in range(128):
        deep, high, core, across = place_of(o)
        if stage == 2:
            deep = deep ^ shift
        elif core == stage:
            across = across ^ shift
        else:
            high = high ^ shift
        pairs.append((o, owner_of(deep, high, core, across)))
    return pairs


def dot(left, right, left_dim=1, right_dim=0):
    return lax.dot_general(
        left, right, (((left_dim,), (right_dim,)), ((), ())), preferred_element_type=F32
    )


def normalise(rows):
    center = rows - jnp.sum(rows, -1, keepdims=True) * (1 / D)
    rate = lax.rsqrt(jnp.sum(center * center, -1, keepdims=True) * (1 / D) + 1e-06)
    return center * rate, rate


def norm_back(grad, unit, rate, gain):
    scaled = grad * gain
    first = jnp.sum(scaled, -1, keepdims=True) * (1 / D)
    second = jnp.sum(scaled * unit, -1, keepdims=True) * (1 / D)
    return rate * (scaled - first - unit * second)


def gelu_parts(value):
    area = 0.5 + 0.5 * lax.erf(value * 0.7071067811865476)
    bell = jnp.exp(-0.5 * value * value)
    return value * area, area + value * bell * 0.3989422804014327


def fold(values):
    return jnp.sum(values.reshape(-1, 8, values.shape[-1]), 0)


def halves_of(rows, low, keep):
    zero = jnp.zeros_like(rows)
    top = jnp.where(keep & low, rows, zero)
    bottom = jnp.where(keep & ~low, rows, zero)
    return jnp.concatenate([top, bottom], 0).astype(BF)


def masks():
    low = lax.broadcasted_iota(jnp.int32, (64, 128), 1) < 64
    keep = lax.broadcasted_iota(jnp.int32, (64, 128), 0) < SEQ
    return low, keep


def bias(r, start, stop):
    return r.vec[r.layer : r.layer + 1, start:stop]


def unpack(images, base, target):
    target[0, REAL - 4 : RUN, :] = jnp.zeros((RUN + 4 - REAL, D), F32)
    for image in range(IMG):
        target[0, SEQ * image : SEQ * (image + 1), :] = images[base + image].astype(F32)


def ahead_norm(r):
    def norm_block(i, carry):
        rows = pl.ds(pl.multiple_of(i * 64, 64), 64)
        unit, _ = normalise(r.stream[0, rows, :])
        r.normed[rows, :] = (unit * bias(r, G1, B1) + bias(r, B1, BQ)).astype(BF)
        return carry

    lax.fori_loop(0, RUN // 64, norm_block, 0)


def ahead_attention(r):
    proj, heads = r.proj, r.heads
    for third in range(3):
        result = dot(r.normed[...], r.w_attn[0, :, D * third : D * (third + 1)])
        if third == 0:
            result = result + bias(r, BQ, BV)
        if third == 2:
            result = result + bias(r, BV, BO)
        for block in range(3):
            proj[3 * third + block, 0:RUN, :] = result[:, 128 * block : 128 * (block + 1)]

    low, keep = masks()
    keep_keys = keep[0:56]

    def attend(i, carry):
        items = [(i * TOGETHER + k, pair) for k in range(TOGETHER) for pair in range(3)]
        loaded = []
        for image, pair in items:
            at = pl.ds(image * SEQ, 64)
            query = proj[pair, at, :]
            key = jnp.where(keep, proj[3 + pair, at, :], 0.0).astype(BF)
            value = jnp.where(keep, proj[6 + pair, at, :], 0.0).astype(BF)
            r.p_img[image, pair] = jnp.where(keep, query, 0.0).astype(BF)
            r.p_img[image, 3 + pair] = key
            r.p_img[image, 6 + pair] = value
            loaded.append((key, halves_of(query * 0.125, low, keep), value))
        scores = [dot(key, spread, 1, 1)[0:56] for key, spread, _ in loaded]
        weights = []
        for (image, pair), score in zip(items, scores):
            score = jnp.where(keep_keys, score, -1e30)
            raised = jnp.exp(score - jnp.max(score, 0, keepdims=True))
            weight = raised * (1.0 / jnp.sum(raised, 0, keepdims=True))
            weight = jnp.concatenate([weight, jnp.zeros((8, 128), F32)], 0).astype(BF)
            r.a_img[image, pair] = weight
            weights.append(weight)
        results = [dot(weight, value, 0, 0) for weight, (_, _, value) in zip(weights, loaded)]
        for (image, pair), both in zip(items, results):
            one = jnp.where(low, both[0:64], both[64:128])
            heads[pair, pl.ds(image * SEQ, SEQ), :] = one[0:SEQ]
        return carry

    lax.fori_loop(0, IMG // TOGETHER, attend, 0)
    for block in range(3):
        r.mixed[0, :, 128 * block : 128 * (block + 1)] = heads[block, 0:RUN, :].astype(BF)


def ahead_mlp(r):
    totals = r.totals
    real = lax.broadcasted_iota(jnp.int32, (RUN, D), 0) < REAL
    before = r.stream[0]
    branch = dot(r.mixed[0], r.w_out[0]) + bias(r, BO, G2)
    between = before + branch
    r.middle[0] = between
    totals[0:8, :] += fold(jnp.where(real, before * before, 0.0))
    totals[8:16, :] += fold(jnp.where(real, branch * branch, 0.0))

    def norm_block(i, carry):
        rows = pl.ds(pl.multiple_of(i * 64, 64), 64)
        unit, _ = normalise(r.middle[0, rows, :])
        r.normed[rows, :] = (unit * bias(r, G2, B2) + bias(r, B2, BU)).astype(BF)
        return carry

    lax.fori_loop(0, RUN // 64, norm_block, 0)
    r.hidden[...] = dot(r.normed[...], r.w_up[0])
    for row in range(0, RUN, 32):
        for column in range(0, FF, 256):
            part = r.hidden[row : row + 32, column : column + 256]
            part = part + bias(r, BU + column, BU + column + 256)
            bent, tilt = gelu_parts(part)
            r.act[0, row : row + 32, column : column + 256] = bent.astype(BF)
            r.slope[0, row : row + 32, column : column + 256] = tilt.astype(BF)
    tail = dot(r.act[0], r.w_down[0]) + bias(r, BD, BD + D)
    totals[16:24, :] += fold(jnp.where(real, tail * tail, 0.0))
    r.after[0] = r.middle[0] + tail


def total_row(totals):
    lane = lax.broadcasted_iota(jnp.int32, (1, 128), 1)
    row = jnp.zeros((1, 128), F32)
    for k in range(3):
        row = jnp.where(lane == SUMS_AT + k, jnp.sum(totals[8 * k : 8 * k + 8, :]), row)
    return row


def chunked(*dims):
    return pl.BlockSpec((1,) + dims, lambda c: (c,) + (0,) * len(dims))


def imaged(*dims):
    return pl.BlockSpec((IMG,) + dims, lambda c: (c,) + (0,) * len(dims))


def whole(*dims):
    return pl.BlockSpec(dims, lambda c: (0,) * len(dims))


def held(*dims):
    return pl.BlockSpec(dims, lambda c: (0,) * len(dims), pipeline_mode=pl.Buffered(1))


def shape(kind, *dims):
    return jax.ShapeDtypeStruct(dims, kind)


def emit_packed(core, plan):
    def emit(own):
        @pl.loop(0, 16)
        def _(block):
            deep, high = block // 4, block % 4
            for source, each, width, *targets in plan:
                height = 8 * each
                base = pl.multiple_of(block * height, 8)
                for column in range(width):
                    rows = source[pl.ds(base, height), column * 128 : (column + 1) * 128]
                    for k in range(8):
                        target, start = targets[0 if k // 4 == own else 1]
                        at = start + each * column
                        first, second = (k, high) if k < 4 else (high, k - 4)
                        target.at[first, second, deep][at : at + each, :] = rows[
                            each * k : each * (k + 1)
                        ]

    for own in range(2):

        @pl.when(core == own)
        def _():
            emit(own)


HEADS_P, HEADS_A, MIXED, STREAM, MIDDLE, ACT, SLOPE, GRAD, ATTN, OUT, UP, DOWN = range(12)


def back_mlp(r, grad):
    r.ready(GRAD, DOWN)
    here = grad[0]
    r.acc_vec[:, BD : BD + D] += fold(here)
    r.low_grad[...] = here.astype(BF)
    r.hidden[...] = dot(r.low_grad[...], r.w_down[0], 1, 1)
    r.ready(SLOPE)
    for column in range(0, FF, 256):
        total = jnp.zeros((8, 256), F32)
        for row in range(0, RUN, 32):
            at = slice(row, row + 32)
            part = r.hidden[at, column : column + 256]
            part = part * r.slope[0, at, column : column + 256].astype(F32)
            r.d_hidden[at, column : column + 256] = part.astype(BF)
            total = total + fold(part)
        r.acc_vec[:, BU + column : BU + column + 256] += total
    r.ready(UP, MIDDLE)
    d_normed = dot(r.d_hidden[...], r.w_up[0], 1, 1)
    unit, rate = normalise(r.middle[0])
    gain = bias(r, G2, B2)
    r.normed[...] = (unit * gain + bias(r, B2, BU)).astype(BF)
    r.acc_vec[:, G2:B2] += fold(d_normed * unit)
    r.acc_vec[:, B2:BU] += fold(d_normed)
    r.d_mid[0] = grad[0] + norm_back(d_normed, unit, rate, gain)
    r.ready(ACT)
    r.acc_down[...] = jnp.where(r.first, 0.0, r.acc_down[...]) + dot(r.act[0], r.low_grad[...], 0, 0)
    r.acc_up[...] = jnp.where(r.first, 0.0, r.acc_up[...]) + dot(r.normed[...], r.d_hidden[...], 0, 0)


def back_attention(r, d_mid, result):
    between = d_mid[0]
    r.acc_vec[:, BO:G2] += fold(between)
    r.d_branch[...] = between.astype(BF)
    r.ready(OUT, MIXED)
    product = dot(r.d_branch[...], r.w_out[0], 1, 1)
    for block in range(3):
        r.d_heads[block, 0:RUN, :] = product[:, 128 * block : 128 * (block + 1)]
    r.acc_out[...] = jnp.where(r.first, 0.0, r.acc_out[...]) + dot(r.mixed[0], r.d_branch[...], 0, 0)
    low, keep = masks()
    p_img, a_img, d_heads, d_proj = r.p_img, r.a_img, r.d_heads, r.proj
    for block in range(9):
        d_proj[block, REAL - 4 : RUN + 16, :] = jnp.zeros((RUN + 20 - REAL, 128), F32)

    def attend(i, carry):
        items = [(i * TOGETHER_BACK + k, pair) for k in range(TOGETHER_BACK) for pair in range(3)]
        loaded = []
        for image, pair in items:
            rows = d_heads[pair, pl.ds(image * SEQ, 64), :]
            spread = halves_of(p_img[image, pair].astype(F32) * 0.125, low, keep)
            loaded.append((spread, halves_of(rows, low, keep)))
        d_weights = [
            dot(p_img[image, 6 + pair], d_spread, 1, 1)
            for (image, pair), (_, d_spread) in zip(items, loaded)
        ]
        d_values = [
            dot(a_img[image, pair], d_spread) for (image, pair), (_, d_spread) in zip(items, loaded)
        ]
        d_scores = []
        for (image, pair), d_weight in zip(items, d_weights):
            weight = a_img[image, pair].astype(F32)
            product = weight * d_weight
            d_scores.append((product - weight * jnp.sum(product, 0, keepdims=True)).astype(BF))
        d_keys = [dot(d_score, spread) for d_score, (spread, _) in zip(d_scores, loaded)]
        d_both = [
            dot(d_score, p_img[image, 3 + pair], 0, 0)
            for (image, pair), d_score in zip(items, d_scores)
        ]
        for (image, pair), d_key, both, d_value in zip(items, d_keys, d_both, d_values):
            d_query = jnp.where(low, both[0:64], both[64:128]) * 0.125
            at = pl.ds(image * SEQ, SEQ)
            d_proj[pair, at, :] = d_query[0:SEQ]
            d_proj[3 + pair, at, :] = d_key[0:SEQ]
            d_proj[6 + pair, at, :] = d_value[0:SEQ]
        return carry

    r.ready(HEADS_P, HEADS_A)
    lax.fori_loop(0, IMG // TOGETHER_BACK, attend, 0)
    for block in range(9):
        part = d_proj[block, 0:RUN, :]
        r.d_low[:, 128 * block : 128 * (block + 1)] = part.astype(BF)
        if block < 3:
            r.acc_vec[:, BQ + 128 * block : BQ + 128 * (block + 1)] += fold(part)
        if block >= 6:
            r.acc_vec[:, BV + 128 * (block - 6) : BV + 128 * (block - 5)] += fold(part)
    r.ready(ATTN, STREAM)
    d_normed = dot(r.d_low[...], r.w_attn[0], 1, 1)
    unit, rate = normalise(r.stream[0])
    gain = bias(r, G1, B1)
    r.normed[...] = (unit * gain + bias(r, B1, BQ)).astype(BF)
    r.acc_vec[:, G1:B1] += fold(d_normed * unit)
    r.acc_vec[:, B1:BQ] += fold(d_normed)
    result[0] = d_mid[0] + norm_back(d_normed, unit, rate, gain)
    r.acc_attn[...] = jnp.where(r.first, 0.0, r.acc_attn[...]) + dot(r.normed[...], r.d_low[...], 0, 0)


def fill_small(small, acc_vec, row):
    total = jnp.sum(acc_vec[...], 0, keepdims=True)
    small[...] = jnp.broadcast_to(row, (128, 128))
    for owner in range(128):
        small[owner : owner + 1, 0:36] = total[:, 36 * owner : 36 * (owner + 1)]


def mlp_plan(r, keep, send_up, send_down, up_at, down_at):
    return [
        (r.acc_up, 3, 12, (keep, UP_AT), (send_up, up_at)),
        (r.acc_down, 12, 3, (keep, DOWN_AT), (send_down, down_at)),
    ]


def attention_plan(r, keep, send, shift):
    return [
        (r.acc_attn, 3, 9, (keep, QKV_AT - shift), (send, QKV_AT - shift)),
        (r.acc_out, 3, 3, (keep, PROJ_AT - shift), (send, PROJ_AT - shift)),
        (r.small, 1, 1, (keep, SMALL_AT - shift), (send, SMALL_AT - shift)),
    ]


def spaces(ins, outs, scratch, refs):
    return types.SimpleNamespace(**dict(zip([*ins, *outs, *scratch], refs)))


def call_kernel(kernel, ins, outs, scratch, limit, name):
    results = pl.pallas_call(
        lambda *refs: kernel(spaces(ins, outs, scratch, refs)),
        grid=(CHUNKS,),
        out_shape=[v[0] for v in outs.values()],
        in_specs=[v[1] for v in ins.values()],
        out_specs=[v[1] for v in outs.values()],
        scratch_shapes=list(scratch.values()),
        compiler_params=pltpu.CompilerParams(vmem_limit_bytes=limit * 2**20),
        name=name,
    )(*[v[0] for v in ins.values()])
    return types.SimpleNamespace(**dict(zip(outs, results)))


class Kept(typing.NamedTuple):
    p_img: typing.Any
    a_img: typing.Any
    mixed: typing.Any
    stream: typing.Any
    middle: typing.Any
    act: typing.Any
    slope: typing.Any


class Weights(typing.NamedTuple):
    w_attn: typing.Any
    w_out: typing.Any
    w_up: typing.Any
    w_down: typing.Any


KEPT_BLOCKS = Kept(
    ((IMG, 9, 64, 128), BF),
    ((IMG, 3, 64, 128), BF),
    ((1, RUN, D), BF),
    ((1, RUN, D), F32),
    ((1, RUN, D), F32),
    ((1, RUN, FF), BF),
    ((1, RUN, FF), BF),
)


def front_kernel(r):
    step = pl.program_id(0)
    first, final = step == 0, step == CHUNKS - 1
    kept = [Kept(*[getattr(r, n + s) for n in Kept._fields]) for s in ("_a", "_b")]
    weights = [Weights(*[getattr(r, n + s) for n in Weights._fields]) for s in ("_a", "_b")]
    kept_out = [getattr(r, n) for n in Kept._fields]
    weights_out = [getattr(r, n) for n in Weights._fields]
    masters = (r.m_attn, r.m_out, r.m_up, r.m_down)
    stages = (r.acc_attn, r.acc_out, r.acc_up, r.acc_down)

    def load(layer, k):
        return pltpu.make_async_copy(masters[k].at[layer], stages[k], r.load_sem.at[k])

    def save(k, chunk):
        size = kept[0][k].shape[0]
        target = kept_out[k].at[pl.ds(chunk * size, size)]
        return pltpu.make_async_copy(kept[0][k], target, r.save_sem.at[k])

    def save_weight(k):
        return pltpu.make_async_copy(weights[0][k], weights_out[k], r.weight_sem.at[k])

    def take(layer, k):
        load(layer, k).wait()
        weights[layer][k][0] = stages[k][...].astype(BF)

    def fetch(k):
        source, target = ((r.tokens, r.tokens_in), (r.grad_in, r.grad_low))[k]
        return pltpu.make_async_copy(source, target, r.fetch_sem.at[k])

    @pl.when(first)
    def _():
        fetch(0).start()
        for k in range(4):
            load(0, k).start()
        fetch(1).start()
        r.totals_a[...] = jnp.zeros_like(r.totals_a)
        r.totals_b[...] = jnp.zeros_like(r.totals_b)
        r.acc_vec[...] = jnp.zeros_like(r.acc_vec)
        for block in range(9):
            r.proj[block, RUN : RUN + 16, :] = jnp.zeros((16, 128), F32)
        for block in range(3):
            r.heads[block, REAL - 4 : RUN + 16, :] = jnp.zeros((RUN + 20 - REAL, 128), F32)
            r.d_heads[block, RUN : RUN + 16, :] = jnp.zeros((16, 128), F32)
        fetch(0).wait()

    @pl.when(step > 0)
    def _():
        for k in range(7):
            save(k, step - 1).wait()

    shared = dict(
        first=first,
        ready=lambda *which: None,
        vec=r.vec,
        normed=r.normed,
        proj=r.proj,
        heads=r.heads,
        hidden=r.hidden,
    )
    zero = types.SimpleNamespace(
        **shared,
        **kept[0]._asdict(),
        **weights[0]._asdict(),
        layer=0,
        totals=r.totals_a,
        after=kept[1].stream,
    )
    one = types.SimpleNamespace(
        **shared,
        **kept[1]._asdict(),
        **weights[1]._asdict(),
        layer=1,
        totals=r.totals_b,
        after=r.d_mid,
        d_heads=r.d_heads,
        d_hidden=r.d_hidden,
        d_low=r.d_low,
        d_mid=r.d_mid,
        d_branch=r.d_branch,
        low_grad=r.low_grad,
        acc_vec=r.acc_vec,
        acc_attn=r.acc_attn,
        acc_out=r.acc_out,
        acc_up=r.acc_up,
        acc_down=r.acc_down,
        small=r.small,
    )
    unpack(r.tokens_in, step * IMG, zero.stream)
    ahead_norm(zero)

    @pl.when(first)
    def _():
        take(0, 0)

    ahead_attention(zero)
    for k in range(4):
        save(k, step).start()

    @pl.when(first)
    def _():
        for k in range(1, 4):
            take(0, k)
        for k in range(4):
            load(1, k).start()
            save_weight(k).start()

    ahead_mlp(zero)
    for k in range(4, 7):
        save(k, step).start()
    ahead_norm(one)

    @pl.when(first)
    def _():
        for k in range(4):
            take(1, k)
        fetch(1).wait()

    ahead_attention(one)
    ahead_mlp(one)
    for image in range(IMG):
        r.block_out[image] = one.after[0, SEQ * image : SEQ * (image + 1), :].astype(BF)
    unpack(r.grad_low, step * IMG, r.grad)
    back_mlp(one, r.grad)
    back_attention(one, one.d_mid, r.grad_out)

    @pl.when(final)
    def _():
        r.sums[...] = total_row(r.totals_a)
        fill_small(r.small, r.acc_vec, total_row(r.totals_b))
        plan = mlp_plan(r, r.keep, r.send, r.send, UP_AT, DOWN_AT)
        emit_packed(r.core[0], plan + attention_plan(r, r.keep, r.send, 0))
        for k in range(7):
            save(k, step).wait()
        for k in range(4):
            save_weight(k).wait()


def front(core, tokens, grad_out, masters, vector):
    smem = pl.BlockSpec(memory_space=pltpu.SMEM)
    ins = dict(
        core=(core, smem),
        tokens=(tokens, ANYWHERE),
        grad_in=(grad_out, ANYWHERE),
        vec=(vector, whole(2, 12 * D)),
        m_attn=(masters[0], ANYWHERE),
        m_out=(masters[1], ANYWHERE),
        m_up=(masters[2], ANYWHERE),
        m_down=(masters[3], ANYWHERE),
    )
    half = shape(F32, 4, 4, 4, ROWS, 128)
    outs = {
        n: (shape(kind, CHUNKS * dims[0], *dims[1:]), ANYWHERE)
        for n, (dims, kind) in KEPT_BLOCKS._asdict().items()
    }
    outs.update({n: (shape(BF, 1, *s), ANYWHERE) for n, s in zip(Weights._fields, WEIGHT_SIZES)})
    outs.update(
        sums=(shape(F32, 1, 128), whole(1, 128)),
        block_out=(shape(BF, IMG * CHUNKS, SEQ, D), imaged(SEQ, D)),
        grad_out=(shape(F32, CHUNKS, RUN, D), chunked(RUN, D)),
        keep=(half, VMEM_WHOLE),
        send=(half, VMEM_WHOLE),
    )
    scratch = {}
    for suffix in ("_a", "_b"):
        for n, (dims, kind) in KEPT_BLOCKS._asdict().items():
            scratch[n + suffix] = pltpu.VMEM(dims, kind)
        for n, size in zip(Weights._fields, WEIGHT_SIZES):
            scratch[n + suffix] = pltpu.VMEM((1,) + size, BF)
    scratch.update(
        totals_a=pltpu.VMEM((24, D), F32),
        totals_b=pltpu.VMEM((24, D), F32),
        heads=pltpu.VMEM((3, RUN + 16, 128), F32),
        **mlp_scratch(),
        **attention_scratch(),
        d_mid=pltpu.VMEM((1, RUN, D), F32),
        grad=pltpu.VMEM((1, RUN, D), F32),
        normed=pltpu.VMEM((RUN, D), BF),
        acc_vec=pltpu.VMEM((8, 12 * D), F32),
        tokens_in=pltpu.VMEM((IMG * CHUNKS, SEQ, D), BF),
        grad_low=pltpu.VMEM((IMG * CHUNKS, SEQ, D), BF),
        fetch_sem=pltpu.SemaphoreType.DMA((2,)),
        load_sem=pltpu.SemaphoreType.DMA((4,)),
        save_sem=pltpu.SemaphoreType.DMA((7,)),
        weight_sem=pltpu.SemaphoreType.DMA((4,)),
    )
    return call_kernel(front_kernel, ins, outs, scratch, FRONT_LIMIT, "front")


FRONT_LIMIT = 60


def mlp_scratch():
    return dict(
        low_grad=pltpu.VMEM((RUN, D), BF),
        hidden=pltpu.VMEM((RUN, FF), F32),
        d_hidden=pltpu.VMEM((RUN, FF), BF),
        acc_up=pltpu.VMEM((D, FF), F32),
        acc_down=pltpu.VMEM((FF, D), F32),
    )


def attention_scratch():
    return dict(
        d_branch=pltpu.VMEM((RUN, D), BF),
        d_heads=pltpu.VMEM((3, RUN + 16, 128), F32),
        proj=pltpu.VMEM((9, RUN + 16, 128), F32),
        d_low=pltpu.VMEM((RUN, 3 * D), BF),
        acc_attn=pltpu.VMEM((D, 3 * D), F32),
        acc_out=pltpu.VMEM((D, D), F32),
        small=pltpu.VMEM((128, 128), F32),
    )


def back_kernel(r):
    step = pl.program_id(0)
    first = step == 0
    kept_in = [getattr(r, n + "_in") for n in Kept._fields] + [r.grad_in]
    kept = [getattr(r, n) for n in Kept._fields] + [r.grad_all]
    weights_in = [getattr(r, n + "_in") for n in Weights._fields]
    weights = [getattr(r, n) for n in Weights._fields]

    def load(k, chunk):
        if k >= ATTN:
            return pltpu.make_async_copy(weights_in[k - ATTN], weights[k - ATTN], r.sem.at[k, 0])
        size = kept[k].shape[0] // CHUNKS
        at = pl.ds(chunk * size, size)
        return pltpu.make_async_copy(kept_in[k].at[at], kept[k].at[at], r.sem.at[k, chunk])

    @pl.when(first)
    def _():
        for chunk in range(CHUNKS):
            for k in (GRAD, DOWN, SLOPE, UP, MIDDLE, ACT, OUT, MIXED, HEADS_P, HEADS_A, ATTN, STREAM):
                if k < ATTN or chunk == 0:
                    load(k, chunk).start()
        r.acc_vec[...] = jnp.zeros_like(r.acc_vec)
        for block in range(3):
            r.d_heads[block, RUN : RUN + 16, :] = jnp.zeros((16, 128), F32)

    def ready(*which):
        for k in which:
            if k < ATTN:
                load(k, step).wait()
            else:

                @pl.when(first)
                def _():
                    load(k, 0).wait()

    views = {}
    for n, ref in zip(Kept._fields, kept):
        size = ref.shape[0] // CHUNKS
        views[n] = ref.at[pl.ds(step * size, size)]
    q = types.SimpleNamespace(**{**vars(r), **views}, layer=0, first=first, ready=ready)
    back_mlp(q, r.grad_all.at[pl.ds(step, 1)])
    back_attention(q, r.d_mid, r.grad)
    for image in range(IMG):
        r.grad_out[image] = r.grad[0, SEQ * image : SEQ * (image + 1), :]

    @pl.when(step == CHUNKS - 1)
    def _():
        fill_small(r.small, r.acc_vec, r.sums[...])
        plan = mlp_plan(r, r.keep, r.send, r.send, UP_AT, DOWN_AT)
        emit_packed(r.core[0], plan + attention_plan(r, r.keep, r.send, 0))


def back_call(core, grad, vector, ahead):
    half = shape(F32, 4, 4, 4, ROWS, 128)
    ins = dict(
        core=(core, pl.BlockSpec(memory_space=pltpu.SMEM)),
        grad_in=(grad, ANYWHERE),
        vec=(vector, whole(2, 12 * D)),
        sums=(ahead.sums, whole(1, 128)),
    )
    scratch = {}
    for n, size in zip(Weights._fields, WEIGHT_SIZES):
        ins[n + "_in"] = (getattr(ahead, n), ANYWHERE)
        scratch[n] = pltpu.VMEM((1,) + size, BF)
    for n, (dims, kind) in KEPT_BLOCKS._asdict().items():
        ins[n + "_in"] = (getattr(ahead, n), ANYWHERE)
        scratch[n] = pltpu.VMEM((CHUNKS * dims[0],) + dims[1:], kind)
    outs = dict(
        grad_out=(shape(F32, IMG * CHUNKS, SEQ, D), imaged(SEQ, D)),
        keep=(half, VMEM_WHOLE),
        send=(half, VMEM_WHOLE),
    )
    scratch.update(
        **mlp_scratch(),
        **attention_scratch(),
        grad_all=pltpu.VMEM((CHUNKS, RUN, D), F32),
        d_mid=pltpu.VMEM((1, RUN, D), F32),
        grad=pltpu.VMEM((1, RUN, D), F32),
        normed=pltpu.VMEM((RUN, D), BF),
        acc_vec=pltpu.VMEM((8, 12 * D), F32),
        sem=pltpu.SemaphoreType.DMA((12, CHUNKS)),
    )
    return call_kernel(back_kernel, ins, outs, scratch, BACK_LIMIT, "back")


BACK_LIMIT = 58


def local_step(core, tokens, grad_out, masters, vector, shares):
    ahead = front(core, tokens, grad_out, masters, vector)
    got, early = lax.optimization_barrier((swap_core(ahead.send), shares[:2]))
    parts = add_core(ahead.keep, got)
    grad, parts = lax.optimization_barrier((ahead.grad_out, parts))
    parts_one = ring(0, parts)
    back = back_call(core, grad, vector, ahead)
    send, parts_one = lax.optimization_barrier((back.send, parts_one))
    got, late = lax.optimization_barrier((swap_core(send), shares[2:]))
    parts_zero = ring(0, add_core(back.keep, got))
    return ahead.block_out, back.grad_out, parts_zero + parts_one, early + late


def stage_position(stage):
    deep, high, core, across = place_of(lax.axis_index(GROUP_AXES))
    if stage == 2:
        return deep
    return jnp.where(core == stage, across, high)


def add_core_kernel(keep, got, *outs):
    me = stage_position(0)
    for shift in range(4):
        at = me ^ shift

        @pl.loop(0, 16)
        def _(i):
            outs[shift][i // 4, i % 4] = keep[at, i // 4, i % 4] + got[at, i // 4, i % 4]


def add_first_kernel(*refs):
    sources = [refs[4 * k : 4 * k + 4] for k in range(2)]
    outs = refs[-4:]
    me = stage_position(1)
    for shift in range(4):
        at = me ^ shift

        @pl.loop(0, 4)
        def _(i):
            for layer, (own, one, two, three) in enumerate(sources):
                outs[shift][i, layer] = (own[at, i] + one[at, i]) + (two[at, i] + three[at, i])


def add_second_kernel(own, one, two, three, *outs):
    me = stage_position(2)
    for shift in range(4):
        at = me ^ shift
        outs[shift][...] = (own[at] + one[at]) + (two[at] + three[at])


def add_third_kernel(own, one, two, three, out):
    out[...] = (own[...] + one[...]) + (two[...] + three[...])


def call_add(kernel, values, out_dims, count, name):
    return pl.pallas_call(
        kernel,
        out_shape=[shape(F32, *out_dims, 128)] * count,
        in_specs=[VMEM_WHOLE] * len(values),
        out_specs=[VMEM_WHOLE] * count,
        compiler_params=pltpu.CompilerParams(vmem_limit_bytes=32 * 2**20),
        name=name,
    )(*values)


def ring(stage, parts):
    got = [lax.ppermute(parts[s], GROUP_AXES, ring_pairs(stage, s)) for s in (2, 1, 3)]
    return [parts[0]] + got


def swap_core(send):
    return lax.ppermute(send, GROUP_AXES, core_pairs())


def add_core(keep, got):
    return call_add(add_core_kernel, [keep, got], (4, 4, ROWS), 4, "add_core")


def finish_sums(parts):
    parts = call_add(add_first_kernel, parts, (4, 2, ROWS), 4, "add_first")
    parts = call_add(add_second_kernel, ring(1, parts), (2, ROWS), 4, "add_second")
    own = call_add(add_third_kernel, ring(2, parts), (2, ROWS), 1, "add_third")[0]
    return own, lax.ppermute(own, "grp", [(0, 1), (1, 0)])


def adam_step(gradient, moment_one, moment_two, weight, rate):
    moment_one = beta_one * moment_one + (1 - beta_one) * gradient
    moment_two = beta_two * moment_two + (1 - beta_two) * gradient * gradient
    fix_one = 1 - beta_one**STEP
    fix_two = 1 - beta_two**STEP
    update = (
        moment_one / fix_one / (jnp.sqrt(moment_two / fix_two) + adam_eps) + decay_rate * weight
    )
    return (moment_one, moment_two, weight - rate * update)


def finish_kernel(*refs):
    own, other = ([ref.at[k] for k in range(2)] for ref in refs[:2])
    weights, firsts, seconds, outers = (refs[2 + 5 * k : 7 + 5 * k] for k in range(4))
    outs = refs[22:]
    new_firsts, new_seconds, changes, new_outers, finals, copies = (
        outs[5 * k : 5 * k + 5] for k in range(6)
    )
    rms = outs[30]

    def gathered(refs, kind, row):
        if kind == 4:
            return jnp.concatenate([ref[SMALL_AT : SMALL_AT + 1, 0:36] for ref in refs], 0)
        start, rows, width = (
            (QKV_AT, 3, 9),
            (PROJ_AT, 3, 3),
            (UP_AT, 3, 12),
            (DOWN_AT, 12, 3),
        )[kind]
        lines = [start + rows * c + row for c in range(width)]
        return jnp.concatenate(
            [
                jnp.concatenate([ref[line : line + 1, :] for ref in refs], 0)
                for line in lines
            ],
            1,
        )

    for kind in range(5):
        rate = rates()[kind]
        for row in range(1 if kind == 4 else weights[kind].shape[0]):
            at = slice(None) if kind == 4 else row
            weight = weights[kind][at]
            moments = (firsts[kind][at], seconds[kind][at])
            one, two, updated = adam_step(gathered(own, kind, row), *moments, weight, rate)
            updated_other = adam_step(gathered(other, kind, row), *moments, weight, rate)[2]
            change = ((weight - updated) + (weight - updated_other)) / 2
            outer = outer_decay * outers[kind][at] + change
            final = weight - outer_rate * (change + outer_decay * outer)
            new_firsts[kind][at] = one
            new_seconds[kind][at] = two
            changes[kind][at] = change
            new_outers[kind][at] = outer
            finals[kind][at] = final
            copies[kind][at] = final.astype(jnp.bfloat16)
    for layer in range(2):
        totals = [
            ref[SMALL_AT : SMALL_AT + 1, SUMS_AT : SUMS_AT + 3] for ref in (own[layer], other[layer])
        ]
        rms[layer : layer + 1, :] = jnp.sqrt((totals[0] + totals[1]) / ENTRIES)


def rows_first(value):
    return value if value.ndim == 2 else jnp.swapaxes(value, 0, 1)


def finish(own, other, weights, firsts, seconds, outers):
    given = [*weights, *[rows_first(v) for v in (*firsts, *seconds, *outers)]]
    full = [jax.ShapeDtypeStruct(v.shape, jnp.float32) for v in given[:5]]
    low = [jax.ShapeDtypeStruct(v.shape, jnp.bfloat16) for v in given[:5]]
    results = pl.pallas_call(
        finish_kernel,
        out_shape=full * 5 + low + [jax.ShapeDtypeStruct((2, 3), jnp.float32)],
        in_specs=[VMEM_WHOLE] * 22,
        out_specs=[VMEM_WHOLE] * 31,
        name="finish",
    )(own, other, *given)
    results = [rows_first(v) for v in results[:30]] + [results[30]]
    return [v[None] for v in results[:10]] + results[10:]

def body(
    tokens,
    grad_out,
    weight_qkv,
    weight_proj,
    weight_up,
    weight_down,
    weight_vector,
    old_first_qkv,
    old_first_proj,
    old_first_up,
    old_first_down,
    old_first_vector,
    old_second_qkv,
    old_second_proj,
    old_second_up,
    old_second_down,
    old_second_vector,
    old_outer_qkv,
    old_outer_proj,
    old_outer_up,
    old_outer_down,
    old_outer_vector,
):
    masters = (weight_qkv, weight_proj, weight_up, weight_down, weight_vector)
    old_firsts = (old_first_qkv, old_first_proj, old_first_up, old_first_down, old_first_vector)
    old_seconds = (
        old_second_qkv,
        old_second_proj,
        old_second_up,
        old_second_down,
        old_second_vector,
    )
    old_outers = (old_outer_qkv, old_outer_proj, old_outer_up, old_outer_down, old_outer_vector)
    owner_index = lax.axis_index(GROUP_AXES)
    core = jnp.reshape(owner_index // 4 % 2, (1,)).astype(jnp.int32)
    shares = []
    for kind_index in range(5):
        share_rows = old_firsts[kind_index].shape[1]
        at = owner_index * share_rows
        share = lax.dynamic_slice_in_dim(masters[kind_index], at, share_rows, 1)
        shares.append(rows_first(share))
    block_out, grad_tokens, parts, shares = local_step(
        core, tokens, grad_out, masters[:4], weight_vector, shares
    )
    own, other = finish_sums(parts)
    results = finish(own, other, shares, old_firsts, old_seconds, old_outers)
    return (block_out, grad_tokens, *results)


def solution(mesh):
    placed = (
        P(("grp", "wide", "narrow"), None, None),
        P(("grp", "wide", "narrow"), None, None),
        P(),
        P(),
        P(),
        P(),
        P(),
        P(None, ("wide", "narrow"), None),
        P(None, ("wide", "narrow"), None),
        P(None, ("wide", "narrow"), None),
        P(None, ("wide", "narrow"), None),
        P(None, ("wide", "narrow")),
        P(None, ("wide", "narrow"), None),
        P(None, ("wide", "narrow"), None),
        P(None, ("wide", "narrow"), None),
        P(None, ("wide", "narrow"), None),
        P(None, ("wide", "narrow")),
        P(None, ("wide", "narrow"), None),
        P(None, ("wide", "narrow"), None),
        P(None, ("wide", "narrow"), None),
        P(None, ("wide", "narrow"), None),
        P(None, ("wide", "narrow")),
    )
    return jax.shard_map(
        body,
        mesh=mesh,
        in_specs=placed,
        out_specs=(
            P(("grp", "wide", "narrow"), None, None),
            P(("grp", "wide", "narrow"), None, None),
            P("grp", None, ("wide", "narrow"), None),
            P("grp", None, ("wide", "narrow"), None),
            P("grp", None, ("wide", "narrow"), None),
            P("grp", None, ("wide", "narrow"), None),
            P("grp", None, ("wide", "narrow")),
            P("grp", None, ("wide", "narrow"), None),
            P("grp", None, ("wide", "narrow"), None),
            P("grp", None, ("wide", "narrow"), None),
            P("grp", None, ("wide", "narrow"), None),
            P("grp", None, ("wide", "narrow")),
            P(None, ("wide", "narrow"), None),
            P(None, ("wide", "narrow"), None),
            P(None, ("wide", "narrow"), None),
            P(None, ("wide", "narrow"), None),
            P(None, ("wide", "narrow")),
            P(None, ("wide", "narrow"), None),
            P(None, ("wide", "narrow"), None),
            P(None, ("wide", "narrow"), None),
            P(None, ("wide", "narrow"), None),
            P(None, ("wide", "narrow")),
            P(None, ("wide", "narrow"), None),
            P(None, ("wide", "narrow"), None),
            P(None, ("wide", "narrow"), None),
            P(None, ("wide", "narrow"), None),
            P(None, ("wide", "narrow")),
            P(None, ("wide", "narrow"), None),
            P(None, ("wide", "narrow"), None),
            P(None, ("wide", "narrow"), None),
            P(None, ("wide", "narrow"), None),
            P(None, ("wide", "narrow")),
            P(),
        ),
        check_vma=False,
    )
```

```python
import types
import typing

import jax
import jax.numpy as jnp
from jax import lax
from jax.experimental import pallas as pl
from jax.experimental.pallas import tpu as pltpu
from jax.sharding import PartitionSpec as P

D = 384
HEADS = 6
HEAD_DIM = 64
FF = 1536
SEQ = 50
STEP = 10


beta_one = 0.9
beta_two = 0.95
adam_eps = 1e-08
decay_rate = 0.1
outer_decay = 0.9
outer_rate = 0.7

ROWS = 112
UP_AT, DOWN_AT, QKV_AT, PROJ_AT, SMALL_AT = 0, 36, 72, 99, 108
SUMS_AT = 64
ENTRIES = 98304000
VMEM_WHOLE = pl.BlockSpec(memory_space=pltpu.VMEM)
ANYWHERE = pl.BlockSpec(memory_space=pl.ANY)
GROUP_AXES = ("wide", "narrow")
IMG = 10
CHUNKS = 2
RUN = 512
REAL = IMG * SEQ
TOGETHER = 5
TOGETHER_BACK = 5
G1, B1, BQ, BV, BO, G2, B2, BU, BD = 0, 384, 768, 1152, 1536, 1920, 2304, 2688, 4224
BF = jnp.bfloat16
F32 = jnp.float32
WEIGHT_SIZES = ((D, 3 * D), (D, D), (D, FF), (FF, D))


def rates():
    return (1.5 * D ** (-0.5), 1.5 * (D // 4) ** (-0.5), 1.5 * D ** (-0.5), 1.5 * FF ** (-0.5), 2.0)


def place_of(owner):
    return owner // 32, owner // 8 % 4, owner // 4 % 2, owner % 4


def owner_of(deep, high, core, across):
    return ((deep * 4 + high) * 2 + core) * 4 + across


def core_pairs():
    return [(o, o ^ 4) for o in range(128)]


def ring_pairs(stage, shift):
    pairs = []
    for o in range(128):
        deep, high, core, across = place_of(o)
        if stage == 2:
            deep = deep ^ shift
        elif core == stage:
            across = across ^ shift
        else:
            high = high ^ shift
        pairs.append((o, owner_of(deep, high, core, across)))
    return pairs


def dot(left, right, left_dim=1, right_dim=0):
    return lax.dot_general(
        left, right, (((left_dim,), (right_dim,)), ((), ())), preferred_element_type=F32
    )


def normalise(rows):
    center = rows - jnp.sum(rows, -1, keepdims=True) * (1 / D)
    rate = lax.rsqrt(jnp.sum(center * center, -1, keepdims=True) * (1 / D) + 1e-06)
    return center * rate, rate


def norm_back(grad, unit, rate, gain):
    scaled = grad * gain
    first = jnp.sum(scaled, -1, keepdims=True) * (1 / D)
    second = jnp.sum(scaled * unit, -1, keepdims=True) * (1 / D)
    return rate * (scaled - first - unit * second)


def gelu_parts(value):
    area = 0.5 + 0.5 * lax.erf(value * 0.7071067811865476)
    bell = jnp.exp(-0.5 * value * value)
    return value * area, area + value * bell * 0.3989422804014327


def fold(values):
    return jnp.sum(values.reshape(-1, 8, values.shape[-1]), 0)


def halves_of(rows, low, keep):
    zero = jnp.zeros_like(rows)
    top = jnp.where(keep & low, rows, zero)
    bottom = jnp.where(keep & ~low, rows, zero)
    return jnp.concatenate([top, bottom], 0).astype(BF)


def masks():
    low = lax.broadcasted_iota(jnp.int32, (64, 128), 1) < 64
    keep = lax.broadcasted_iota(jnp.int32, (64, 128), 0) < SEQ
    return low, keep


def bias(r, start, stop):
    return r.vec[r.layer : r.layer + 1, start:stop]


def unpack(images, base, target):
    target[0, REAL - 4 : RUN, :] = jnp.zeros((RUN + 4 - REAL, D), F32)
    for image in range(IMG):
        target[0, SEQ * image : SEQ * (image + 1), :] = images[base + image].astype(F32)


def ahead_norm(r):
    def norm_block(i, carry):
        rows = pl.ds(pl.multiple_of(i * 64, 64), 64)
        unit, _ = normalise(r.stream[0, rows, :])
        r.normed[rows, :] = (unit * bias(r, G1, B1) + bias(r, B1, BQ)).astype(BF)
        return carry

    lax.fori_loop(0, RUN // 64, norm_block, 0)


def ahead_attention(r):
    proj, heads = r.proj, r.heads
    for third in range(3):
        result = dot(r.normed[...], r.w_attn[0, :, D * third : D * (third + 1)])
        if third == 0:
            result = result + bias(r, BQ, BV)
        if third == 2:
            result = result + bias(r, BV, BO)
        for block in range(3):
            proj[3 * third + block, 0:RUN, :] = result[:, 128 * block : 128 * (block + 1)]

    low, keep = masks()
    keep_keys = keep[0:56]

    def attend(i, carry):
        items = [(i * TOGETHER + k, pair) for k in range(TOGETHER) for pair in range(3)]
        loaded = []
        for image, pair in items:
            at = pl.ds(image * SEQ, 64)
            query = proj[pair, at, :]
            key = jnp.where(keep, proj[3 + pair, at, :], 0.0).astype(BF)
            value = jnp.where(keep, proj[6 + pair, at, :], 0.0).astype(BF)
            r.p_img[image, pair] = jnp.where(keep, query, 0.0).astype(BF)
            r.p_img[image, 3 + pair] = key
            r.p_img[image, 6 + pair] = value
            loaded.append((key, halves_of(query * 0.125, low, keep), value))
        scores = [dot(key, spread, 1, 1)[0:56] for key, spread, _ in loaded]
        weights = []
        for (image, pair), score in zip(items, scores):
            score = jnp.where(keep_keys, score, -1e30)
            raised = jnp.exp(score - jnp.max(score, 0, keepdims=True))
            weight = raised * (1.0 / jnp.sum(raised, 0, keepdims=True))
            weight = jnp.concatenate([weight, jnp.zeros((8, 128), F32)], 0).astype(BF)
            r.a_img[image, pair] = weight
            weights.append(weight)
        results = [dot(weight, value, 0, 0) for weight, (_, _, value) in zip(weights, loaded)]
        for (image, pair), both in zip(items, results):
            one = jnp.where(low, both[0:64], both[64:128])
            heads[pair, pl.ds(image * SEQ, SEQ), :] = one[0:SEQ]
        return carry

    lax.fori_loop(0, IMG // TOGETHER, attend, 0)
    for block in range(3):
        r.mixed[0, :, 128 * block : 128 * (block + 1)] = heads[block, 0:RUN, :].astype(BF)


def ahead_mlp(r):
    totals = r.totals
    real = lax.broadcasted_iota(jnp.int32, (RUN, D), 0) < REAL
    before = r.stream[0]
    branch = dot(r.mixed[0], r.w_out[0]) + bias(r, BO, G2)
    between = before + branch
    r.middle[0] = between
    totals[0:8, :] += fold(jnp.where(real, before * before, 0.0))
    totals[8:16, :] += fold(jnp.where(real, branch * branch, 0.0))

    def norm_block(i, carry):
        rows = pl.ds(pl.multiple_of(i * 64, 64), 64)
        unit, _ = normalise(r.middle[0, rows, :])
        r.normed[rows, :] = (unit * bias(r, G2, B2) + bias(r, B2, BU)).astype(BF)
        return carry

    lax.fori_loop(0, RUN // 64, norm_block, 0)
    r.hidden[...] = dot(r.normed[...], r.w_up[0])
    for row in range(0, RUN, 32):
        for column in range(0, FF, 256):
            part = r.hidden[row : row + 32, column : column + 256]
            part = part + bias(r, BU + column, BU + column + 256)
            bent, tilt = gelu_parts(part)
            r.act[0, row : row + 32, column : column + 256] = bent.astype(BF)
            r.slope[0, row : row + 32, column : column + 256] = tilt.astype(BF)
    tail = dot(r.act[0], r.w_down[0]) + bias(r, BD, BD + D)
    totals[16:24, :] += fold(jnp.where(real, tail * tail, 0.0))
    r.after[0] = r.middle[0] + tail


def total_row(totals):
    lane = lax.broadcasted_iota(jnp.int32, (1, 128), 1)
    row = jnp.zeros((1, 128), F32)
    for k in range(3):
        row = jnp.where(lane == SUMS_AT + k, jnp.sum(totals[8 * k : 8 * k + 8, :]), row)
    return row


def chunked(*dims):
    return pl.BlockSpec((1,) + dims, lambda c: (c,) + (0,) * len(dims))


def imaged(*dims):
    return pl.BlockSpec((IMG,) + dims, lambda c: (c,) + (0,) * len(dims))


def whole(*dims):
    return pl.BlockSpec(dims, lambda c: (0,) * len(dims))


def held(*dims):
    return pl.BlockSpec(dims, lambda c: (0,) * len(dims), pipeline_mode=pl.Buffered(1))


def shape(kind, *dims):
    return jax.ShapeDtypeStruct(dims, kind)


def emit_packed(core, plan):
    def emit(own):
        @pl.loop(0, 16)
        def _(block):
            deep, high = block // 4, block % 4
            for source, each, width, *targets in plan:
                height = 8 * each
                base = pl.multiple_of(block * height, 8)
                for column in range(width):
                    rows = source[pl.ds(base, height), column * 128 : (column + 1) * 128]
                    for k in range(8):
                        target, start = targets[0 if k // 4 == own else 1]
                        at = start + each * column
                        first, second = (k, high) if k < 4 else (high, k - 4)
                        target.at[first, second, deep][at : at + each, :] = rows[
                            each * k : each * (k + 1)
                        ]

    for own in range(2):

        @pl.when(core == own)
        def _():
            emit(own)


HEADS_P, HEADS_A, MIXED, STREAM, MIDDLE, ACT, SLOPE, GRAD, ATTN, OUT, UP, DOWN = range(12)


def back_mlp(r, grad):
    r.ready(GRAD, DOWN)
    here = grad[0]
    r.acc_vec[:, BD : BD + D] += fold(here)
    r.low_grad[...] = here.astype(BF)
    r.hidden[...] = dot(r.low_grad[...], r.w_down[0], 1, 1)
    r.ready(SLOPE)
    for column in range(0, FF, 256):
        total = jnp.zeros((8, 256), F32)
        for row in range(0, RUN, 32):
            at = slice(row, row + 32)
            part = r.hidden[at, column : column + 256]
            part = part * r.slope[0, at, column : column + 256].astype(F32)
            r.d_hidden[at, column : column + 256] = part.astype(BF)
            total = total + fold(part)
        r.acc_vec[:, BU + column : BU + column + 256] += total
    r.ready(UP, MIDDLE)
    d_normed = dot(r.d_hidden[...], r.w_up[0], 1, 1)
    unit, rate = normalise(r.middle[0])
    gain = bias(r, G2, B2)
    r.normed[...] = (unit * gain + bias(r, B2, BU)).astype(BF)
    r.acc_vec[:, G2:B2] += fold(d_normed * unit)
    r.acc_vec[:, B2:BU] += fold(d_normed)
    r.d_mid[0] = grad[0] + norm_back(d_normed, unit, rate, gain)
    r.ready(ACT)
    r.acc_down[...] = jnp.where(r.first, 0.0, r.acc_down[...]) + dot(r.act[0], r.low_grad[...], 0, 0)
    r.acc_up[...] = jnp.where(r.first, 0.0, r.acc_up[...]) + dot(r.normed[...], r.d_hidden[...], 0, 0)


def back_attention(r, d_mid, result):
    between = d_mid[0]
    r.acc_vec[:, BO:G2] += fold(between)
    r.d_branch[...] = between.astype(BF)
    r.ready(OUT, MIXED)
    product = dot(r.d_branch[...], r.w_out[0], 1, 1)
    for block in range(3):
        r.d_heads[block, 0:RUN, :] = product[:, 128 * block : 128 * (block + 1)]
    r.acc_out[...] = jnp.where(r.first, 0.0, r.acc_out[...]) + dot(r.mixed[0], r.d_branch[...], 0, 0)
    low, keep = masks()
    p_img, a_img, d_heads, d_proj = r.p_img, r.a_img, r.d_heads, r.proj
    for block in range(9):
        d_proj[block, REAL - 4 : RUN + 16, :] = jnp.zeros((RUN + 20 - REAL, 128), F32)

    def attend(i, carry):
        items = [(i * TOGETHER_BACK + k, pair) for k in range(TOGETHER_BACK) for pair in range(3)]
        loaded = []
        for image, pair in items:
            rows = d_heads[pair, pl.ds(image * SEQ, 64), :]
            spread = halves_of(p_img[image, pair].astype(F32) * 0.125, low, keep)
            loaded.append((spread, halves_of(rows, low, keep)))
        d_weights = [
            dot(p_img[image, 6 + pair], d_spread, 1, 1)
            for (image, pair), (_, d_spread) in zip(items, loaded)
        ]
        d_values = [
            dot(a_img[image, pair], d_spread) for (image, pair), (_, d_spread) in zip(items, loaded)
        ]
        d_scores = []
        for (image, pair), d_weight in zip(items, d_weights):
            weight = a_img[image, pair].astype(F32)
            product = weight * d_weight
            d_scores.append((product - weight * jnp.sum(product, 0, keepdims=True)).astype(BF))
        d_keys = [dot(d_score, spread) for d_score, (spread, _) in zip(d_scores, loaded)]
        d_both = [
            dot(d_score, p_img[image, 3 + pair], 0, 0)
            for (image, pair), d_score in zip(items, d_scores)
        ]
        for (image, pair), d_key, both, d_value in zip(items, d_keys, d_both, d_values):
            d_query = jnp.where(low, both[0:64], both[64:128]) * 0.125
            at = pl.ds(image * SEQ, SEQ)
            d_proj[pair, at, :] = d_query[0:SEQ]
            d_proj[3 + pair, at, :] = d_key[0:SEQ]
            d_proj[6 + pair, at, :] = d_value[0:SEQ]
        return carry

    r.ready(HEADS_P, HEADS_A)
    lax.fori_loop(0, IMG // TOGETHER_BACK, attend, 0)
    for block in range(9):
        part = d_proj[block, 0:RUN, :]
        r.d_low[:, 128 * block : 128 * (block + 1)] = part.astype(BF)
        if block < 3:
            r.acc_vec[:, BQ + 128 * block : BQ + 128 * (block + 1)] += fold(part)
        if block >= 6:
            r.acc_vec[:, BV + 128 * (block - 6) : BV + 128 * (block - 5)] += fold(part)
    r.ready(ATTN, STREAM)
    d_normed = dot(r.d_low[...], r.w_attn[0], 1, 1)
    unit, rate = normalise(r.stream[0])
    gain = bias(r, G1, B1)
    r.normed[...] = (unit * gain + bias(r, B1, BQ)).astype(BF)
    r.acc_vec[:, G1:B1] += fold(d_normed * unit)
    r.acc_vec[:, B1:BQ] += fold(d_normed)
    result[0] = d_mid[0] + norm_back(d_normed, unit, rate, gain)
    r.acc_attn[...] = jnp.where(r.first, 0.0, r.acc_attn[...]) + dot(r.normed[...], r.d_low[...], 0, 0)


def fill_small(small, acc_vec, row):
    total = jnp.sum(acc_vec[...], 0, keepdims=True)
    small[...] = jnp.broadcast_to(row, (128, 128))
    for owner in range(128):
        small[owner : owner + 1, 0:36] = total[:, 36 * owner : 36 * (owner + 1)]


def mlp_plan(r, keep, send_up, send_down, up_at, down_at):
    return [
        (r.acc_up, 3, 12, (keep, UP_AT), (send_up, up_at)),
        (r.acc_down, 12, 3, (keep, DOWN_AT), (send_down, down_at)),
    ]


def attention_plan(r, keep, send, shift):
    return [
        (r.acc_attn, 3, 9, (keep, QKV_AT - shift), (send, QKV_AT - shift)),
        (r.acc_out, 3, 3, (keep, PROJ_AT - shift), (send, PROJ_AT - shift)),
        (r.small, 1, 1, (keep, SMALL_AT - shift), (send, SMALL_AT - shift)),
    ]


def spaces(ins, outs, scratch, refs):
    return types.SimpleNamespace(**dict(zip([*ins, *outs, *scratch], refs)))


def call_kernel(kernel, ins, outs, scratch, limit, name):
    results = pl.pallas_call(
        lambda *refs: kernel(spaces(ins, outs, scratch, refs)),
        grid=(CHUNKS,),
        out_shape=[v[0] for v in outs.values()],
        in_specs=[v[1] for v in ins.values()],
        out_specs=[v[1] for v in outs.values()],
        scratch_shapes=list(scratch.values()),
        compiler_params=pltpu.CompilerParams(vmem_limit_bytes=limit * 2**20),
        name=name,
    )(*[v[0] for v in ins.values()])
    return types.SimpleNamespace(**dict(zip(outs, results)))


class Kept(typing.NamedTuple):
    p_img: typing.Any
    a_img: typing.Any
    mixed: typing.Any
    stream: typing.Any
    middle: typing.Any
    act: typing.Any
    slope: typing.Any


class Weights(typing.NamedTuple):
    w_attn: typing.Any
    w_out: typing.Any
    w_up: typing.Any
    w_down: typing.Any


KEPT_BLOCKS = Kept(
    ((IMG, 9, 64, 128), BF),
    ((IMG, 3, 64, 128), BF),
    ((1, RUN, D), BF),
    ((1, RUN, D), F32),
    ((1, RUN, D), F32),
    ((1, RUN, FF), BF),
    ((1, RUN, FF), BF),
)


def front_kernel(r):
    step = pl.program_id(0)
    first, final = step == 0, step == CHUNKS - 1
    kept = [Kept(*[getattr(r, n + s) for n in Kept._fields]) for s in ("_a", "_b")]
    weights = [Weights(*[getattr(r, n + s) for n in Weights._fields]) for s in ("_a", "_b")]
    kept_out = [getattr(r, n) for n in Kept._fields]
    weights_out = [getattr(r, n) for n in Weights._fields]
    masters = (r.m_attn, r.m_out, r.m_up, r.m_down)
    stages = (r.acc_attn, r.acc_out, r.acc_up, r.acc_down)

    def load(layer, k):
        return pltpu.make_async_copy(masters[k].at[layer], stages[k], r.load_sem.at[k])

    def save(k, chunk):
        size = kept[0][k].shape[0]
        target = kept_out[k].at[pl.ds(chunk * size, size)]
        return pltpu.make_async_copy(kept[0][k], target, r.save_sem.at[k])

    def save_weight(k):
        return pltpu.make_async_copy(weights[0][k], weights_out[k], r.weight_sem.at[k])

    def take(layer, k):
        load(layer, k).wait()
        weights[layer][k][0] = stages[k][...].astype(BF)

    def fetch(k):
        source, target = ((r.tokens, r.tokens_in), (r.grad_in, r.grad_low))[k]
        return pltpu.make_async_copy(source, target, r.fetch_sem.at[k])

    @pl.when(first)
    def _():
        fetch(0).start()
        for k in range(4):
            load(0, k).start()
        fetch(1).start()
        r.totals_a[...] = jnp.zeros_like(r.totals_a)
        r.totals_b[...] = jnp.zeros_like(r.totals_b)
        r.acc_vec[...] = jnp.zeros_like(r.acc_vec)
        for block in range(9):
            r.proj[block, RUN : RUN + 16, :] = jnp.zeros((16, 128), F32)
        for block in range(3):
            r.heads[block, REAL - 4 : RUN + 16, :] = jnp.zeros((RUN + 20 - REAL, 128), F32)
            r.d_heads[block, RUN : RUN + 16, :] = jnp.zeros((16, 128), F32)
        fetch(0).wait()

    @pl.when(step > 0)
    def _():
        for k in range(7):
            save(k, step - 1).wait()

    shared = dict(
        first=first,
        ready=lambda *which: None,
        vec=r.vec,
        normed=r.normed,
        proj=r.proj,
        heads=r.heads,
        hidden=r.hidden,
    )
    zero = types.SimpleNamespace(
        **shared,
        **kept[0]._asdict(),
        **weights[0]._asdict(),
        layer=0,
        totals=r.totals_a,
        after=kept[1].stream,
    )
    one = types.SimpleNamespace(
        **shared,
        **kept[1]._asdict(),
        **weights[1]._asdict(),
        layer=1,
        totals=r.totals_b,
        after=r.d_mid,
        d_heads=r.d_heads,
        d_hidden=r.d_hidden,
        d_low=r.d_low,
        d_mid=r.d_mid,
        d_branch=r.d_branch,
        low_grad=r.low_grad,
        acc_vec=r.acc_vec,
        acc_attn=r.acc_attn,
        acc_out=r.acc_out,
        acc_up=r.acc_up,
        acc_down=r.acc_down,
        small=r.small,
    )
    unpack(r.tokens_in, step * IMG, zero.stream)
    ahead_norm(zero)

    @pl.when(first)
    def _():
        take(0, 0)

    ahead_attention(zero)
    for k in range(4):
        save(k, step).start()

    @pl.when(first)
    def _():
        for k in range(1, 4):
            take(0, k)
        for k in range(4):
            load(1, k).start()
            save_weight(k).start()

    ahead_mlp(zero)
    for k in range(4, 7):
        save(k, step).start()
    ahead_norm(one)

    @pl.when(first)
    def _():
        for k in range(4):
            take(1, k)
        fetch(1).wait()

    ahead_attention(one)
    ahead_mlp(one)
    for image in range(IMG):
        r.block_out[image] = one.after[0, SEQ * image : SEQ * (image + 1), :].astype(BF)
    unpack(r.grad_low, step * IMG, r.grad)
    back_mlp(one, r.grad)
    back_attention(one, one.d_mid, r.grad_out)

    @pl.when(final)
    def _():
        r.sums[...] = total_row(r.totals_a)
        fill_small(r.small, r.acc_vec, total_row(r.totals_b))
        plan = mlp_plan(r, r.keep, r.send, r.send, UP_AT, DOWN_AT)
        emit_packed(r.core[0], plan + attention_plan(r, r.keep, r.send, 0))
        for k in range(7):
            save(k, step).wait()
        for k in range(4):
            save_weight(k).wait()


def front(core, tokens, grad_out, masters, vector):
    smem = pl.BlockSpec(memory_space=pltpu.SMEM)
    ins = dict(
        core=(core, smem),
        tokens=(tokens, ANYWHERE),
        grad_in=(grad_out, ANYWHERE),
        vec=(vector, whole(2, 12 * D)),
        m_attn=(masters[0], ANYWHERE),
        m_out=(masters[1], ANYWHERE),
        m_up=(masters[2], ANYWHERE),
        m_down=(masters[3], ANYWHERE),
    )
    half = shape(F32, 4, 4, 4, ROWS, 128)
    outs = {
        n: (shape(kind, CHUNKS * dims[0], *dims[1:]), ANYWHERE)
        for n, (dims, kind) in KEPT_BLOCKS._asdict().items()
    }
    outs.update({n: (shape(BF, 1, *s), ANYWHERE) for n, s in zip(Weights._fields, WEIGHT_SIZES)})
    outs.update(
        sums=(shape(F32, 1, 128), whole(1, 128)),
        block_out=(shape(BF, IMG * CHUNKS, SEQ, D), imaged(SEQ, D)),
        grad_out=(shape(F32, CHUNKS, RUN, D), chunked(RUN, D)),
        keep=(half, VMEM_WHOLE),
        send=(half, VMEM_WHOLE),
    )
    scratch = {}
    for suffix in ("_a", "_b"):
        for n, (dims, kind) in KEPT_BLOCKS._asdict().items():
            scratch[n + suffix] = pltpu.VMEM(dims, kind)
        for n, size in zip(Weights._fields, WEIGHT_SIZES):
            scratch[n + suffix] = pltpu.VMEM((1,) + size, BF)
    scratch.update(
        totals_a=pltpu.VMEM((24, D), F32),
        totals_b=pltpu.VMEM((24, D), F32),
        heads=pltpu.VMEM((3, RUN + 16, 128), F32),
        **mlp_scratch(),
        **attention_scratch(),
        d_mid=pltpu.VMEM((1, RUN, D), F32),
        grad=pltpu.VMEM((1, RUN, D), F32),
        normed=pltpu.VMEM((RUN, D), BF),
        acc_vec=pltpu.VMEM((8, 12 * D), F32),
        tokens_in=pltpu.VMEM((IMG * CHUNKS, SEQ, D), BF),
        grad_low=pltpu.VMEM((IMG * CHUNKS, SEQ, D), BF),
        fetch_sem=pltpu.SemaphoreType.DMA((2,)),
        load_sem=pltpu.SemaphoreType.DMA((4,)),
        save_sem=pltpu.SemaphoreType.DMA((7,)),
        weight_sem=pltpu.SemaphoreType.DMA((4,)),
    )
    return call_kernel(front_kernel, ins, outs, scratch, FRONT_LIMIT, "front")


FRONT_LIMIT = 60


def mlp_scratch():
    return dict(
        low_grad=pltpu.VMEM((RUN, D), BF),
        hidden=pltpu.VMEM((RUN, FF), F32),
        d_hidden=pltpu.VMEM((RUN, FF), BF),
        acc_up=pltpu.VMEM((D, FF), F32),
        acc_down=pltpu.VMEM((FF, D), F32),
    )


def attention_scratch():
    return dict(
        d_branch=pltpu.VMEM((RUN, D), BF),
        d_heads=pltpu.VMEM((3, RUN + 16, 128), F32),
        proj=pltpu.VMEM((9, RUN + 16, 128), F32),
        d_low=pltpu.VMEM((RUN, 3 * D), BF),
        acc_attn=pltpu.VMEM((D, 3 * D), F32),
        acc_out=pltpu.VMEM((D, D), F32),
        small=pltpu.VMEM((128, 128), F32),
    )


def back_kernel(r):
    step = pl.program_id(0)
    first = step == 0
    kept_in = [getattr(r, n + "_in") for n in Kept._fields] + [r.grad_in]
    kept = [getattr(r, n) for n in Kept._fields] + [r.grad_all]
    weights_in = [getattr(r, n + "_in") for n in Weights._fields]
    weights = [getattr(r, n) for n in Weights._fields]

    def load(k, chunk):
        if k >= ATTN:
            return pltpu.make_async_copy(weights_in[k - ATTN], weights[k - ATTN], r.sem.at[k, 0])
        size = kept[k].shape[0] // CHUNKS
        at = pl.ds(chunk * size, size)
        return pltpu.make_async_copy(kept_in[k].at[at], kept[k].at[at], r.sem.at[k, chunk])

    @pl.when(first)
    def _():
        for chunk in range(CHUNKS):
            for k in (GRAD, DOWN, SLOPE, UP, MIDDLE, ACT, OUT, MIXED, HEADS_P, HEADS_A, ATTN, STREAM):
                if k < ATTN or chunk == 0:
                    load(k, chunk).start()
        r.acc_vec[...] = jnp.zeros_like(r.acc_vec)
        for block in range(3):
            r.d_heads[block, RUN : RUN + 16, :] = jnp.zeros((16, 128), F32)

    def ready(*which):
        for k in which:
            if k < ATTN:
                load(k, step).wait()
            else:

                @pl.when(first)
                def _():
                    load(k, 0).wait()

    views = {}
    for n, ref in zip(Kept._fields, kept):
        size = ref.shape[0] // CHUNKS
        views[n] = ref.at[pl.ds(step * size, size)]
    q = types.SimpleNamespace(**{**vars(r), **views}, layer=0, first=first, ready=ready)
    back_mlp(q, r.grad_all.at[pl.ds(step, 1)])
    back_attention(q, r.d_mid, r.grad)
    for image in range(IMG):
        r.grad_out[image] = r.grad[0, SEQ * image : SEQ * (image + 1), :]

    @pl.when(step == CHUNKS - 1)
    def _():
        fill_small(r.small, r.acc_vec, r.sums[...])
        plan = mlp_plan(r, r.keep, r.send, r.send, UP_AT, DOWN_AT)
        emit_packed(r.core[0], plan + attention_plan(r, r.keep, r.send, 0))


def back_call(core, grad, vector, ahead):
    half = shape(F32, 4, 4, 4, ROWS, 128)
    ins = dict(
        core=(core, pl.BlockSpec(memory_space=pltpu.SMEM)),
        grad_in=(grad, ANYWHERE),
        vec=(vector, whole(2, 12 * D)),
        sums=(ahead.sums, whole(1, 128)),
    )
    scratch = {}
    for n, size in zip(Weights._fields, WEIGHT_SIZES):
        ins[n + "_in"] = (getattr(ahead, n), ANYWHERE)
        scratch[n] = pltpu.VMEM((1,) + size, BF)
    for n, (dims, kind) in KEPT_BLOCKS._asdict().items():
        ins[n + "_in"] = (getattr(ahead, n), ANYWHERE)
        scratch[n] = pltpu.VMEM((CHUNKS * dims[0],) + dims[1:], kind)
    outs = dict(
        grad_out=(shape(F32, IMG * CHUNKS, SEQ, D), imaged(SEQ, D)),
        keep=(half, VMEM_WHOLE),
        send=(half, VMEM_WHOLE),
    )
    scratch.update(
        **mlp_scratch(),
        **attention_scratch(),
        grad_all=pltpu.VMEM((CHUNKS, RUN, D), F32),
        d_mid=pltpu.VMEM((1, RUN, D), F32),
        grad=pltpu.VMEM((1, RUN, D), F32),
        normed=pltpu.VMEM((RUN, D), BF),
        acc_vec=pltpu.VMEM((8, 12 * D), F32),
        sem=pltpu.SemaphoreType.DMA((12, CHUNKS)),
    )
    return call_kernel(back_kernel, ins, outs, scratch, BACK_LIMIT, "back")


BACK_LIMIT = 50


def local_step(core, tokens, grad_out, masters, vector, shares):
    ahead = front(core, tokens, grad_out, masters, vector)
    got, early = lax.optimization_barrier((swap_core(ahead.send), shares[:2]))
    parts = add_core(ahead.keep, got)
    grad, parts = lax.optimization_barrier((ahead.grad_out, parts))
    parts_one = ring(0, parts)
    back = back_call(core, grad, vector, ahead)
    send, parts_one = lax.optimization_barrier((back.send, parts_one))
    got, late = lax.optimization_barrier((swap_core(send), shares[2:]))
    parts_zero = ring(0, add_core(back.keep, got))
    return ahead.block_out, back.grad_out, parts_zero + parts_one, early + late


def stage_position(stage):
    deep, high, core, across = place_of(lax.axis_index(GROUP_AXES))
    if stage == 2:
        return deep
    return jnp.where(core == stage, across, high)


def add_core_kernel(keep, got, *outs):
    me = stage_position(0)
    for shift in range(4):
        at = me ^ shift

        @pl.loop(0, 16)
        def _(i):
            outs[shift][i // 4, i % 4] = keep[at, i // 4, i % 4] + got[at, i // 4, i % 4]


def add_first_kernel(*refs):
    sources = [refs[4 * k : 4 * k + 4] for k in range(2)]
    outs = refs[-4:]
    me = stage_position(1)
    for shift in range(4):
        at = me ^ shift

        @pl.loop(0, 4)
        def _(i):
            for layer, (own, one, two, three) in enumerate(sources):
                outs[shift][i, layer] = (own[at, i] + one[at, i]) + (two[at, i] + three[at, i])


def add_second_kernel(own, one, two, three, *outs):
    me = stage_position(2)
    for shift in range(4):
        at = me ^ shift
        outs[shift][...] = (own[at] + one[at]) + (two[at] + three[at])


def add_third_kernel(own, one, two, three, out):
    out[...] = (own[...] + one[...]) + (two[...] + three[...])


def call_add(kernel, values, out_dims, count, name):
    return pl.pallas_call(
        kernel,
        out_shape=[shape(F32, *out_dims, 128)] * count,
        in_specs=[VMEM_WHOLE] * len(values),
        out_specs=[VMEM_WHOLE] * count,
        compiler_params=pltpu.CompilerParams(vmem_limit_bytes=32 * 2**20),
        name=name,
    )(*values)


def ring(stage, parts):
    got = [lax.ppermute(parts[s], GROUP_AXES, ring_pairs(stage, s)) for s in (2, 1, 3)]
    return [parts[0]] + got


def swap_core(send):
    return lax.ppermute(send, GROUP_AXES, core_pairs())


def add_core(keep, got):
    return call_add(add_core_kernel, [keep, got], (4, 4, ROWS), 4, "add_core")


def finish_sums(parts):
    parts = call_add(add_first_kernel, parts, (4, 2, ROWS), 4, "add_first")
    parts = call_add(add_second_kernel, ring(1, parts), (2, ROWS), 4, "add_second")
    own = call_add(add_third_kernel, ring(2, parts), (2, ROWS), 1, "add_third")[0]
    return own, lax.ppermute(own, "grp", [(0, 1), (1, 0)])


def adam_step(gradient, moment_one, moment_two, weight, rate):
    moment_one = beta_one * moment_one + (1 - beta_one) * gradient
    moment_two = beta_two * moment_two + (1 - beta_two) * gradient * gradient
    fix_one = 1 - beta_one**STEP
    fix_two = 1 - beta_two**STEP
    update = (
        moment_one / fix_one / (jnp.sqrt(moment_two / fix_two) + adam_eps) + decay_rate * weight
    )
    return (moment_one, moment_two, weight - rate * update)


def finish_kernel(*refs):
    own, other = ([ref.at[k] for k in range(2)] for ref in refs[:2])
    weights, firsts, seconds, outers = (refs[2 + 5 * k : 7 + 5 * k] for k in range(4))
    outs = refs[22:]
    new_firsts, new_seconds, changes, new_outers, finals, copies = (
        outs[5 * k : 5 * k + 5] for k in range(6)
    )
    rms = outs[30]

    def gathered(refs, kind, row):
        if kind == 4:
            return jnp.concatenate([ref[SMALL_AT : SMALL_AT + 1, 0:36] for ref in refs], 0)
        start, rows, width = (
            (QKV_AT, 3, 9),
            (PROJ_AT, 3, 3),
            (UP_AT, 3, 12),
            (DOWN_AT, 12, 3),
        )[kind]
        lines = [start + rows * c + row for c in range(width)]
        return jnp.concatenate(
            [
                jnp.concatenate([ref[line : line + 1, :] for ref in refs], 0)
                for line in lines
            ],
            1,
        )

    for kind in range(5):
        rate = rates()[kind]
        for row in range(1 if kind == 4 else weights[kind].shape[0]):
            at = slice(None) if kind == 4 else row
            weight = weights[kind][at]
            moments = (firsts[kind][at], seconds[kind][at])
            one, two, updated = adam_step(gathered(own, kind, row), *moments, weight, rate)
            updated_other = adam_step(gathered(other, kind, row), *moments, weight, rate)[2]
            change = ((weight - updated) + (weight - updated_other)) / 2
            outer = outer_decay * outers[kind][at] + change
            final = weight - outer_rate * (change + outer_decay * outer)
            new_firsts[kind][at] = one
            new_seconds[kind][at] = two
            changes[kind][at] = change
            new_outers[kind][at] = outer
            finals[kind][at] = final
            copies[kind][at] = final.astype(jnp.bfloat16)
    for layer in range(2):
        totals = [
            ref[SMALL_AT : SMALL_AT + 1, SUMS_AT : SUMS_AT + 3] for ref in (own[layer], other[layer])
        ]
        rms[layer : layer + 1, :] = jnp.sqrt((totals[0] + totals[1]) / ENTRIES)


def rows_first(value):
    return value if value.ndim == 2 else jnp.swapaxes(value, 0, 1)


def finish(own, other, weights, firsts, seconds, outers):
    given = [*weights, *[rows_first(v) for v in (*firsts, *seconds, *outers)]]
    full = [jax.ShapeDtypeStruct(v.shape, jnp.float32) for v in given[:5]]
    low = [jax.ShapeDtypeStruct(v.shape, jnp.bfloat16) for v in given[:5]]
    results = pl.pallas_call(
        finish_kernel,
        out_shape=full * 5 + low + [jax.ShapeDtypeStruct((2, 3), jnp.float32)],
        in_specs=[VMEM_WHOLE] * 22,
        out_specs=[VMEM_WHOLE] * 31,
        name="finish",
    )(own, other, *given)
    results = [rows_first(v) for v in results[:30]] + [results[30]]
    return [v[None] for v in results[:10]] + results[10:]

def body(
    tokens,
    grad_out,
    weight_qkv,
    weight_proj,
    weight_up,
    weight_down,
    weight_vector,
    old_first_qkv,
    old_first_proj,
    old_first_up,
    old_first_down,
    old_first_vector,
    old_second_qkv,
    old_second_proj,
    old_second_up,
    old_second_down,
    old_second_vector,
    old_outer_qkv,
    old_outer_proj,
    old_outer_up,
    old_outer_down,
    old_outer_vector,
):
    masters = (weight_qkv, weight_proj, weight_up, weight_down, weight_vector)
    old_firsts = (old_first_qkv, old_first_proj, old_first_up, old_first_down, old_first_vector)
    old_seconds = (
        old_second_qkv,
        old_second_proj,
        old_second_up,
        old_second_down,
        old_second_vector,
    )
    old_outers = (old_outer_qkv, old_outer_proj, old_outer_up, old_outer_down, old_outer_vector)
    owner_index = lax.axis_index(GROUP_AXES)
    core = jnp.reshape(owner_index // 4 % 2, (1,)).astype(jnp.int32)
    shares = []
    for kind_index in range(5):
        share_rows = old_firsts[kind_index].shape[1]
        at = owner_index * share_rows
        share = lax.dynamic_slice_in_dim(masters[kind_index], at, share_rows, 1)
        shares.append(rows_first(share))
    block_out, grad_tokens, parts, shares = local_step(
        core, tokens, grad_out, masters[:4], weight_vector, shares
    )
    own, other = finish_sums(parts)
    results = finish(own, other, shares, old_firsts, old_seconds, old_outers)
    return (block_out, grad_tokens, *results)


def solution(mesh):
    placed = (
        P(("grp", "wide", "narrow"), None, None),
        P(("grp", "wide", "narrow"), None, None),
        P(),
        P(),
        P(),
        P(),
        P(),
        P(None, ("wide", "narrow"), None),
        P(None, ("wide", "narrow"), None),
        P(None, ("wide", "narrow"), None),
        P(None, ("wide", "narrow"), None),
        P(None, ("wide", "narrow")),
        P(None, ("wide", "narrow"), None),
        P(None, ("wide", "narrow"), None),
        P(None, ("wide", "narrow"), None),
        P(None, ("wide", "narrow"), None),
        P(None, ("wide", "narrow")),
        P(None, ("wide", "narrow"), None),
        P(None, ("wide", "narrow"), None),
        P(None, ("wide", "narrow"), None),
        P(None, ("wide", "narrow"), None),
        P(None, ("wide", "narrow")),
    )
    return jax.shard_map(
        body,
        mesh=mesh,
        in_specs=placed,
        out_specs=(
            P(("grp", "wide", "narrow"), None, None),
            P(("grp", "wide", "narrow"), None, None),
            P("grp", None, ("wide", "narrow"), None),
            P("grp", None, ("wide", "narrow"), None),
            P("grp", None, ("wide", "narrow"), None),
            P("grp", None, ("wide", "narrow"), None),
            P("grp", None, ("wide", "narrow")),
            P("grp", None, ("wide", "narrow"), None),
            P("grp", None, ("wide", "narrow"), None),
            P("grp", None, ("wide", "narrow"), None),
            P("grp", None, ("wide", "narrow"), None),
            P("grp", None, ("wide", "narrow")),
            P(None, ("wide", "narrow"), None),
            P(None, ("wide", "narrow"), None),
            P(None, ("wide", "narrow"), None),
            P(None, ("wide", "narrow"), None),
            P(None, ("wide", "narrow")),
            P(None, ("wide", "narrow"), None),
            P(None, ("wide", "narrow"), None),
            P(None, ("wide", "narrow"), None),
            P(None, ("wide", "narrow"), None),
            P(None, ("wide", "narrow")),
            P(None, ("wide", "narrow"), None),
            P(None, ("wide", "narrow"), None),
            P(None, ("wide", "narrow"), None),
            P(None, ("wide", "narrow"), None),
            P(None, ("wide", "narrow")),
            P(None, ("wide", "narrow"), None),
            P(None, ("wide", "narrow"), None),
            P(None, ("wide", "narrow"), None),
            P(None, ("wide", "narrow"), None),
            P(None, ("wide", "narrow")),
            P(),
        ),
        check_vma=False,
    )
```
